32 devices in a mesh: fsdp: 4 (over x, core), ctx: 4 (over z), tp: 2 (over y).
Axes of the slice: x: 2, y: 2, z: 4, core: 2. Of those that a mesh axis runs over, the one named last changes fastest.
Arguments:
- tokens: bfloat16 [4, 1024, 1024], P('fsdp', 'ctx'), may hold values from -6 to 6
- segments: int32 [4, 1024], P('fsdp'), may hold values from 0 to 4, as said below
- attn_gain: bfloat16 [1024], P('fsdp'), may hold values from 0.25 to 1.75
- qkv_weight: bfloat16 [1024, 3, 1024], P('fsdp', None, 'tp'), may hold values from -0.1875 to 0.1875
- out_weight: bfloat16 [1024, 1024], P('tp', 'fsdp'), may hold values from -3.5 to 3.5
- mlp_gain: bfloat16 [1024], P('fsdp'), may hold values from 0.25 to 1.75
- inner_weight: bfloat16 [1024, 2, 2624], P('fsdp', None, 'tp'), may hold values from -0.1875 to 0.1875
- outer_weight: bfloat16 [2624, 1024], P('tp', 'fsdp'), may hold values from -0.125 to 0.125
- cotangent: bfloat16 [4, 1024, 1024], P('fsdp', 'ctx'), may hold values from -6 to 6
Outputs:
- block_out: bfloat16 [4, 1024, 1024], P('fsdp', 'ctx')
- input_grad: float32 [4, 1024, 1024], P('fsdp', 'ctx')
- attn_gain_grad: float32 [1024], P('fsdp')
- qkv_grad: float32 [1024, 3, 1024], P('fsdp', None, 'tp')
- out_grad: float32 [1024, 1024], P('tp', 'fsdp')
- mlp_gain_grad: float32 [1024], P('fsdp')
- inner_grad: float32 [1024, 2, 2624], P('fsdp', None, 'tp')
- outer_grad: float32 [2624, 1024], P('tp', 'fsdp')
The draws below stay inside these ranges and needn't reach their ends.
Inputs may be any that keep to these rules, and one draw needn't show every extreme that they name: `segments`: every row is non-decreasing and holds five documents: two that end within its first 128 positions, one from there to within its last 128 positions, and two after it.
All inputs are finite; a program needn't handle non-finite values.
Results may differ from the reference program's by a relative error of at most 0.02.
Values may be sent and summed in bfloat16 or wider, within the bound.
No kernel may reach another device: no remote copies, remote signals or barrier semaphores. Data moves between devices by JAX's collectives and lax.ppermute only.
A program may use at most 192 MiB of HBM per device.

```python
import jax
import jax.numpy as jnp
from jax import lax

D = 1024
HEADS = 16
HD = 64
FF = 2624
LOCAL_LEN = 256
SEQS = 4
LENGTH = 1024


def draw_segments(key, part):
    key = jax.random.fold_in(key, 11)
    sub_keys = jax.random.split(key, 4)
    half_len = LOCAL_LEN // 2
    first_cut = jax.random.randint(sub_keys[0], (SEQS, 1), 2, half_len)
    head_cut = jax.random.randint(sub_keys[1], (SEQS, 1), 1, first_cut)
    last_cut = jax.random.randint(sub_keys[2], (SEQS, 1), LENGTH - half_len, LENGTH - 1)
    tail_cut = jax.random.randint(sub_keys[3], (SEQS, 1), last_cut + 1, LENGTH)
    places = jnp.arange(LENGTH, dtype=jnp.int32)[None, :]
    total = (places >= head_cut).astype(jnp.int32) + (places >= first_cut).astype(jnp.int32)
    total = total + (places >= last_cut).astype(jnp.int32) + (places >= tail_cut).astype(jnp.int32)
    return total.astype(jnp.int32)


def steps_of(own_key, shape, shards, smallest, largest):
    loudness, own = 1.0, jax.random.fold_in(own_key, 6)
    for axis_at, blocks in shards:
        draws = jnp.exp(jax.random.uniform(jax.random.fold_in(own, axis_at), (blocks,), jnp.float32, smallest / len(shards), largest / len(shards)))
        loudness = loudness * jnp.repeat(draws, shape[axis_at] // blocks).reshape([-1 if axis == axis_at else 1 for axis in range(len(shape))])
    return loudness


def scatter_about(rng, shape, scale, bound, shards=(), kind=jnp.bfloat16):
    entries = scale * jax.random.normal(rng, shape, jnp.float32)
    if shards:
        entries = entries * steps_of(rng, shape, shards, -0.22, 0.18)
    return jnp.clip(entries, -bound, bound).astype(kind)


def setup_inputs(seed: int = 0) -> dict:
    arg_keys = jax.random.split(jax.random.key(seed), 10)
    tokens = scatter_about(arg_keys[0], (SEQS, LENGTH, D), 1.0, 6.0, ((0, 4), (1, 4)))
    segments = draw_segments(jax.random.fold_in(arg_keys[9], 71), 0)
    attn_gain = jnp.clip(1.0 + 0.15 * jax.random.normal(arg_keys[2], (D,), jnp.float32), 0.25, 1.75).astype(jnp.bfloat16)
    qkv_weight = scatter_about(arg_keys[3], (D, 3, D), D ** -0.5, 0.1875, ((0, 4), (2, 2)))
    out_weight = scatter_about(arg_keys[4], (D, D), (max(1, 3 * D // LENGTH)) ** -0.5, 3.5, ((0, 2), (1, 4)))
    mlp_gain = jnp.clip(1.0 + 0.15 * jax.random.normal(arg_keys[5], (D,), jnp.float32), 0.25, 1.75).astype(jnp.bfloat16)
    inner_weight = scatter_about(arg_keys[6], (D, 2, FF), D ** -0.5, 0.1875, ((0, 4), (2, 2)))
    outer_weight = scatter_about(arg_keys[7], (FF, D), FF ** -0.5, 0.125, ((0, 2), (1, 4)))
    cotangent = scatter_about(arg_keys[8], (SEQS, LENGTH, D), 1.0, 6.0, ((0, 4), (1, 4)))
    return dict(tokens=tokens, segments=segments, attn_gain=attn_gain, qkv_weight=qkv_weight, out_weight=out_weight, mlp_gain=mlp_gain, inner_weight=inner_weight, outer_weight=outer_weight, cotangent=cotangent)


EPSILON = 1e-05
ROPE_BASE = 160000.0
MASKED = -1e+30
TOP_PRECISION = lax.Precision.HIGHEST

@jax.custom_vjp
def low(v):
    return lax.optimization_barrier(v.astype(jnp.bfloat16)).astype(jnp.float32)

@jax.custom_vjp
def reduced_backward(v):
    return v

def low_keep(v):
    return (low(v), None)

def low_pass(kept, grad):
    return (grad,)

def back_keep(v):
    return (v, None)

def back_low(kept, grad):
    return (low(grad),)
low.defvjp(low_keep, low_pass)
reduced_backward.defvjp(back_keep, back_low)

def normalize(values, gain_row):
    row_mean = lax.optimization_barrier(jnp.mean(values, axis=-1, keepdims=True))
    centered = values - row_mean
    spread = lax.optimization_barrier(jnp.mean(centered * centered, axis=-1, keepdims=True))
    return centered * lax.rsqrt(spread + EPSILON) * gain_row

def angle_tables(row_count, offset, depth):
    half_width = depth // 2
    inverse = jnp.power(jnp.float32(ROPE_BASE), -(2.0 * jnp.arange(half_width, dtype=jnp.float32)) / depth)
    places = (offset + jnp.arange(row_count, dtype=jnp.int32)).astype(jnp.float32)
    angles = places[:, None] * inverse[None, :]
    angles = jnp.concatenate([angles, angles], axis=-1)
    return (jnp.cos(angles)[:, None, :], jnp.sin(angles)[:, None, :])

def rotate(values, cosine, sine):
    half_width = values.shape[-1] // 2
    turned = jnp.concatenate([-values[..., half_width:], values[..., :half_width]], axis=-1)
    return values * cosine + turned * sine

def attend_sequence(queries, key_low, value_low, seg_row):
    block_size = min(512, LENGTH)
    score_scale = HD ** (-0.5)

    def one_block(packed):
        query_block, block_seg = packed
        scores = reduced_backward(jnp.einsum('qhe,khe->hqk', query_block, key_low, precision=TOP_PRECISION))
        same_doc = (block_seg[:, None] == seg_row[None, :])[None]
        logits = jnp.where(same_doc, scores * score_scale, MASKED)
        peak_val = lax.optimization_barrier(jnp.max(logits, axis=-1, keepdims=True))
        weights = jnp.exp(logits - peak_val)
        probs = weights / lax.optimization_barrier(jnp.sum(weights, axis=-1, keepdims=True))
        return jnp.einsum('hqk,khe->qhe', low(probs), value_low, precision=TOP_PRECISION)
    blocks = (queries.reshape(LENGTH // block_size, block_size, HEADS, HD), seg_row.reshape(LENGTH // block_size, block_size))
    parts = lax.map(jax.checkpoint(one_block), blocks)
    return parts.reshape(LENGTH, HEADS, HD)

def reference(tokens, segments, attn_gain, qkv_weight, out_weight, mlp_gain, inner_weight, outer_weight, cotangent):

    def layer(input_rows, gain_one, query_key_value_matrix, output_matrix, gain_two, inner_matrix, outer_matrix):
        norm_output = low(normalize(input_rows, gain_one))
        projected_output = reduced_backward(jnp.einsum('bhi,iva->bhva', norm_output, query_key_value_matrix, precision=TOP_PRECISION))
        projected_output = projected_output.reshape(SEQS, LENGTH, 3, HEADS, HD)
        cosine, sine = angle_tables(LENGTH, 0, HD)
        queries = low(rotate(projected_output[:, :, 0], cosine, sine))
        key_low = low(rotate(projected_output[:, :, 1], cosine, sine))
        value_low = low(projected_output[:, :, 2])
        attention_output = lax.map(lambda packed: attend_sequence(packed[0], packed[1], packed[2], packed[3]), (queries, key_low, value_low, segments))
        attention_output = low(reduced_backward(attention_output.reshape(SEQS, LENGTH, D)))
        middle_activation = input_rows + reduced_backward(jnp.einsum('roc,cg->rog', attention_output, output_matrix, precision=TOP_PRECISION))
        second_residual = low(normalize(middle_activation, gain_two))
        hidden_input = reduced_backward(jnp.einsum('bhi,iva->bhva', second_residual, inner_matrix, precision=TOP_PRECISION))
        hidden_state = low(jax.nn.gelu(hidden_input[:, :, 0], approximate=False) * hidden_input[:, :, 1])
        return middle_activation + reduced_backward(jnp.einsum('owz,zu->owu', hidden_state, outer_matrix, precision=TOP_PRECISION))
    primals = (tokens.astype(jnp.float32), attn_gain.astype(jnp.float32), qkv_weight.astype(jnp.float32), out_weight.astype(jnp.float32), mlp_gain.astype(jnp.float32), inner_weight.astype(jnp.float32), outer_weight.astype(jnp.float32))
    result, backward = jax.vjp(layer, *primals)
    gradients = backward(cotangent.astype(jnp.float32))
    return (result.astype(jnp.bfloat16), gradients[0], gradients[1], gradients[2], gradients[3], gradients[4], gradients[5], gradients[6])
```

```python
import math

import jax
import jax.numpy as jnp
from jax import lax
from jax.experimental import pallas as pl
from jax.experimental.pallas import tpu as pltpu
from jax.sharding import PartitionSpec as P

HD = 64


EPSILON = 1e-05
ROPE_BASE = 160000.0
MASKED = -1e30


def normalize(values, gain_row):
    row_mean = jnp.mean(values, axis=-1, keepdims=True)
    centered = values - row_mean
    spread = jnp.mean(centered * centered, axis=-1, keepdims=True)
    return centered * lax.rsqrt(spread + EPSILON) * gain_row


def geglu(gate_in, upper):
    return jax.nn.gelu(gate_in, approximate=False) * upper


def angle_tables(row_count, offset, depth):
    half_width = depth // 2
    inverse = jnp.power(
        jnp.float32(ROPE_BASE), -(2.0 * jnp.arange(half_width, dtype=jnp.float32)) / depth
    )
    places = (offset + jnp.arange(row_count, dtype=jnp.int32)).astype(jnp.float32)
    angles = places[:, None] * inverse[None, :]
    angles = jnp.concatenate([angles, angles], axis=-1)
    return (jnp.cos(angles)[:, None, :], jnp.sin(angles)[:, None, :])


def rotate(values, cosine, sine):
    half_width = values.shape[-1] // 2
    turned = jnp.concatenate([-values[..., half_width:], values[..., :half_width]], axis=-1)
    return values * cosine + turned * sine


def rotate_back(grad_in, cosine, sine):
    half_width = grad_in.shape[-1] // 2
    scaled = grad_in * sine
    turned = jnp.concatenate([scaled[..., half_width:], -scaled[..., :half_width]], axis=-1)
    return grad_in * cosine + turned


def attend_forward(queries, query_seg, seg_row, key_low, value_low, score_scale):
    row_count, heads_here, depth = queries.shape
    initial = (
        jnp.full((heads_here, row_count), MASKED, jnp.float32),
        jnp.zeros((heads_here, row_count), jnp.float32),
        jnp.zeros((row_count, heads_here, depth), jnp.float32),
    )
    key_piece = lax.all_gather(key_low, "ctx", axis=0, tiled=True)
    value_piece = lax.all_gather(value_low, "ctx", axis=0, tiled=True)
    piece_rows = key_piece.shape[0]
    block_size = math.gcd(piece_rows, 512)
    blocks = (
        key_piece.reshape(piece_rows // block_size, block_size, heads_here, depth),
        value_piece.reshape(piece_rows // block_size, block_size, heads_here, depth),
        seg_row.reshape(piece_rows // block_size, block_size),
    )

    def step(state, block_data):
        running_peak, running_total, accum = state
        key_block, value_block, block_seg = block_data
        scores = jnp.einsum("qhe,khe->hqk", queries, key_block, preferred_element_type=jnp.float32)
        same_doc = (query_seg[:, None] == block_seg[None, :])[None]
        logits = jnp.where(same_doc, scores * score_scale, MASKED)
        new_peak = jnp.maximum(running_peak, jnp.max(logits, axis=-1))
        rescale = jnp.exp(running_peak - new_peak)
        weights = jnp.where(same_doc, jnp.exp(logits - new_peak[:, :, None]), 0.0)
        running_total = running_total * rescale + jnp.sum(weights, axis=-1)
        mixed_out = jnp.einsum(
            "hqk,khe->qhe",
            weights.astype(jnp.bfloat16),
            value_block,
            preferred_element_type=jnp.float32,
        )
        accum = accum * rescale.T[:, :, None] + mixed_out
        return ((new_peak, running_total, accum), None)

    result, unused = lax.scan(step, initial, blocks)
    running_peak, running_total, accum = result
    return (accum / running_total.T[:, :, None], running_peak + jnp.log(running_total))


def probs_and_grads(
    query_block, key_block, grad_block, value_block, same_doc, log_total, delta_rows, score_scale
):
    scores = jnp.einsum("qhe,khe->hqk", query_block, key_block, preferred_element_type=jnp.float32)
    probs = jnp.where(same_doc, jnp.exp(scores * score_scale - log_total[:, :, None]), 0.0)
    prob_grad = jnp.einsum(
        "qhe,khe->hqk", grad_block, value_block, preferred_element_type=jnp.float32
    )
    score_grad = (probs * (prob_grad - delta_rows[:, :, None]) * score_scale).astype(jnp.bfloat16)
    return (probs.astype(jnp.bfloat16), score_grad)


def attend_backward(
    queries, key_low, value_low, grad_low, log_total, delta_rows, query_seg, seg_row, score_scale
):
    row_count, heads_here, depth = queries.shape
    seq_length = seg_row.shape[0]
    block_size = math.gcd(seq_length, 512)
    block_count = seq_length // block_size
    key_all, value_all = (
        lax.all_gather(key_low, "ctx", axis=0, tiled=True),
        lax.all_gather(value_low, "ctx", axis=0, tiled=True),
    )
    blocks = (
        key_all.reshape(block_count, block_size, heads_here, depth),
        value_all.reshape(block_count, block_size, heads_here, depth),
        seg_row.reshape(block_count, block_size),
    )

    def key_step(query_acc, block_data):
        key_block, value_block, block_seg = block_data
        same_doc = (query_seg[:, None] == block_seg[None, :])[None]
        prob_low, score_grad = probs_and_grads(
            queries, key_block, grad_low, value_block, same_doc, log_total, delta_rows, score_scale
        )
        query_acc = query_acc + jnp.einsum(
            "hqk,khe->qhe", score_grad, key_block, preferred_element_type=jnp.float32
        )
        key_part = jnp.einsum(
            "hqk,qhe->khe", score_grad, queries, preferred_element_type=jnp.float32
        )
        value_part = jnp.einsum(
            "hqk,qhe->khe", prob_low, grad_low, preferred_element_type=jnp.float32
        )
        return (query_acc, (key_part, value_part))

    query_grad, key_value_parts = lax.scan(
        key_step, jnp.zeros((row_count, heads_here, depth), jnp.float32), blocks
    )
    key_parts = key_value_parts[0].reshape(seq_length, heads_here * depth)
    value_parts = key_value_parts[1].reshape(seq_length, heads_here * depth)
    key_grad, value_grad = (
        lax.psum_scatter(
            key_parts.astype(jnp.bfloat16), "ctx", scatter_dimension=0, tiled=True
        ).astype(jnp.float32),
        lax.psum_scatter(
            value_parts.astype(jnp.bfloat16), "ctx", scatter_dimension=0, tiled=True
        ).astype(jnp.float32),
    )
    key_grad = key_grad.reshape(row_count, heads_here, depth)
    value_grad = value_grad.reshape(row_count, heads_here, depth)
    return (query_grad, key_grad, value_grad)


def per_device(
    tokens,
    segments,
    attn_gain,
    qkv_weight,
    out_weight,
    mlp_gain,
    inner_weight,
    outer_weight,
    cotangent,
):
    qkv_full, out_full, gain_one = (
        lax.all_gather(qkv_weight, "fsdp", axis=0, tiled=True),
        lax.all_gather(out_weight, "fsdp", axis=1, tiled=True),
        lax.all_gather(attn_gain, "fsdp", axis=0, tiled=True),
    )
    inner_full, outer_full, gain_two = (
        lax.all_gather(inner_weight, "fsdp", axis=0, tiled=True),
        lax.all_gather(outer_weight, "fsdp", axis=1, tiled=True),
        lax.all_gather(mlp_gain, "fsdp", axis=0, tiled=True),
    )
    seq_count, row_count, model_width = tokens.shape
    local_width = qkv_full.shape[2]
    heads_here = local_width // HD
    score_scale = HD ** (-0.5)
    offset = lax.axis_index("ctx") * row_count
    cosine, sine = angle_tables(row_count, offset, HD)
    input_rows = tokens.reshape(-1, model_width).astype(jnp.float32)
    normed_one, norm_one_back = jax.vjp(normalize, input_rows, gain_one.astype(jnp.float32))
    first_low = normed_one.astype(jnp.bfloat16)
    projected_output = jnp.einsum(
        "td,dcf->tcf", first_low, qkv_full, preferred_element_type=jnp.float32
    )
    projected_output = projected_output.reshape(seq_count, row_count, 3, heads_here, HD)
    query_low = rotate(projected_output[:, :, 0], cosine, sine).astype(jnp.bfloat16)
    key_low = rotate(projected_output[:, :, 1], cosine, sine).astype(jnp.bfloat16)
    value_low = projected_output[:, :, 2].astype(jnp.bfloat16)
    seq_index = 0
    seg_row = segments[seq_index]
    query_seg = lax.dynamic_slice_in_dim(seg_row, offset, row_count)
    raw_out, log_total = attend_forward(
        query_low[seq_index],
        query_seg,
        seg_row,
        key_low[seq_index],
        value_low[seq_index],
        score_scale,
    )
    query_segs = [query_seg]
    raw_outs = [raw_out]
    log_totals = [log_total]
    attended_low = jnp.stack(raw_outs).astype(jnp.bfloat16).reshape(-1, local_width)
    attn_part = jnp.dot(attended_low, out_full, preferred_element_type=jnp.float32)
    middle_activation = input_rows + lax.psum(attn_part.astype(jnp.bfloat16), "tp").astype(
        jnp.float32
    )
    normed_two, norm_two_back = jax.vjp(normalize, middle_activation, gain_two.astype(jnp.float32))
    second_low = normed_two.astype(jnp.bfloat16)
    hidden_input = jnp.einsum(
        "td,dcf->tcf", second_low, inner_full, preferred_element_type=jnp.float32
    )
    hidden_state, geglu_back = jax.vjp(geglu, hidden_input[:, 0], hidden_input[:, 1])
    hidden_low = hidden_state.astype(jnp.bfloat16)
    mlp_part = jnp.dot(hidden_low, outer_full, preferred_element_type=jnp.float32)
    block_out = (
        middle_activation + lax.psum(mlp_part.astype(jnp.bfloat16), "tp").astype(jnp.float32)
    ).astype(jnp.bfloat16)
    out_cot = cotangent.reshape(-1, model_width)
    outer_local = jnp.einsum("tf,td->fd", hidden_low, out_cot, preferred_element_type=jnp.float32)
    hidden_grad = jnp.einsum("td,fd->tf", out_cot, outer_full, preferred_element_type=jnp.float32)
    gate_grad, up_grad = geglu_back(hidden_grad)
    inner_low = jnp.stack([gate_grad, up_grad], axis=1).astype(jnp.bfloat16)
    inner_local = jnp.einsum(
        "td,tcf->dcf", second_low, inner_low, preferred_element_type=jnp.float32
    )
    normed_two_grad = lax.psum(
        jnp.einsum("tcf,dcf->td", inner_low, inner_full, preferred_element_type=jnp.float32).astype(
            jnp.bfloat16
        ),
        "tp",
    ).astype(jnp.float32)
    middle_part, gain_two_grad = norm_two_back(normed_two_grad)
    middle_grad = out_cot.astype(jnp.float32) + middle_part
    attn_low = middle_grad.astype(jnp.bfloat16)
    out_local = jnp.einsum("tf,td->fd", attended_low, attn_low, preferred_element_type=jnp.float32)
    attended_grad = jnp.einsum("td,fd->tf", attn_low, out_full, preferred_element_type=jnp.float32)
    attended_grad = attended_grad.astype(jnp.bfloat16).reshape(seq_count, row_count, heads_here, HD)
    seq_index = 0
    grad_low = attended_grad[seq_index]
    delta_rows = jnp.sum(grad_low.astype(jnp.float32) * raw_outs[seq_index], axis=-1).T
    query_grad, key_grad, value_grad = attend_backward(
        query_low[seq_index],
        key_low[seq_index],
        value_low[seq_index],
        grad_low,
        log_totals[seq_index],
        delta_rows,
        query_segs[seq_index],
        segments[seq_index],
        score_scale,
    )
    stacked = jnp.stack(
        [rotate_back(query_grad, cosine, sine), rotate_back(key_grad, cosine, sine), value_grad],
        axis=1,
    )
    qkv_grads = stacked.reshape(row_count, 3, local_width)
    qkv_low = qkv_grads.astype(jnp.bfloat16)
    qkv_local = jnp.einsum("td,tcf->dcf", first_low, qkv_low, preferred_element_type=jnp.float32)
    normed_one_grad = lax.psum(
        jnp.einsum("tcf,dcf->td", qkv_low, qkv_full, preferred_element_type=jnp.float32).astype(
            jnp.bfloat16
        ),
        "tp",
    ).astype(jnp.float32)
    input_part, gain_one_grad = norm_one_back(normed_one_grad)
    input_grad = (middle_grad + input_part).reshape(tokens.shape)
    summed = (
        lax.psum_scatter(gain_one_grad, ("fsdp", "ctx"), scatter_dimension=0, tiled=True),
        lax.psum_scatter(qkv_local, ("fsdp", "ctx"), scatter_dimension=0, tiled=True),
        lax.psum_scatter(out_local, ("fsdp", "ctx"), scatter_dimension=1, tiled=True),
        lax.psum_scatter(gain_two_grad, ("fsdp", "ctx"), scatter_dimension=0, tiled=True),
        lax.psum_scatter(inner_local, ("fsdp", "ctx"), scatter_dimension=0, tiled=True),
        lax.psum_scatter(outer_local, ("fsdp", "ctx"), scatter_dimension=1, tiled=True),
    )
    gain_one_sum, qkv_sum, out_sum, gain_two_sum, inner_sum, outer_sum = summed
    shards = (
        lax.all_gather(gain_one_sum.astype(jnp.bfloat16), "ctx", axis=0, tiled=True).astype(
            gain_one_sum.dtype
        ),
        lax.all_gather(qkv_sum.astype(jnp.bfloat16), "ctx", axis=0, tiled=True).astype(
            qkv_sum.dtype
        ),
        lax.all_gather(out_sum.astype(jnp.bfloat16), "ctx", axis=1, tiled=True).astype(
            out_sum.dtype
        ),
        lax.all_gather(gain_two_sum.astype(jnp.bfloat16), "ctx", axis=0, tiled=True).astype(
            gain_two_sum.dtype
        ),
        lax.all_gather(inner_sum.astype(jnp.bfloat16), "ctx", axis=0, tiled=True).astype(
            inner_sum.dtype
        ),
        lax.all_gather(outer_sum.astype(jnp.bfloat16), "ctx", axis=1, tiled=True).astype(
            outer_sum.dtype
        ),
    )
    return (
        block_out.reshape(tokens.shape),
        input_grad,
        shards[0],
        shards[1],
        shards[2],
        shards[3],
        shards[4],
        shards[5],
    )


LANES = 128
WIDE_VMEM = 50 * 1024 * 1024


def hop(value, axis, bit, count):
    return lax.ppermute(value, axis, [(i, i ^ bit) for i in range(count)])


def after(value, *earlier):
    return lax.optimization_barrier((value,) + earlier)[0]


def pick(stacked, index):
    return lax.dynamic_index_in_dim(stacked, index, 0, keepdims=False)


def place(pieces, indices):
    whole = jnp.zeros((len(pieces),) + pieces[0].shape, pieces[0].dtype)
    for piece, index in zip(pieces, indices):
        whole = lax.dynamic_update_index_in_dim(whole, piece, index, 0)
    return whole.reshape((-1,) + pieces[0].shape[1:])


def lane_half(shape):
    return lax.broadcasted_iota(jnp.int32, shape, 1) < HD


def swap_halves(values):
    lane = lax.broadcasted_iota(jnp.int32, values.shape, 1)
    low_part = lax.rem(lane, HD) < HD // 2
    return jnp.where(
        low_part,
        pltpu.roll(values, LANES - HD // 2, 1),
        pltpu.roll(values, HD // 2, 1),
    )


def dot_nt(left, right):
    return lax.dot_general(left, right, (((1,), (1,)), ((), ())), preferred_element_type=jnp.float32)


def dot_nn(left, right):
    return lax.dot_general(left, right, (((1,), (0,)), ((), ())), preferred_element_type=jnp.float32)


def dot_tn(left, right):
    return lax.dot_general(left, right, (((0,), (0,)), ((), ())), preferred_element_type=jnp.float32)


def one_head(values, head):
    first = lane_half(values.shape)
    keep = first if head == 0 else jnp.logical_not(first)
    return jnp.where(keep, values, jnp.zeros_like(values))


def attention_forward_kernel(
    x_ref, gain_ref, weight_ref, cos_ref, sin_ref, seg_col, seg_line,
    h_ref, q_ref, k_ref, v_ref, raw_ref, low_ref, lse_ref,
):
    length = x_ref.shape[0]
    block = 256
    gain = gain_ref[...]
    for start in range(0, length, block):
        rows = pl.ds(start, block)
        normed = normalize(x_ref[rows, :].astype(jnp.float32), gain).astype(jnp.bfloat16)
        h_ref[rows, :] = normed
        projected = dot_nn(normed, weight_ref[...])
        cosine, sine = cos_ref[rows, :], sin_ref[rows, :]
        for ref, part in ((q_ref, projected[:, :LANES]), (k_ref, projected[:, LANES : 2 * LANES])):
            ref[rows, :] = (part * cosine + swap_halves(part) * sine).astype(jnp.bfloat16)
        v_ref[rows, :] = projected[:, 2 * LANES :].astype(jnp.bfloat16)
    for start in range(0, length, block):
        rows = pl.ds(start, block)
        queries = q_ref[rows, :] * jnp.bfloat16(HD ** (-0.5))
        same = seg_col[rows, :] == seg_line[...]
        outs, logs = [], []
        for head in range(2):
            scores = dot_nt(one_head(queries, head), k_ref[...])
            scores = jnp.where(same, scores, MASKED)
            peak = jnp.max(scores, axis=1, keepdims=True)
            weights = jnp.exp(scores - peak)
            total = jnp.sum(weights, axis=1, keepdims=True)
            probs = (weights * (1.0 / total)).astype(jnp.bfloat16)
            outs.append(dot_nn(probs, v_ref[...]))
            logs.append(peak + jnp.log(total))
        first = lane_half(outs[0].shape)
        raw = jnp.where(first, outs[0], outs[1])
        raw_ref[rows, :] = raw
        low_ref[rows, :] = raw.astype(jnp.bfloat16)
        lane = lax.broadcasted_iota(jnp.int32, (block, LANES), 1)
        lse_ref[:, rows] = jnp.where(lane == 0, logs[0], logs[1]).T[:8, :]


def attention_forward(x_all, gain_row, weight, cosine, sine, seg_row):
    length, width = x_all.shape
    low = jax.ShapeDtypeStruct((length, LANES), jnp.bfloat16)
    return pl.pallas_call(
        attention_forward_kernel,
        name="attention_forward",
        out_shape=(
            jax.ShapeDtypeStruct((length, width), jnp.bfloat16),
            low,
            low,
            low,
            jax.ShapeDtypeStruct((length, LANES), jnp.float32),
            low,
            jax.ShapeDtypeStruct((8, length), jnp.float32),
        ),
        compiler_params=pltpu.CompilerParams(vmem_limit_bytes=WIDE_VMEM),
        cost_estimate=pl.CostEstimate(
            flops=2 * length * width * 3 * LANES + 8 * length * length * LANES,
            bytes_accessed=3 * length * width * 2,
            transcendentals=2 * length * length,
        ),
    )(x_all, gain_row, weight, cosine, sine, seg_row.reshape(length, 1), seg_row.reshape(1, length))


def attention_backward_kernel(
    q_ref, k_ref, v_ref, do_ref, raw_ref, lse_ref, cos_ref, sin_ref, seg_col, seg_line,
    out_ref, turned_ref,
):
    length = q_ref.shape[0]
    block = 256
    grads = do_ref[...]
    product = grads.astype(jnp.float32) * raw_ref[...]
    first = lane_half(product.shape)
    whole = jnp.sum(jnp.where(first, product, 0.0), axis=1, keepdims=True)
    other = jnp.sum(jnp.where(first, 0.0, product), axis=1, keepdims=True)
    lane = lax.broadcasted_iota(jnp.int32, product.shape, 1)
    delta = jnp.where(lane == 0, whole, other).T
    scale = HD ** (-0.5)
    queries = q_ref[...]
    scaled = queries * jnp.bfloat16(scale)
    for start in range(0, length, block):
        rows = pl.ds(start, block)
        keys, values = k_ref[rows, :], v_ref[rows, :]
        keys_turned = keys.T
        same = seg_col[rows, :] == seg_line[...]
        key_parts, value_parts = [], []
        for head in range(2):
            scores = dot_nt(one_head(keys, head), scaled)
            probs = jnp.where(same, jnp.exp(scores - lse_ref[head : head + 1, :]), 0.0)
            prob_grad = dot_nt(one_head(values, head), grads)
            score_grad = (probs * (prob_grad - delta[head : head + 1, :]) * scale).astype(jnp.bfloat16)
            value_parts.append(dot_nn(probs.astype(jnp.bfloat16), grads))
            key_parts.append(dot_nn(score_grad, queries))
            here = slice(head * HD, (head + 1) * HD)
            part = dot_nn(keys_turned[here, :], score_grad)
            if start == 0:
                turned_ref[here, :] = part
            else:
                turned_ref[here, :] += part
        half = lane_half((block, LANES))
        key_grad = jnp.where(half, key_parts[0], key_parts[1])
        value_grad = jnp.where(half, value_parts[0], value_parts[1])
        key_grad = key_grad * cos_ref[rows, :] - swap_halves(key_grad) * sin_ref[rows, :]
        out_ref[rows, LANES : 2 * LANES] = key_grad.astype(jnp.bfloat16)
        out_ref[rows, 2 * LANES :] = value_grad.astype(jnp.bfloat16)
    query_grad = turned_ref[...].T
    query_grad = query_grad * cos_ref[...] - swap_halves(query_grad) * sin_ref[...]
    out_ref[:, :LANES] = query_grad.astype(jnp.bfloat16)


def attention_backward(queries, keys, values, grads, raw, lse, cosine, sine, seg_row):
    length = queries.shape[0]
    return pl.pallas_call(
        attention_backward_kernel,
        name="attention_backward",
        out_shape=jax.ShapeDtypeStruct((length, 3 * LANES), jnp.bfloat16),
        scratch_shapes=[pltpu.VMEM((LANES, length), jnp.float32)],
        compiler_params=pltpu.CompilerParams(vmem_limit_bytes=WIDE_VMEM),
        cost_estimate=pl.CostEstimate(
            flops=20 * length * length * LANES,
            bytes_accessed=12 * length * LANES * 2,
            transcendentals=2 * length * length,
        ),
    )(
        queries, keys, values, grads, raw, lse, cosine, sine,
        seg_row.reshape(length, 1), seg_row.reshape(1, length),
    )


def short_sequences(
    tokens, segments, attn_gain, qkv_weight, out_weight, mlp_gain, inner_weight, outer_weight, cotangent
):
    f = lax.axis_index("fsdp")
    c = lax.axis_index("ctx")
    t = lax.axis_index("tp")
    row_count, width = tokens.shape[1:]
    half_rows = row_count // 2
    shard = attn_gain.shape[0]
    units = inner_weight.shape[2]
    length = segments.shape[1]
    seg_row = segments[0]
    own_tokens = tokens[0]
    out_cot = cotangent[0]
    f_order = [f ^ r for r in range(4)]
    c_order = [c ^ r for r in range(4)]

    def across(value):
        return hop(value, "fsdp", 2, 4)

    def beside(value):
        return hop(value, "fsdp", 1, 4)

    def over_tp(value):
        return hop(value, "tp", 1, 2)

    def gathered(value, crossed):
        return place([value, beside(value), crossed, beside(crossed)], f_order)

    gains = jnp.stack([attn_gain, mlp_gain])
    gain_parts = [gains] + [hop(gains, "fsdp", r, 4) for r in (1, 2, 3)]
    gain_all = place([g[None] for g in gain_parts], f_order).reshape(4, 2, shard)
    gain_one = gain_all[:, 0].reshape(1, width).astype(jnp.float32)
    gain_two = gain_all[:, 1].reshape(1, width).astype(jnp.float32)

    head_cols = qkv_weight.shape[2] // 4
    by_ctx = qkv_weight.reshape(shard, 3, 4, head_cols).transpose(2, 0, 1, 3).reshape(4, shard, 3 * head_cols)
    qkv_own = pick(by_ctx, c)
    qkv_rest = jnp.concatenate([pick(by_ctx, c ^ r) for r in (1, 2, 3)], axis=1)
    out_blocks = out_weight.reshape(4, head_cols, shard)
    out_own = jnp.concatenate([pick(out_blocks, c ^ r).T for r in range(4)], axis=1)
    gate_own, up_own = inner_weight[:, 0], inner_weight[:, 1]
    outer_own = outer_weight.T

    qkv_crossed = across(qkv_own)
    qkv_here = gathered(qkv_own, qkv_crossed)
    out_pair = jnp.concatenate([out_own, over_tp(out_own)], axis=1)
    out_pair = after(out_pair, qkv_crossed)
    out_crossed = across(out_pair)
    out_all = gathered(out_pair, out_crossed)
    gate_own = after(gate_own, out_crossed)
    gate_crossed = across(gate_own)
    gate_all = gathered(gate_own, gate_crossed)
    up_own = after(up_own, gate_crossed)
    up_crossed = across(up_own)
    up_all = gathered(up_own, up_crossed)
    outer_own = after(outer_own, up_crossed)
    outer_crossed = across(outer_own)
    outer_all = gathered(outer_own, outer_crossed)
    qkv_rest = after(qkv_rest, outer_crossed)
    rest_crossed = across(qkv_rest)
    rest_all = gathered(qkv_rest, rest_crossed)

    own_half = lax.dynamic_slice_in_dim(own_tokens, t * half_rows, half_rows)
    upward, downward = own_half, own_half
    sequence = jnp.zeros((4, 2, half_rows, width), own_tokens.dtype)
    halves = {}
    for step in (1, 2, 3):
        upward = lax.ppermute(upward, "ctx", [(i, i + 1) for i in range(3)])
        downward = lax.ppermute(downward, "ctx", [(i, i - 1) for i in range(1, 4)])
        pairs_up = [(i * 2 + j, i * 2 + 1 - j) for i in range(step, 4) for j in range(2)]
        pairs_down = [(i * 2 + j, i * 2 + 1 - j) for i in range(0, 4 - step) for j in range(2)]
        halves["up", step] = (upward, lax.ppermute(upward, ("ctx", "tp"), pairs_up))
        halves["down", step] = (downward, lax.ppermute(downward, ("ctx", "tp"), pairs_down))
    blocks = [own_tokens]
    for ahead in (1, 2, 3):
        inside = c + ahead < 4
        mine = jnp.where(inside, halves["down", ahead][0], halves["up", 4 - ahead][0])
        theirs = jnp.where(inside, halves["down", ahead][1], halves["up", 4 - ahead][1])
        blocks.append(
            jnp.concatenate([jnp.where(t == 0, mine, theirs), jnp.where(t == 0, theirs, mine)], axis=0)
        )
    x_all = place(blocks, [lax.rem(c + ahead, 4) for ahead in range(4)])

    cosine, sine = angle_tables(length, 0, HD)
    sign = jnp.where(jnp.arange(HD) < HD // 2, -1.0, 1.0).astype(jnp.float32)
    cosine = jnp.concatenate([cosine[:, 0]] * 2, axis=1)
    sine = jnp.concatenate([sine[:, 0] * sign] * 2, axis=1)

    h_all, queries, keys, values, raw, low, lse = attention_forward(
        x_all, gain_one, qkv_here, cosine, sine, seg_row
    )

    place_index = c * 2 + t
    low_blocks = low.reshape(4, row_count, LANES)

    def with_partner(value, bits):
        return lax.ppermute(value, ("ctx", "tp"), [(i, i ^ bits) for i in range(8)])

    partner_bits = [2 * k + b for b in range(2) for k in range(4)]
    head_parts = []
    for bits in partner_bits:
        part = pick(low_blocks, (place_index ^ bits) >> 1)
        head_parts.append(part if bits == 0 else with_partner(part, bits))
    attended = jnp.concatenate(head_parts, axis=1)
    attended_half = place(
        [p.T for p in head_parts[:4]], c_order
    )

    input_rows = own_tokens.astype(jnp.float32)
    middle = input_rows + dot_nt(attended, out_all)
    normed_two, norm_two_back = jax.vjp(lambda v: normalize(v, 1.0), middle)
    second_low = (normed_two * gain_two).astype(jnp.bfloat16)
    gate_in = dot_nn(second_low, gate_all)
    up_in = dot_nn(second_low, up_all)
    hidden, geglu_back = jax.vjp(geglu, gate_in, up_in)
    hidden_low = hidden.astype(jnp.bfloat16)
    hidden_grad = dot_nn(out_cot, outer_all)
    gate_grad, up_grad = geglu_back(hidden_grad)
    gate_grad, up_grad = gate_grad.astype(jnp.bfloat16), up_grad.astype(jnp.bfloat16)
    second_part = dot_nt(gate_grad, gate_all) + dot_nt(up_grad, up_all)
    second_low_part = second_part.astype(jnp.bfloat16)

    part_halves = second_low_part.reshape(2, half_rows, width)
    other_half = over_tp(pick(part_halves, 1 - t))
    second_grad = pick(part_halves, t).astype(jnp.float32) + other_half.astype(jnp.float32)
    half_start = t * half_rows
    middle_half = lax.dynamic_slice_in_dim(middle, half_start, half_rows)
    unused, half_back = jax.vjp(lambda v: normalize(v, 1.0), middle_half)
    middle_grad = (
        lax.dynamic_slice_in_dim(out_cot, half_start, half_rows).astype(jnp.float32)
        + half_back(second_grad * gain_two)[0]
    )
    attn_low = middle_grad.astype(jnp.bfloat16)
    head_grads = dot_nn(attn_low, out_all).astype(jnp.bfloat16)
    grad_parts = []
    for at, bits in enumerate(partner_bits):
        part = head_grads[:, at * LANES : (at + 1) * LANES]
        grad_parts.append(part if bits == 0 else with_partner(part, bits))
    head_grad_all = place(grad_parts, [place_index ^ bits for bits in partner_bits])

    projected_grad = attention_backward(
        queries, keys, values, head_grad_all, raw, lse, cosine, sine, seg_row
    )

    mlp_part = dot_nt(hidden_low, outer_all).astype(jnp.bfloat16)
    mlp_part = lax.optimization_barrier(mlp_part)
    block_out = (
        middle + (mlp_part.astype(jnp.float32) + over_tp(mlp_part).astype(jnp.float32))
    ).astype(jnp.bfloat16)

    def over_fsdp(whole):
        pieces = whole.reshape(4, shard, whole.shape[1])
        first = pick(pieces, f) + beside(pick(pieces, f ^ 1))
        second = pick(pieces, f ^ 2) + beside(pick(pieces, f ^ 3))
        return first + across(second)

    at_end = jnp.logical_or(c == 0, c == 3)

    def over_line(value):
        value = value + lax.ppermute(value, "ctx", [(0, 1), (3, 2)])
        value = value + lax.ppermute(value, "ctx", [(1, 2), (2, 1)])
        value = lax.optimization_barrier(value)
        return jnp.where(at_end, lax.ppermute(value, "ctx", [(1, 0), (2, 3)]), value)

    outer_sum = over_line(over_fsdp(dot_tn(out_cot, hidden_low).astype(jnp.bfloat16)))
    gate_sum = over_line(over_fsdp(dot_tn(second_low, gate_grad).astype(jnp.bfloat16)))
    up_sum = over_line(over_fsdp(dot_tn(second_low, up_grad).astype(jnp.bfloat16)))
    attn_other = over_tp(attn_low)
    attn_full = jnp.concatenate(
        [jnp.where(t == 0, attn_low, attn_other), jnp.where(t == 0, attn_other, attn_low)], axis=0
    )
    out_sum = over_line(over_fsdp(dot_nn(attn_full.T, attended_half.T).astype(jnp.bfloat16)))

    qkv_sum = over_fsdp(dot_tn(h_all, projected_grad).astype(jnp.bfloat16))
    qkv_sum = lax.optimization_barrier(qkv_sum)
    qkv_parts = [qkv_sum] + [hop(qkv_sum, "ctx", r, 4) for r in (1, 2, 3)]
    qkv_grad = place([p[None] for p in qkv_parts], c_order).reshape(4, shard, 3, head_cols)
    qkv_grad = qkv_grad.transpose(1, 2, 0, 3).reshape(shard, 3, 4 * head_cols).astype(jnp.float32)

    grad_blocks = projected_grad.reshape(4, row_count, 3 * LANES)
    first_parts = [pick(grad_blocks, c)] + [
        hop(pick(grad_blocks, c ^ r), "ctx", r, 4) for r in (1, 2, 3)
    ]
    first_part = dot_nt(first_parts[0], qkv_here) + dot_nt(
        jnp.concatenate(first_parts[1:], axis=1), rest_all
    )
    first_low_part = lax.optimization_barrier(first_part.astype(jnp.bfloat16))
    first_grad = first_low_part.astype(jnp.float32) + over_tp(first_low_part).astype(jnp.float32)
    normed_one, norm_one_back = jax.vjp(lambda v: normalize(v, 1.0), input_rows)
    input_grad = attn_full.astype(jnp.float32) + norm_one_back(first_grad * gain_one)[0]

    gain_parts = jnp.stack([jnp.sum(first_part * normed_one, axis=0), jnp.sum(second_part * normed_two, axis=0)])
    gain_parts = gain_parts + over_tp(gain_parts)
    gain_pieces = gain_parts.reshape(2, 4, shard).transpose(1, 0, 2)
    summed = [pick(gain_pieces, f)] + [hop(pick(gain_pieces, f ^ r), "fsdp", r, 4) for r in (1, 2, 3)]
    summed = lax.optimization_barrier((summed[0] + summed[1]) + (summed[2] + summed[3]))
    summed = [summed] + [hop(summed, "ctx", r, 4) for r in (1, 2, 3)]
    summed = (summed[0] + summed[1]) + (summed[2] + summed[3])

    return (
        block_out[None],
        input_grad[None],
        summed[0],
        qkv_grad,
        out_sum.astype(jnp.float32).T,
        summed[1],
        jnp.stack([gate_sum, up_sum], axis=1).astype(jnp.float32),
        outer_sum.astype(jnp.float32).T,
    )


def solution(mesh):
    placed = (
        P("fsdp", "ctx", None),
        P("fsdp", None),
        P("fsdp"),
        P("fsdp", None, "tp"),
        P("tp", "fsdp"),
        P("fsdp"),
        P("fsdp", None, "tp"),
        P("tp", "fsdp"),
        P("fsdp", "ctx", None),
    )
    sizes = dict(mesh.shape)

    def layer(*args):
        tokens, segments, qkv_weight = args[0], args[1], args[3]
        heads_apart = qkv_weight.shape[2] == 4 * LANES
        short = segments.shape[1] == 4 * tokens.shape[1] and segments.shape[1] <= 1024
        small = (sizes["fsdp"], sizes["ctx"], sizes["tp"]) == (4, 4, 2)
        if small and short and heads_apart and tokens.shape[0] == 1:
            return short_sequences(*args)
        return per_device(*args)

    return jax.shard_map(
        layer,
        mesh=mesh,
        in_specs=placed,
        out_specs=(
            P("fsdp", "ctx", None),
            P("fsdp", "ctx", None),
            P("fsdp"),
            P("fsdp", None, "tp"),
            P("tp", "fsdp"),
            P("fsdp"),
            P("fsdp", None, "tp"),
            P("tp", "fsdp"),
        ),
        check_vma=False,
    )
```

```python
import functools
import math

import jax
import jax.numpy as jnp
from jax import lax
from jax.experimental import pallas as pl
from jax.experimental.pallas import tpu as pltpu
from jax.sharding import PartitionSpec as P

HD = 64


EPSILON = 1e-05
ROPE_BASE = 160000.0
MASKED = -1e30


def normalize(values, gain_row):
    row_mean = jnp.mean(values, axis=-1, keepdims=True)
    centered = values - row_mean
    spread = jnp.mean(centered * centered, axis=-1, keepdims=True)
    return centered * lax.rsqrt(spread + EPSILON) * gain_row


def geglu(gate_in, upper):
    return jax.nn.gelu(gate_in, approximate=False) * upper


def angle_tables(row_count, offset, depth):
    half_width = depth // 2
    inverse = jnp.power(
        jnp.float32(ROPE_BASE), -(2.0 * jnp.arange(half_width, dtype=jnp.float32)) / depth
    )
    places = (offset + jnp.arange(row_count, dtype=jnp.int32)).astype(jnp.float32)
    angles = places[:, None] * inverse[None, :]
    angles = jnp.concatenate([angles, angles], axis=-1)
    return (jnp.cos(angles)[:, None, :], jnp.sin(angles)[:, None, :])


def rotate(values, cosine, sine):
    half_width = values.shape[-1] // 2
    turned = jnp.concatenate([-values[..., half_width:], values[..., :half_width]], axis=-1)
    return values * cosine + turned * sine


def rotate_back(grad_in, cosine, sine):
    half_width = grad_in.shape[-1] // 2
    scaled = grad_in * sine
    turned = jnp.concatenate([scaled[..., half_width:], -scaled[..., :half_width]], axis=-1)
    return grad_in * cosine + turned


def attend_forward(queries, query_seg, seg_row, key_low, value_low, score_scale):
    row_count, heads_here, depth = queries.shape
    initial = (
        jnp.full((heads_here, row_count), MASKED, jnp.float32),
        jnp.zeros((heads_here, row_count), jnp.float32),
        jnp.zeros((row_count, heads_here, depth), jnp.float32),
    )
    key_piece = lax.all_gather(key_low, "ctx", axis=0, tiled=True)
    value_piece = lax.all_gather(value_low, "ctx", axis=0, tiled=True)
    piece_rows = key_piece.shape[0]
    block_size = math.gcd(piece_rows, 512)
    blocks = (
        key_piece.reshape(piece_rows // block_size, block_size, heads_here, depth),
        value_piece.reshape(piece_rows // block_size, block_size, heads_here, depth),
        seg_row.reshape(piece_rows // block_size, block_size),
    )

    def step(state, block_data):
        running_peak, running_total, accum = state
        key_block, value_block, block_seg = block_data
        scores = jnp.einsum("qhe,khe->hqk", queries, key_block, preferred_element_type=jnp.float32)
        same_doc = (query_seg[:, None] == block_seg[None, :])[None]
        logits = jnp.where(same_doc, scores * score_scale, MASKED)
        new_peak = jnp.maximum(running_peak, jnp.max(logits, axis=-1))
        rescale = jnp.exp(running_peak - new_peak)
        weights = jnp.where(same_doc, jnp.exp(logits - new_peak[:, :, None]), 0.0)
        running_total = running_total * rescale + jnp.sum(weights, axis=-1)
        mixed_out = jnp.einsum(
            "hqk,khe->qhe",
            weights.astype(jnp.bfloat16),
            value_block,
            preferred_element_type=jnp.float32,
        )
        accum = accum * rescale.T[:, :, None] + mixed_out
        return ((new_peak, running_total, accum), None)

    result, unused = lax.scan(step, initial, blocks)
    running_peak, running_total, accum = result
    return (accum / running_total.T[:, :, None], running_peak + jnp.log(running_total))


def probs_and_grads(
    query_block, key_block, grad_block, value_block, same_doc, log_total, delta_rows, score_scale
):
    scores = jnp.einsum("qhe,khe->hqk", query_block, key_block, preferred_element_type=jnp.float32)
    probs = jnp.where(same_doc, jnp.exp(scores * score_scale - log_total[:, :, None]), 0.0)
    prob_grad = jnp.einsum(
        "qhe,khe->hqk", grad_block, value_block, preferred_element_type=jnp.float32
    )
    score_grad = (probs * (prob_grad - delta_rows[:, :, None]) * score_scale).astype(jnp.bfloat16)
    return (probs.astype(jnp.bfloat16), score_grad)


def attend_backward(
    queries, key_low, value_low, grad_low, log_total, delta_rows, query_seg, seg_row, score_scale
):
    row_count, heads_here, depth = queries.shape
    seq_length = seg_row.shape[0]
    block_size = math.gcd(seq_length, 512)
    block_count = seq_length // block_size
    key_all, value_all = (
        lax.all_gather(key_low, "ctx", axis=0, tiled=True),
        lax.all_gather(value_low, "ctx", axis=0, tiled=True),
    )
    blocks = (
        key_all.reshape(block_count, block_size, heads_here, depth),
        value_all.reshape(block_count, block_size, heads_here, depth),
        seg_row.reshape(block_count, block_size),
    )

    def key_step(query_acc, block_data):
        key_block, value_block, block_seg = block_data
        same_doc = (query_seg[:, None] == block_seg[None, :])[None]
        prob_low, score_grad = probs_and_grads(
            queries, key_block, grad_low, value_block, same_doc, log_total, delta_rows, score_scale
        )
        query_acc = query_acc + jnp.einsum(
            "hqk,khe->qhe", score_grad, key_block, preferred_element_type=jnp.float32
        )
        key_part = jnp.einsum(
            "hqk,qhe->khe", score_grad, queries, preferred_element_type=jnp.float32
        )
        value_part = jnp.einsum(
            "hqk,qhe->khe", prob_low, grad_low, preferred_element_type=jnp.float32
        )
        return (query_acc, (key_part, value_part))

    query_grad, key_value_parts = lax.scan(
        key_step, jnp.zeros((row_count, heads_here, depth), jnp.float32), blocks
    )
    key_parts = key_value_parts[0].reshape(seq_length, heads_here * depth)
    value_parts = key_value_parts[1].reshape(seq_length, heads_here * depth)
    key_grad, value_grad = (
        lax.psum_scatter(
            key_parts.astype(jnp.bfloat16), "ctx", scatter_dimension=0, tiled=True
        ).astype(jnp.float32),
        lax.psum_scatter(
            value_parts.astype(jnp.bfloat16), "ctx", scatter_dimension=0, tiled=True
        ).astype(jnp.float32),
    )
    key_grad = key_grad.reshape(row_count, heads_here, depth)
    value_grad = value_grad.reshape(row_count, heads_here, depth)
    return (query_grad, key_grad, value_grad)


def per_device(
    tokens,
    segments,
    attn_gain,
    qkv_weight,
    out_weight,
    mlp_gain,
    inner_weight,
    outer_weight,
    cotangent,
):
    qkv_full, out_full, gain_one = (
        lax.all_gather(qkv_weight, "fsdp", axis=0, tiled=True),
        lax.all_gather(out_weight, "fsdp", axis=1, tiled=True),
        lax.all_gather(attn_gain, "fsdp", axis=0, tiled=True),
    )
    inner_full, outer_full, gain_two = (
        lax.all_gather(inner_weight, "fsdp", axis=0, tiled=True),
        lax.all_gather(outer_weight, "fsdp", axis=1, tiled=True),
        lax.all_gather(mlp_gain, "fsdp", axis=0, tiled=True),
    )
    seq_count, row_count, model_width = tokens.shape
    local_width = qkv_full.shape[2]
    heads_here = local_width // HD
    score_scale = HD ** (-0.5)
    offset = lax.axis_index("ctx") * row_count
    cosine, sine = angle_tables(row_count, offset, HD)
    input_rows = tokens.reshape(-1, model_width).astype(jnp.float32)
    normed_one, norm_one_back = jax.vjp(normalize, input_rows, gain_one.astype(jnp.float32))
    first_low = normed_one.astype(jnp.bfloat16)
    projected_output = jnp.einsum(
        "td,dcf->tcf", first_low, qkv_full, preferred_element_type=jnp.float32
    )
    projected_output = projected_output.reshape(seq_count, row_count, 3, heads_here, HD)
    query_low = rotate(projected_output[:, :, 0], cosine, sine).astype(jnp.bfloat16)
    key_low = rotate(projected_output[:, :, 1], cosine, sine).astype(jnp.bfloat16)
    value_low = projected_output[:, :, 2].astype(jnp.bfloat16)
    seq_index = 0
    seg_row = segments[seq_index]
    query_seg = lax.dynamic_slice_in_dim(seg_row, offset, row_count)
    raw_out, log_total = attend_forward(
        query_low[seq_index],
        query_seg,
        seg_row,
        key_low[seq_index],
        value_low[seq_index],
        score_scale,
    )
    query_segs = [query_seg]
    raw_outs = [raw_out]
    log_totals = [log_total]
    attended_low = jnp.stack(raw_outs).astype(jnp.bfloat16).reshape(-1, local_width)
    attn_part = jnp.dot(attended_low, out_full, preferred_element_type=jnp.float32)
    middle_activation = input_rows + lax.psum(attn_part.astype(jnp.bfloat16), "tp").astype(
        jnp.float32
    )
    normed_two, norm_two_back = jax.vjp(normalize, middle_activation, gain_two.astype(jnp.float32))
    second_low = normed_two.astype(jnp.bfloat16)
    hidden_input = jnp.einsum(
        "td,dcf->tcf", second_low, inner_full, preferred_element_type=jnp.float32
    )
    hidden_state, geglu_back = jax.vjp(geglu, hidden_input[:, 0], hidden_input[:, 1])
    hidden_low = hidden_state.astype(jnp.bfloat16)
    mlp_part = jnp.dot(hidden_low, outer_full, preferred_element_type=jnp.float32)
    block_out = (
        middle_activation + lax.psum(mlp_part.astype(jnp.bfloat16), "tp").astype(jnp.float32)
    ).astype(jnp.bfloat16)
    out_cot = cotangent.reshape(-1, model_width)
    outer_local = jnp.einsum("tf,td->fd", hidden_low, out_cot, preferred_element_type=jnp.float32)
    hidden_grad = jnp.einsum("td,fd->tf", out_cot, outer_full, preferred_element_type=jnp.float32)
    gate_grad, up_grad = geglu_back(hidden_grad)
    inner_low = jnp.stack([gate_grad, up_grad], axis=1).astype(jnp.bfloat16)
    inner_local = jnp.einsum(
        "td,tcf->dcf", second_low, inner_low, preferred_element_type=jnp.float32
    )
    normed_two_grad = lax.psum(
        jnp.einsum("tcf,dcf->td", inner_low, inner_full, preferred_element_type=jnp.float32).astype(
            jnp.bfloat16
        ),
        "tp",
    ).astype(jnp.float32)
    middle_part, gain_two_grad = norm_two_back(normed_two_grad)
    middle_grad = out_cot.astype(jnp.float32) + middle_part
    attn_low = middle_grad.astype(jnp.bfloat16)
    out_local = jnp.einsum("tf,td->fd", attended_low, attn_low, preferred_element_type=jnp.float32)
    attended_grad = jnp.einsum("td,fd->tf", attn_low, out_full, preferred_element_type=jnp.float32)
    attended_grad = attended_grad.astype(jnp.bfloat16).reshape(seq_count, row_count, heads_here, HD)
    seq_index = 0
    grad_low = attended_grad[seq_index]
    delta_rows = jnp.sum(grad_low.astype(jnp.float32) * raw_outs[seq_index], axis=-1).T
    query_grad, key_grad, value_grad = attend_backward(
        query_low[seq_index],
        key_low[seq_index],
        value_low[seq_index],
        grad_low,
        log_totals[seq_index],
        delta_rows,
        query_segs[seq_index],
        segments[seq_index],
        score_scale,
    )
    stacked = jnp.stack(
        [rotate_back(query_grad, cosine, sine), rotate_back(key_grad, cosine, sine), value_grad],
        axis=1,
    )
    qkv_grads = stacked.reshape(row_count, 3, local_width)
    qkv_low = qkv_grads.astype(jnp.bfloat16)
    qkv_local = jnp.einsum("td,tcf->dcf", first_low, qkv_low, preferred_element_type=jnp.float32)
    normed_one_grad = lax.psum(
        jnp.einsum("tcf,dcf->td", qkv_low, qkv_full, preferred_element_type=jnp.float32).astype(
            jnp.bfloat16
        ),
        "tp",
    ).astype(jnp.float32)
    input_part, gain_one_grad = norm_one_back(normed_one_grad)
    input_grad = (middle_grad + input_part).reshape(tokens.shape)
    summed = (
        lax.psum_scatter(gain_one_grad, ("fsdp", "ctx"), scatter_dimension=0, tiled=True),
        lax.psum_scatter(qkv_local, ("fsdp", "ctx"), scatter_dimension=0, tiled=True),
        lax.psum_scatter(out_local, ("fsdp", "ctx"), scatter_dimension=1, tiled=True),
        lax.psum_scatter(gain_two_grad, ("fsdp", "ctx"), scatter_dimension=0, tiled=True),
        lax.psum_scatter(inner_local, ("fsdp", "ctx"), scatter_dimension=0, tiled=True),
        lax.psum_scatter(outer_local, ("fsdp", "ctx"), scatter_dimension=1, tiled=True),
    )
    gain_one_sum, qkv_sum, out_sum, gain_two_sum, inner_sum, outer_sum = summed
    shards = (
        lax.all_gather(gain_one_sum.astype(jnp.bfloat16), "ctx", axis=0, tiled=True).astype(
            gain_one_sum.dtype
        ),
        lax.all_gather(qkv_sum.astype(jnp.bfloat16), "ctx", axis=0, tiled=True).astype(
            qkv_sum.dtype
        ),
        lax.all_gather(out_sum.astype(jnp.bfloat16), "ctx", axis=1, tiled=True).astype(
            out_sum.dtype
        ),
        lax.all_gather(gain_two_sum.astype(jnp.bfloat16), "ctx", axis=0, tiled=True).astype(
            gain_two_sum.dtype
        ),
        lax.all_gather(inner_sum.astype(jnp.bfloat16), "ctx", axis=0, tiled=True).astype(
            inner_sum.dtype
        ),
        lax.all_gather(outer_sum.astype(jnp.bfloat16), "ctx", axis=1, tiled=True).astype(
            outer_sum.dtype
        ),
    )
    return (
        block_out.reshape(tokens.shape),
        input_grad,
        shards[0],
        shards[1],
        shards[2],
        shards[3],
        shards[4],
        shards[5],
    )


LANES = 128
BLOCK = 256
WIDE_VMEM = 50 * 1024 * 1024


def hop(value, axis, bit, count):
    return lax.ppermute(value, axis, [(i, i ^ bit) for i in range(count)])


def after(value, *earlier):
    return lax.optimization_barrier((value,) + earlier)[0]


def place(pieces, indices):
    whole = jnp.zeros((len(pieces),) + pieces[0].shape, pieces[0].dtype)
    for piece, index in zip(pieces, indices):
        whole = lax.dynamic_update_index_in_dim(whole, piece, index, 0)
    return whole.reshape((-1,) + pieces[0].shape[1:])


def lane_half(shape):
    return lax.broadcasted_iota(jnp.int32, shape, 1) < HD


def swap_halves(values):
    lane = lax.broadcasted_iota(jnp.int32, values.shape, 1)
    low_part = lax.rem(lane, HD) < HD // 2
    return jnp.where(
        low_part,
        pltpu.roll(values, LANES - HD // 2, 1),
        pltpu.roll(values, HD // 2, 1),
    )


def dot_nt(left, right):
    return lax.dot_general(left, right, (((1,), (1,)), ((), ())), preferred_element_type=jnp.float32)


def dot_nn(left, right):
    return lax.dot_general(left, right, (((1,), (0,)), ((), ())), preferred_element_type=jnp.float32)


def dot_tn(left, right):
    return lax.dot_general(left, right, (((0,), (0,)), ((), ())), preferred_element_type=jnp.float32)


def one_head(values, head):
    first = lane_half(values.shape)
    keep = first if head == 0 else jnp.logical_not(first)
    return jnp.where(keep, values, jnp.zeros_like(values))


def part_of(index, size):
    return pl.ds(pl.multiple_of(index * size, size), size)


def standardize(values):
    row_mean = jnp.mean(values, axis=-1, keepdims=True)
    centered = values - row_mean
    spread = jnp.mean(centered * centered, axis=-1, keepdims=True)
    scale = lax.rsqrt(spread + EPSILON)
    return centered * scale, scale


def standardize_back(normed, scale, grad):
    inner = jnp.mean(grad * normed, axis=-1, keepdims=True)
    return scale * (grad - jnp.mean(grad, axis=-1, keepdims=True) - normed * inner)


def local_call(body, outs, places, operands, scratch=(), flops=0, transcendentals=0):
    moved = sum(math.prod(o.shape) * o.dtype.itemsize for o in list(operands) + list(outs))
    return pl.pallas_call(
        body,
        name=body.__name__ if hasattr(body, "__name__") else body.func.__name__,
        out_shape=tuple(outs),
        in_specs=[pl.BlockSpec(memory_space=pltpu.SMEM)]
        + [pl.BlockSpec(memory_space=pltpu.VMEM)] * len(operands),
        out_specs=tuple([pl.BlockSpec(memory_space=pltpu.VMEM)] * len(outs)),
        scratch_shapes=list(scratch),
        compiler_params=pltpu.CompilerParams(vmem_limit_bytes=WIDE_VMEM),
        cost_estimate=pl.CostEstimate(
            flops=int(flops), bytes_accessed=int(moved), transcendentals=int(transcendentals)
        ),
    )(places, *operands)


def low_shape(*shape):
    return jax.ShapeDtypeStruct(shape, jnp.bfloat16)


def wide_shape(*shape):
    return jax.ShapeDtypeStruct(shape, jnp.float32)


def attention_forward(
    at, own, u1, u2, u3, d1, d2, d3, v1, v2, v3, e1, e2, e3,
    gain_ref, w0, w1, w2, w3, cos_ref, sin_ref, seg_col, seg_line,
    h0, h1, h2, h3, q_ref, k_ref, v_ref, raw_ref, l0, l1, l2, l3, lse_ref,
    x_ref,
):
    f, c, t = at[0], at[1], at[2]
    rows_here = own.shape[0]
    half = rows_here // 2
    x_ref[part_of(c, rows_here), :] = own[...]
    for ahead, down, down_other, up, up_other in (
        (1, d1, e1, u3, v3), (2, d2, e2, u2, v2), (3, d3, e3, u1, v1)
    ):
        block = lax.rem(c + ahead, 4)
        mine, theirs = part_of(block * 2 + t, half), part_of(block * 2 + 1 - t, half)

        @pl.when(c + ahead < 4)
        def _():
            x_ref[mine, :] = down[...]
            x_ref[theirs, :] = down_other[...]

        @pl.when(c + ahead >= 4)
        def _():
            x_ref[mine, :] = up[...]
            x_ref[theirs, :] = up_other[...]

    gain = gain_ref[...]
    for k, h_ref in enumerate((h0, h1, h2, h3)):
        rows = part_of(c ^ k, rows_here)
        h_ref[...] = (standardize(x_ref[rows, :].astype(jnp.float32))[0] * gain).astype(jnp.bfloat16)
        projected = 0.0
        for r, weight in enumerate((w0, w1, w2, w3)):
            projected += dot_nn(h_ref[:, part_of(f ^ r, weight.shape[0])], weight[...])
        cosine, sine = cos_ref[rows, :], sin_ref[rows, :]
        for ref, part in ((q_ref, projected[:, :LANES]), (k_ref, projected[:, LANES : 2 * LANES])):
            ref[rows, :] = (part * cosine + swap_halves(part) * sine).astype(jnp.bfloat16)
        v_ref[rows, :] = projected[:, 2 * LANES :].astype(jnp.bfloat16)
    for k, low_ref in reversed(list(enumerate((l0, l1, l2, l3)))):
        rows = part_of(c ^ k, rows_here)
        queries = q_ref[rows, :] * jnp.bfloat16(HD ** (-0.5))
        same = seg_col[rows, :] == seg_line[...]
        outs, logs = [], []
        for head in range(2):
            scores = dot_nt(one_head(queries, head), k_ref[...])
            scores = jnp.where(same, scores, MASKED)
            peak = jnp.max(scores, axis=1, keepdims=True)
            weights = jnp.exp(scores - peak)
            total = jnp.sum(weights, axis=1, keepdims=True)
            probs = (weights * (1.0 / total)).astype(jnp.bfloat16)
            outs.append(dot_nn(probs, v_ref[...]))
            logs.append(peak + jnp.log(total))
        raw = jnp.where(lane_half(outs[0].shape), outs[0], outs[1])
        raw_ref[rows, :] = raw
        low_ref[...] = raw.astype(jnp.bfloat16)
        lane = lax.broadcasted_iota(jnp.int32, (rows_here, LANES), 1)
        lse_ref[:, rows] = jnp.where(lane == 0, logs[0], logs[1]).T[:8, :]


def attention_backward(
    at, q_ref, k_ref, v_ref, g0, g1, g2, g3, g4, g5, g6, g7, raw_ref, lse_ref, cos_ref, sin_ref,
    seg_col, seg_line, o0, o1, o2, o3, turned_ref, do_ref,
):
    c, t = at[1], at[2]
    outs = (o0, o1, o2, o3)
    length = q_ref.shape[0]
    rows_here = o0.shape[0]
    for at_part, grad_ref in enumerate((g0, g1, g2, g3, g4, g5, g6, g7)):
        block = (c ^ (at_part % 4)) * 2 + (t ^ (at_part // 4))
        do_ref[part_of(block, rows_here // 2), :] = grad_ref[...]
    grads = do_ref[...]
    product = grads.astype(jnp.float32) * raw_ref[...]
    first = lane_half(product.shape)
    whole = jnp.sum(jnp.where(first, product, 0.0), axis=1, keepdims=True)
    other = jnp.sum(jnp.where(first, 0.0, product), axis=1, keepdims=True)
    lane = lax.broadcasted_iota(jnp.int32, product.shape, 1)
    delta = jnp.where(lane == 0, whole, other).T
    scale = HD ** (-0.5)
    queries = q_ref[...]
    scaled = queries * jnp.bfloat16(scale)
    for k, out_ref in enumerate(outs):
        rows = part_of(c ^ k, rows_here)
        keys, values = k_ref[rows, :], v_ref[rows, :]
        keys_turned = keys.T
        same = seg_col[rows, :] == seg_line[...]
        key_parts, value_parts = [], []
        for head in range(2):
            scores = dot_nt(one_head(keys, head), scaled)
            probs = jnp.where(same, jnp.exp(scores - lse_ref[head : head + 1, :]), 0.0)
            prob_grad = dot_nt(one_head(values, head), grads)
            score_grad = (probs * (prob_grad - delta[head : head + 1, :]) * scale).astype(jnp.bfloat16)
            value_parts.append(dot_nn(probs.astype(jnp.bfloat16), grads))
            key_parts.append(dot_nn(score_grad, queries))
            here = slice(head * HD, (head + 1) * HD)
            part = dot_nn(keys_turned[here, :], score_grad)
            if k == 0:
                turned_ref[here, :] = part
            else:
                turned_ref[here, :] += part
        half = lane_half(key_parts[0].shape)
        key_grad = jnp.where(half, key_parts[0], key_parts[1])
        value_grad = jnp.where(half, value_parts[0], value_parts[1])
        key_grad = key_grad * cos_ref[rows, :] - swap_halves(key_grad) * sin_ref[rows, :]
        out_ref[:, LANES : 2 * LANES] = key_grad.astype(jnp.bfloat16)
        out_ref[:, 2 * LANES :] = value_grad.astype(jnp.bfloat16)
    for k, out_ref in enumerate(outs):
        rows = part_of(c ^ k, rows_here)
        query_grad = turned_ref[:, rows].T
        query_grad = query_grad * cos_ref[rows, :] - swap_halves(query_grad) * sin_ref[rows, :]
        out_ref[:, :LANES] = query_grad.astype(jnp.bfloat16)


def feed_forward(
    at, p0, p1, p2, p3, p4, p5, p6, p7, x_ref, cot_ref, gain_ref,
    o0, o1, o2, o3, gate0, gate1, gate2, gate3, up0, up1, up2, up3, outer0, outer1, outer2, outer3,
    mid_ref, second_ref, hid_ref, dgate_ref, dup_ref, mine_ref, other_ref, gain_grad_ref,
    part_ref,
):
    f, t = at[0], at[2]
    attended = jnp.concatenate([p[...] for p in (p0, p1, p2, p3, p4, p5, p6, p7)], axis=1)
    columns = [part_of(f ^ r, o0.shape[0]) for r in range(4)]
    for r, weight in enumerate((o0, o1, o2, o3)):
        mid_ref[:, columns[r]] = x_ref[:, columns[r]].astype(jnp.float32) + dot_nt(attended, weight[...])
    normed, unused = standardize(mid_ref[...])
    second_ref[...] = (normed * gain_ref[...]).astype(jnp.bfloat16)
    units = gate0.shape[0]
    for start in range(0, units, BLOCK):
        here = slice(start, min(start + BLOCK, units))
        gate, up, hid_grad = 0.0, 0.0, 0.0
        for r in range(4):
            rows = second_ref[:, columns[r]]
            gate += dot_nt(rows, (gate0, gate1, gate2, gate3)[r][here, :])
            up += dot_nt(rows, (up0, up1, up2, up3)[r][here, :])
            hid_grad += dot_nt(cot_ref[:, columns[r]], (outer0, outer1, outer2, outer3)[r][here, :])
        below = 0.5 + 0.5 * lax.erf(gate * (2.0 ** -0.5))
        density = jnp.exp(-0.5 * gate * gate) * ((2.0 * math.pi) ** -0.5)
        active = gate * below
        hid_ref[:, here] = (active * up).astype(jnp.bfloat16)
        dgate_ref[:, here] = (hid_grad * up * (below + gate * density)).astype(jnp.bfloat16)
        dup_ref[:, here] = (hid_grad * active).astype(jnp.bfloat16)
    for r in range(4):
        part_ref[:, columns[r]] = dot_nn(dgate_ref[...], (gate0, gate1, gate2, gate3)[r][...]) + dot_nn(
            dup_ref[...], (up0, up1, up2, up3)[r][...]
        )
    half = mine_ref.shape[0]
    mine_ref[...] = part_ref[part_of(t, half), :].astype(jnp.bfloat16)
    other_ref[...] = part_ref[part_of(1 - t, half), :].astype(jnp.bfloat16)
    gain_grad_ref[...] = jnp.sum(part_ref[...] * normed, axis=0, keepdims=True)


def feed_forward_out(at, hid_ref, outer0, outer1, outer2, outer3, out_ref):
    f = at[0]
    for r, weight in enumerate((outer0, outer1, outer2, outer3)):
        out_ref[:, part_of(f ^ r, weight.shape[1])] = dot_nn(hid_ref[...], weight[...]).astype(jnp.bfloat16)


def head_gradients(
    at, mine_ref, other_ref, mid_ref, cot_ref, gain_ref, o0, o1, o2, o3,
    da_ref, d0, d1, d2, d3, d4, d5, d6, d7,
):
    f, t = at[0], at[2]
    rows = part_of(t, da_ref.shape[0])
    grad = (mine_ref[...].astype(jnp.float32) + other_ref[...].astype(jnp.float32)) * gain_ref[...]
    normed, scale = standardize(mid_ref[rows, :])
    mid_grad = cot_ref[rows, :].astype(jnp.float32) + standardize_back(normed, scale, grad)
    da_ref[...] = mid_grad.astype(jnp.bfloat16)
    total = 0.0
    for r, weight in enumerate((o0, o1, o2, o3)):
        total += dot_nn(da_ref[:, part_of(f ^ r, weight.shape[0])], weight[...])
    for at_part, ref in enumerate((d0, d1, d2, d3, d4, d5, d6, d7)):
        ref[...] = total[:, at_part * LANES : (at_part + 1) * LANES].astype(jnp.bfloat16)


def weight_gradients(count, at, *refs):
    f = at[0]
    lefts, rights, outs = refs[:count], refs[count : 2 * count], refs[2 * count :]
    for r in (1, 3, 2, 0):
        columns = part_of(f ^ r, outs[r].shape[1])
        outs[r][...] = sum(
            dot_tn(left[...], right[:, columns]) for left, right in zip(lefts, rights)
        ).astype(jnp.bfloat16)


def out_gradients(at, mine_ref, other_ref, p0, p1, p2, p3, w0, w1, w2, w3, full_ref, attended_ref):
    f, c, t = at[0], at[1], at[2]
    half = mine_ref.shape[0]
    full_ref[part_of(t, half), :] = mine_ref[...]
    full_ref[part_of(1 - t, half), :] = other_ref[...]
    for k, part in enumerate((p0, p1, p2, p3)):
        attended_ref[:, part_of(c ^ k, LANES)] = part[...]
    for r, out_ref in enumerate((w0, w1, w2, w3)):
        out_ref[...] = dot_tn(
            attended_ref[...], full_ref[:, part_of(f ^ r, out_ref.shape[1])]
        ).astype(jnp.bfloat16)


def first_gradients(
    at, g0, g1, g2, g3, x_ref, q0, q1, q2, q3, rest0, rest1, rest2, rest3, low_ref, gain_grad_ref, part_ref
):
    f = at[0]
    others = jnp.concatenate([g1[...], g2[...], g3[...]], axis=1)
    for r in range(4):
        own, rest = (q0, q1, q2, q3)[r], (rest0, rest1, rest2, rest3)[r]
        part_ref[:, part_of(f ^ r, own.shape[0])] = dot_nt(g0[...], own[...]) + dot_nt(others, rest[...])
    low_ref[...] = part_ref[...].astype(jnp.bfloat16)
    normed, unused = standardize(x_ref[...].astype(jnp.float32))
    gain_grad_ref[...] = jnp.sum(part_ref[...] * normed, axis=0, keepdims=True)


def input_gradients(at, mine_ref, other_ref, x_ref, gain_ref, da_mine, da_other, out_ref):
    t = at[2]
    half = da_mine.shape[0]
    grad = (mine_ref[...].astype(jnp.float32) + other_ref[...].astype(jnp.float32)) * gain_ref[...]
    normed, scale = standardize(x_ref[...].astype(jnp.float32))
    out_ref[...] = standardize_back(normed, scale, grad)
    out_ref[part_of(t, half), :] += da_mine[...].astype(jnp.float32)
    out_ref[part_of(1 - t, half), :] += da_other[...].astype(jnp.float32)


def short_sequences(
    tokens, segments, attn_gain, qkv_weight, out_weight, mlp_gain, inner_weight, outer_weight, cotangent
):
    f = lax.axis_index("fsdp")
    c = lax.axis_index("ctx")
    t = lax.axis_index("tp")
    here = jnp.stack([f, c, t]).astype(jnp.int32)
    row_count, width = tokens.shape[1:]
    half_rows = row_count // 2
    shard = attn_gain.shape[0]
    units = inner_weight.shape[2]
    length = segments.shape[1]
    seg_row = segments[0]
    seg_col, seg_line = seg_row.reshape(length, 1), seg_row.reshape(1, length)
    own_tokens = tokens[0]
    out_cot = cotangent[0]
    f_order = [f ^ r for r in range(4)]
    c_order = [c ^ r for r in range(4)]

    def across(value):
        return hop(value, "fsdp", 2, 4)

    def beside(value):
        return hop(value, "fsdp", 1, 4)

    def over_tp(value):
        return hop(value, "tp", 1, 2)

    def gathered(value, crossed):
        return [value, beside(value), crossed, beside(crossed)]

    gains = jnp.stack([attn_gain, mlp_gain])
    gain_parts = [gains] + [hop(gains, "fsdp", r, 4) for r in (1, 2, 3)]
    gain_all = place([g[None] for g in gain_parts], f_order).reshape(4, 2, shard)
    gain_one = gain_all[:, 0].reshape(1, width).astype(jnp.float32)
    gain_two = gain_all[:, 1].reshape(1, width).astype(jnp.float32)

    head_cols = qkv_weight.shape[2] // 4
    by_ctx = [
        lax.dynamic_slice_in_dim(qkv_weight, p * head_cols, head_cols, 2).reshape(shard, 3 * head_cols)
        for p in c_order
    ]
    qkv_own = by_ctx[0]
    qkv_rest = jnp.concatenate(by_ctx[1:], axis=1)
    out_own = jnp.concatenate(
        [lax.dynamic_slice_in_dim(out_weight, p * head_cols, head_cols, 0).T for p in c_order], axis=1
    )
    gate_own, up_own = inner_weight[:, 0].T, inner_weight[:, 1].T
    outer_own = outer_weight

    qkv_crossed = across(qkv_own)
    qkv_here = gathered(qkv_own, qkv_crossed)
    out_pair = jnp.concatenate([out_own, over_tp(out_own)], axis=1)
    out_pair = after(out_pair, qkv_crossed)
    out_crossed = across(out_pair)
    out_all = gathered(out_pair, out_crossed)
    gate_own = after(gate_own, out_crossed)
    gate_crossed = across(gate_own)
    gate_all = gathered(gate_own, gate_crossed)
    up_own = after(up_own, gate_crossed)
    up_crossed = across(up_own)
    up_all = gathered(up_own, up_crossed)
    outer_own = after(outer_own, up_crossed)
    outer_crossed = across(outer_own)
    outer_all = gathered(outer_own, outer_crossed)
    qkv_rest = after(qkv_rest, outer_crossed)
    rest_crossed = across(qkv_rest)
    rest_all = gathered(qkv_rest, rest_crossed)

    own_half = lax.dynamic_slice_in_dim(own_tokens, t * half_rows, half_rows)
    upward, downward = own_half, own_half
    ups, downs, ups_other, downs_other = [], [], [], []
    for step in (1, 2, 3):
        upward = lax.ppermute(upward, "ctx", [(i, i + 1) for i in range(3)])
        downward = lax.ppermute(downward, "ctx", [(i, i - 1) for i in range(1, 4)])
        pairs_up = [(i * 2 + j, i * 2 + 1 - j) for i in range(step, 4) for j in range(2)]
        pairs_down = [(i * 2 + j, i * 2 + 1 - j) for i in range(0, 4 - step) for j in range(2)]
        ups.append(upward)
        downs.append(downward)
        ups_other.append(lax.ppermute(upward, ("ctx", "tp"), pairs_up))
        downs_other.append(lax.ppermute(downward, ("ctx", "tp"), pairs_down))

    cosine, sine = angle_tables(length, 0, HD)
    sign = jnp.where(jnp.arange(HD) < HD // 2, -1.0, 1.0).astype(jnp.float32)
    cosine = jnp.concatenate([cosine[:, 0]] * 2, axis=1)
    sine = jnp.concatenate([sine[:, 0] * sign] * 2, axis=1)

    results = local_call(
        attention_forward,
        [low_shape(row_count, width)] * 4
        + [low_shape(length, LANES)] * 3
        + [wide_shape(length, LANES)]
        + [low_shape(row_count, LANES)] * 4
        + [wide_shape(8, length)],
        here,
        [own_tokens, *ups, *downs, *ups_other, *downs_other, gain_one, *qkv_here, cosine, sine, seg_col, seg_line],
        scratch=[pltpu.VMEM((length, width), jnp.bfloat16)],
        flops=2 * length * width * 3 * LANES + 8 * length * length * LANES,
        transcendentals=2 * length * length,
    )
    h_parts, (queries, keys, values, raw), low_parts, lse = results[:4], results[4:8], results[8:12], results[12]

    partner_bits = [2 * k + b for b in range(2) for k in range(4)]

    def with_partner(value, bits):
        if bits == 0:
            return value
        return lax.ppermute(value, ("ctx", "tp"), [(i, i ^ bits) for i in range(8)])

    head_parts = [with_partner(low_parts[bits >> 1], bits) for bits in partner_bits]

    middle, second_low, hidden_low, gate_grad, up_grad, part_mine, part_other, gain_two_part = local_call(
        feed_forward,
        [wide_shape(row_count, width), low_shape(row_count, width)]
        + [low_shape(row_count, units)] * 3
        + [low_shape(half_rows, width)] * 2
        + [wide_shape(1, width)],
        here,
        [*head_parts, own_tokens, out_cot, gain_two, *out_all, *gate_all, *up_all, *outer_all],
        scratch=[pltpu.VMEM((row_count, width), jnp.float32)],
        flops=2 * row_count * width * (width + 5 * units),
        transcendentals=2 * row_count * units,
    )

    results = local_call(
        head_gradients,
        [low_shape(half_rows, width)] + [low_shape(half_rows, LANES)] * 8,
        here,
        [part_mine, over_tp(part_other), middle, out_cot, gain_two, *out_all],
        flops=2 * half_rows * width * width,
    )
    attn_low, head_grads = results[0], results[1:]
    head_grad_parts = [with_partner(part, bits) for part, bits in zip(head_grads, partner_bits)]

    projected_grads = local_call(
        attention_backward,
        [low_shape(row_count, 3 * LANES)] * 4,
        here,
        [queries, keys, values, *head_grad_parts, raw, lse, cosine, sine, seg_col, seg_line],
        scratch=[pltpu.VMEM((LANES, length), jnp.float32), pltpu.VMEM((length, LANES), jnp.bfloat16)],
        flops=20 * length * length * LANES,
        transcendentals=2 * length * length,
    )

    (mlp_part,) = local_call(
        feed_forward_out,
        [low_shape(row_count, width)],
        here,
        [hidden_low, *outer_all],
        flops=2 * row_count * width * units,
    )
    block_out = (
        middle + (mlp_part.astype(jnp.float32) + over_tp(mlp_part).astype(jnp.float32))
    ).astype(jnp.bfloat16)

    def over_fsdp(pieces):
        first = pieces[0] + beside(pieces[1])
        second = pieces[2] + beside(pieces[3])
        return first + across(second)

    at_end = jnp.logical_or(c == 0, c == 3)

    def over_line(value):
        value = value + lax.ppermute(value, "ctx", [(0, 1), (3, 2)])
        value = value + lax.ppermute(value, "ctx", [(1, 2), (2, 1)])
        value = lax.optimization_barrier(value)
        return jnp.where(at_end, lax.ppermute(value, "ctx", [(1, 0), (2, 3)]), value)

    def weight_grad(lefts, rights):
        rows = lefts[0].shape[1]
        return local_call(
            functools.partial(weight_gradients, len(lefts)),
            [low_shape(rows, shard)] * 4,
            here,
            [*lefts, *rights],
            flops=2 * sum(left.shape[0] for left in lefts) * width * rows,
        )

    outer_sum = over_line(over_fsdp(weight_grad([hidden_low], [out_cot])))
    gate_sum = over_line(over_fsdp(weight_grad([gate_grad], [second_low])))
    up_sum = over_line(over_fsdp(weight_grad([up_grad], [second_low])))
    attn_other = over_tp(attn_low)
    out_pieces = local_call(
        out_gradients,
        [low_shape(4 * LANES, shard)] * 4,
        here,
        [attn_low, attn_other, *head_parts[:4]],
        scratch=[
            pltpu.VMEM((row_count, width), jnp.bfloat16),
            pltpu.VMEM((row_count, 4 * LANES), jnp.bfloat16),
        ],
        flops=2 * row_count * width * 4 * LANES,
    )
    out_sum = over_line(over_fsdp(out_pieces))
    out_grad = out_sum.astype(jnp.float32)

    qkv_sum = over_fsdp(weight_grad(projected_grads, h_parts))
    qkv_sum = lax.optimization_barrier(qkv_sum)
    qkv_parts = [qkv_sum] + [hop(qkv_sum, "ctx", r, 4) for r in (1, 2, 3)]
    qkv_grad = place([p[None] for p in qkv_parts], c_order).reshape(4, 3, head_cols, shard)
    qkv_grad = qkv_grad.transpose(3, 1, 0, 2).reshape(shard, 3, 4 * head_cols).astype(jnp.float32)

    first_parts = [projected_grads[0]] + [hop(projected_grads[r], "ctx", r, 4) for r in (1, 2, 3)]
    first_low_part, gain_one_part = local_call(
        first_gradients,
        [low_shape(row_count, width), wide_shape(1, width)],
        here,
        [*first_parts, own_tokens, *qkv_here, *rest_all],
        scratch=[pltpu.VMEM((row_count, width), jnp.float32)],
        flops=2 * row_count * width * 12 * LANES,
    )
    (input_grad,) = local_call(
        input_gradients,
        [wide_shape(row_count, width)],
        here,
        [first_low_part, over_tp(first_low_part), own_tokens, gain_one, attn_low, attn_other],
    )

    gain_parts = jnp.concatenate([gain_one_part, gain_two_part], axis=0)
    gain_parts = gain_parts + over_tp(gain_parts)
    gain_pieces = gain_parts.reshape(2, 4, shard).transpose(1, 0, 2)
    summed = [lax.dynamic_index_in_dim(gain_pieces, p, 0, keepdims=False) for p in f_order]
    summed = summed[:1] + [hop(summed[r], "fsdp", r, 4) for r in (1, 2, 3)]
    summed = lax.optimization_barrier((summed[0] + summed[1]) + (summed[2] + summed[3]))
    summed = [summed] + [hop(summed, "ctx", r, 4) for r in (1, 2, 3)]
    summed = (summed[0] + summed[1]) + (summed[2] + summed[3])

    return (
        block_out[None],
        input_grad[None],
        summed[0],
        qkv_grad,
        out_grad,
        summed[1],
        jnp.stack([gate_sum.T, up_sum.T], axis=1).astype(jnp.float32),
        outer_sum.astype(jnp.float32),
    )


def solution(mesh):
    placed = (
        P("fsdp", "ctx", None),
        P("fsdp", None),
        P("fsdp"),
        P("fsdp", None, "tp"),
        P("tp", "fsdp"),
        P("fsdp"),
        P("fsdp", None, "tp"),
        P("tp", "fsdp"),
        P("fsdp", "ctx", None),
    )
    sizes = dict(mesh.shape)

    def layer(*args):
        tokens, segments, qkv_weight = args[0], args[1], args[3]
        heads_apart = qkv_weight.shape[2] == 4 * LANES
        short = segments.shape[1] == 4 * tokens.shape[1] and segments.shape[1] <= 1024
        small = (sizes["fsdp"], sizes["ctx"], sizes["tp"]) == (4, 4, 2)
        if small and short and heads_apart and tokens.shape[0] == 1:
            return short_sequences(*args)
        return per_device(*args)

    return jax.shard_map(
        layer,
        mesh=mesh,
        in_specs=placed,
        out_specs=(
            P("fsdp", "ctx", None),
            P("fsdp", "ctx", None),
            P("fsdp"),
            P("fsdp", None, "tp"),
            P("tp", "fsdp"),
            P("fsdp"),
            P("fsdp", None, "tp"),
            P("tp", "fsdp"),
        ),
        check_vma=False,
    )
```

```python
import functools
import math

import jax
import jax.numpy as jnp
from jax import lax
from jax.experimental import pallas as pl
from jax.experimental.pallas import tpu as pltpu
from jax.sharding import PartitionSpec as P

HD = 64


EPSILON = 1e-05
ROPE_BASE = 160000.0
MASKED = -1e30


def normalize(values, gain_row):
    row_mean = jnp.mean(values, axis=-1, keepdims=True)
    centered = values - row_mean
    spread = jnp.mean(centered * centered, axis=-1, keepdims=True)
    return centered * lax.rsqrt(spread + EPSILON) * gain_row


def geglu(gate_in, upper):
    return jax.nn.gelu(gate_in, approximate=False) * upper


def angle_tables(row_count, offset, depth):
    half_width = depth // 2
    inverse = jnp.power(
        jnp.float32(ROPE_BASE), -(2.0 * jnp.arange(half_width, dtype=jnp.float32)) / depth
    )
    places = (offset + jnp.arange(row_count, dtype=jnp.int32)).astype(jnp.float32)
    angles = places[:, None] * inverse[None, :]
    angles = jnp.concatenate([angles, angles], axis=-1)
    return (jnp.cos(angles)[:, None, :], jnp.sin(angles)[:, None, :])


def rotate(values, cosine, sine):
    half_width = values.shape[-1] // 2
    turned = jnp.concatenate([-values[..., half_width:], values[..., :half_width]], axis=-1)
    return values * cosine + turned * sine


def rotate_back(grad_in, cosine, sine):
    half_width = grad_in.shape[-1] // 2
    scaled = grad_in * sine
    turned = jnp.concatenate([scaled[..., half_width:], -scaled[..., :half_width]], axis=-1)
    return grad_in * cosine + turned


def attend_forward(queries, query_seg, seg_row, key_low, value_low, score_scale):
    row_count, heads_here, depth = queries.shape
    initial = (
        jnp.full((heads_here, row_count), MASKED, jnp.float32),
        jnp.zeros((heads_here, row_count), jnp.float32),
        jnp.zeros((row_count, heads_here, depth), jnp.float32),
    )
    key_piece = lax.all_gather(key_low, "ctx", axis=0, tiled=True)
    value_piece = lax.all_gather(value_low, "ctx", axis=0, tiled=True)
    piece_rows = key_piece.shape[0]
    block_size = math.gcd(piece_rows, 512)
    blocks = (
        key_piece.reshape(piece_rows // block_size, block_size, heads_here, depth),
        value_piece.reshape(piece_rows // block_size, block_size, heads_here, depth),
        seg_row.reshape(piece_rows // block_size, block_size),
    )

    def step(state, block_data):
        running_peak, running_total, accum = state
        key_block, value_block, block_seg = block_data
        scores = jnp.einsum("qhe,khe->hqk", queries, key_block, preferred_element_type=jnp.float32)
        same_doc = (query_seg[:, None] == block_seg[None, :])[None]
        logits = jnp.where(same_doc, scores * score_scale, MASKED)
        new_peak = jnp.maximum(running_peak, jnp.max(logits, axis=-1))
        rescale = jnp.exp(running_peak - new_peak)
        weights = jnp.where(same_doc, jnp.exp(logits - new_peak[:, :, None]), 0.0)
        running_total = running_total * rescale + jnp.sum(weights, axis=-1)
        mixed_out = jnp.einsum(
            "hqk,khe->qhe",
            weights.astype(jnp.bfloat16),
            value_block,
            preferred_element_type=jnp.float32,
        )
        accum = accum * rescale.T[:, :, None] + mixed_out
        return ((new_peak, running_total, accum), None)

    result, unused = lax.scan(step, initial, blocks)
    running_peak, running_total, accum = result
    return (accum / running_total.T[:, :, None], running_peak + jnp.log(running_total))


def probs_and_grads(
    query_block, key_block, grad_block, value_block, same_doc, log_total, delta_rows, score_scale
):
    scores = jnp.einsum("qhe,khe->hqk", query_block, key_block, preferred_element_type=jnp.float32)
    probs = jnp.where(same_doc, jnp.exp(scores * score_scale - log_total[:, :, None]), 0.0)
    prob_grad = jnp.einsum(
        "qhe,khe->hqk", grad_block, value_block, preferred_element_type=jnp.float32
    )
    score_grad = (probs * (prob_grad - delta_rows[:, :, None]) * score_scale).astype(jnp.bfloat16)
    return (probs.astype(jnp.bfloat16), score_grad)


def attend_backward(
    queries, key_low, value_low, grad_low, log_total, delta_rows, query_seg, seg_row, score_scale
):
    row_count, heads_here, depth = queries.shape
    seq_length = seg_row.shape[0]
    block_size = math.gcd(seq_length, 512)
    block_count = seq_length // block_size
    key_all, value_all = (
        lax.all_gather(key_low, "ctx", axis=0, tiled=True),
        lax.all_gather(value_low, "ctx", axis=0, tiled=True),
    )
    blocks = (
        key_all.reshape(block_count, block_size, heads_here, depth),
        value_all.reshape(block_count, block_size, heads_here, depth),
        seg_row.reshape(block_count, block_size),
    )

    def key_step(query_acc, block_data):
        key_block, value_block, block_seg = block_data
        same_doc = (query_seg[:, None] == block_seg[None, :])[None]
        prob_low, score_grad = probs_and_grads(
            queries, key_block, grad_low, value_block, same_doc, log_total, delta_rows, score_scale
        )
        query_acc = query_acc + jnp.einsum(
            "hqk,khe->qhe", score_grad, key_block, preferred_element_type=jnp.float32
        )
        key_part = jnp.einsum(
            "hqk,qhe->khe", score_grad, queries, preferred_element_type=jnp.float32
        )
        value_part = jnp.einsum(
            "hqk,qhe->khe", prob_low, grad_low, preferred_element_type=jnp.float32
        )
        return (query_acc, (key_part, value_part))

    query_grad, key_value_parts = lax.scan(
        key_step, jnp.zeros((row_count, heads_here, depth), jnp.float32), blocks
    )
    key_parts = key_value_parts[0].reshape(seq_length, heads_here * depth)
    value_parts = key_value_parts[1].reshape(seq_length, heads_here * depth)
    key_grad, value_grad = (
        lax.psum_scatter(
            key_parts.astype(jnp.bfloat16), "ctx", scatter_dimension=0, tiled=True
        ).astype(jnp.float32),
        lax.psum_scatter(
            value_parts.astype(jnp.bfloat16), "ctx", scatter_dimension=0, tiled=True
        ).astype(jnp.float32),
    )
    key_grad = key_grad.reshape(row_count, heads_here, depth)
    value_grad = value_grad.reshape(row_count, heads_here, depth)
    return (query_grad, key_grad, value_grad)


def per_device(
    tokens,
    segments,
    attn_gain,
    qkv_weight,
    out_weight,
    mlp_gain,
    inner_weight,
    outer_weight,
    cotangent,
):
    qkv_full, out_full, gain_one = (
        lax.all_gather(qkv_weight, "fsdp", axis=0, tiled=True),
        lax.all_gather(out_weight, "fsdp", axis=1, tiled=True),
        lax.all_gather(attn_gain, "fsdp", axis=0, tiled=True),
    )
    inner_full, outer_full, gain_two = (
        lax.all_gather(inner_weight, "fsdp", axis=0, tiled=True),
        lax.all_gather(outer_weight, "fsdp", axis=1, tiled=True),
        lax.all_gather(mlp_gain, "fsdp", axis=0, tiled=True),
    )
    seq_count, row_count, model_width = tokens.shape
    local_width = qkv_full.shape[2]
    heads_here = local_width // HD
    score_scale = HD ** (-0.5)
    offset = lax.axis_index("ctx") * row_count
    cosine, sine = angle_tables(row_count, offset, HD)
    input_rows = tokens.reshape(-1, model_width).astype(jnp.float32)
    normed_one, norm_one_back = jax.vjp(normalize, input_rows, gain_one.astype(jnp.float32))
    first_low = normed_one.astype(jnp.bfloat16)
    projected_output = jnp.einsum(
        "td,dcf->tcf", first_low, qkv_full, preferred_element_type=jnp.float32
    )
    projected_output = projected_output.reshape(seq_count, row_count, 3, heads_here, HD)
    query_low = rotate(projected_output[:, :, 0], cosine, sine).astype(jnp.bfloat16)
    key_low = rotate(projected_output[:, :, 1], cosine, sine).astype(jnp.bfloat16)
    value_low = projected_output[:, :, 2].astype(jnp.bfloat16)
    seq_index = 0
    seg_row = segments[seq_index]
    query_seg = lax.dynamic_slice_in_dim(seg_row, offset, row_count)
    raw_out, log_total = attend_forward(
        query_low[seq_index],
        query_seg,
        seg_row,
        key_low[seq_index],
        value_low[seq_index],
        score_scale,
    )
    query_segs = [query_seg]
    raw_outs = [raw_out]
    log_totals = [log_total]
    attended_low = jnp.stack(raw_outs).astype(jnp.bfloat16).reshape(-1, local_width)
    attn_part = jnp.dot(attended_low, out_full, preferred_element_type=jnp.float32)
    middle_activation = input_rows + lax.psum(attn_part.astype(jnp.bfloat16), "tp").astype(
        jnp.float32
    )
    normed_two, norm_two_back = jax.vjp(normalize, middle_activation, gain_two.astype(jnp.float32))
    second_low = normed_two.astype(jnp.bfloat16)
    hidden_input = jnp.einsum(
        "td,dcf->tcf", second_low, inner_full, preferred_element_type=jnp.float32
    )
    hidden_state, geglu_back = jax.vjp(geglu, hidden_input[:, 0], hidden_input[:, 1])
    hidden_low = hidden_state.astype(jnp.bfloat16)
    mlp_part = jnp.dot(hidden_low, outer_full, preferred_element_type=jnp.float32)
    block_out = (
        middle_activation + lax.psum(mlp_part.astype(jnp.bfloat16), "tp").astype(jnp.float32)
    ).astype(jnp.bfloat16)
    out_cot = cotangent.reshape(-1, model_width)
    outer_local = jnp.einsum("tf,td->fd", hidden_low, out_cot, preferred_element_type=jnp.float32)
    hidden_grad = jnp.einsum("td,fd->tf", out_cot, outer_full, preferred_element_type=jnp.float32)
    gate_grad, up_grad = geglu_back(hidden_grad)
    inner_low = jnp.stack([gate_grad, up_grad], axis=1).astype(jnp.bfloat16)
    inner_local = jnp.einsum(
        "td,tcf->dcf", second_low, inner_low, preferred_element_type=jnp.float32
    )
    normed_two_grad = lax.psum(
        jnp.einsum("tcf,dcf->td", inner_low, inner_full, preferred_element_type=jnp.float32).astype(
            jnp.bfloat16
        ),
        "tp",
    ).astype(jnp.float32)
    middle_part, gain_two_grad = norm_two_back(normed_two_grad)
    middle_grad = out_cot.astype(jnp.float32) + middle_part
    attn_low = middle_grad.astype(jnp.bfloat16)
    out_local = jnp.einsum("tf,td->fd", attended_low, attn_low, preferred_element_type=jnp.float32)
    attended_grad = jnp.einsum("td,fd->tf", attn_low, out_full, preferred_element_type=jnp.float32)
    attended_grad = attended_grad.astype(jnp.bfloat16).reshape(seq_count, row_count, heads_here, HD)
    seq_index = 0
    grad_low = attended_grad[seq_index]
    delta_rows = jnp.sum(grad_low.astype(jnp.float32) * raw_outs[seq_index], axis=-1).T
    query_grad, key_grad, value_grad = attend_backward(
        query_low[seq_index],
        key_low[seq_index],
        value_low[seq_index],
        grad_low,
        log_totals[seq_index],
        delta_rows,
        query_segs[seq_index],
        segments[seq_index],
        score_scale,
    )
    stacked = jnp.stack(
        [rotate_back(query_grad, cosine, sine), rotate_back(key_grad, cosine, sine), value_grad],
        axis=1,
    )
    qkv_grads = stacked.reshape(row_count, 3, local_width)
    qkv_low = qkv_grads.astype(jnp.bfloat16)
    qkv_local = jnp.einsum("td,tcf->dcf", first_low, qkv_low, preferred_element_type=jnp.float32)
    normed_one_grad = lax.psum(
        jnp.einsum("tcf,dcf->td", qkv_low, qkv_full, preferred_element_type=jnp.float32).astype(
            jnp.bfloat16
        ),
        "tp",
    ).astype(jnp.float32)
    input_part, gain_one_grad = norm_one_back(normed_one_grad)
    input_grad = (middle_grad + input_part).reshape(tokens.shape)
    summed = (
        lax.psum_scatter(gain_one_grad, ("fsdp", "ctx"), scatter_dimension=0, tiled=True),
        lax.psum_scatter(qkv_local, ("fsdp", "ctx"), scatter_dimension=0, tiled=True),
        lax.psum_scatter(out_local, ("fsdp", "ctx"), scatter_dimension=1, tiled=True),
        lax.psum_scatter(gain_two_grad, ("fsdp", "ctx"), scatter_dimension=0, tiled=True),
        lax.psum_scatter(inner_local, ("fsdp", "ctx"), scatter_dimension=0, tiled=True),
        lax.psum_scatter(outer_local, ("fsdp", "ctx"), scatter_dimension=1, tiled=True),
    )
    gain_one_sum, qkv_sum, out_sum, gain_two_sum, inner_sum, outer_sum = summed
    shards = (
        lax.all_gather(gain_one_sum.astype(jnp.bfloat16), "ctx", axis=0, tiled=True).astype(
            gain_one_sum.dtype
        ),
        lax.all_gather(qkv_sum.astype(jnp.bfloat16), "ctx", axis=0, tiled=True).astype(
            qkv_sum.dtype
        ),
        lax.all_gather(out_sum.astype(jnp.bfloat16), "ctx", axis=1, tiled=True).astype(
            out_sum.dtype
        ),
        lax.all_gather(gain_two_sum.astype(jnp.bfloat16), "ctx", axis=0, tiled=True).astype(
            gain_two_sum.dtype
        ),
        lax.all_gather(inner_sum.astype(jnp.bfloat16), "ctx", axis=0, tiled=True).astype(
            inner_sum.dtype
        ),
        lax.all_gather(outer_sum.astype(jnp.bfloat16), "ctx", axis=1, tiled=True).astype(
            outer_sum.dtype
        ),
    )
    return (
        block_out.reshape(tokens.shape),
        input_grad,
        shards[0],
        shards[1],
        shards[2],
        shards[3],
        shards[4],
        shards[5],
    )


LANES = 128
BLOCK = 256
EXTRA = 32
COST = 0.0
WIDE_VMEM = 62 * 1024 * 1024


def hop(value, axis, bit, count):
    return lax.ppermute(value, axis, [(i, i ^ bit) for i in range(count)])


def after(values, *earlier):
    values = list(values)
    return list(lax.optimization_barrier(tuple(values) + earlier))[: len(values)]


def lane_half(shape):
    return lax.broadcasted_iota(jnp.int32, shape, 1) < HD


def swap_halves(values):
    lane = lax.broadcasted_iota(jnp.int32, values.shape, 1)
    low_part = lax.rem(lane, HD) < HD // 2
    return jnp.where(
        low_part,
        pltpu.roll(values, LANES - HD // 2, 1),
        pltpu.roll(values, HD // 2, 1),
    )


def dot_nt(left, right):
    return lax.dot_general(left, right, (((1,), (1,)), ((), ())), preferred_element_type=jnp.float32)


def dot_nn(left, right):
    return lax.dot_general(left, right, (((1,), (0,)), ((), ())), preferred_element_type=jnp.float32)


def dot_tn(left, right):
    return lax.dot_general(left, right, (((0,), (0,)), ((), ())), preferred_element_type=jnp.float32)


def one_head(values, head):
    first = lane_half(values.shape)
    keep = first if head == 0 else jnp.logical_not(first)
    return jnp.where(keep, values, jnp.zeros_like(values))


def part_of(index, size):
    return pl.ds(pl.multiple_of(index * size, size), size)


def standardize(values):
    row_mean = jnp.mean(values, axis=-1, keepdims=True)
    centered = values - row_mean
    spread = jnp.mean(centered * centered, axis=-1, keepdims=True)
    scale = lax.rsqrt(spread + EPSILON)
    return centered * scale, scale


def standardize_back(normed, scale, grad):
    inner = jnp.mean(grad * normed, axis=-1, keepdims=True)
    return scale * (grad - jnp.mean(grad, axis=-1, keepdims=True) - normed * inner)


def local_call(body, outs, places, operands, scratch=(), flops=0, transcendentals=0):
    moved = sum(math.prod(o.shape) * o.dtype.itemsize for o in list(operands) + list(outs))
    return pl.pallas_call(
        body,
        name=body.__name__ if hasattr(body, "__name__") else body.func.__name__,
        out_shape=tuple(outs),
        in_specs=[pl.BlockSpec(memory_space=pltpu.SMEM)]
        + [pl.BlockSpec(memory_space=pltpu.VMEM)] * len(operands),
        out_specs=tuple([pl.BlockSpec(memory_space=pltpu.VMEM)] * len(outs)),
        scratch_shapes=list(scratch),
        compiler_params=pltpu.CompilerParams(vmem_limit_bytes=WIDE_VMEM),
        cost_estimate=pl.CostEstimate(
            flops=int(flops * COST), bytes_accessed=int(moved * COST), transcendentals=int(transcendentals * COST)
        ),
    )(places, *operands)


def low_shape(*shape):
    return jax.ShapeDtypeStruct(shape, jnp.bfloat16)


def wide_shape(*shape):
    return jax.ShapeDtypeStruct(shape, jnp.float32)


def project_block(block, at, *refs):
    f, t = at[0], at[2]
    count = len(refs) - 12
    tokens_in, (w0, w1, w2, w3, cos_ref, sin_ref) = refs[:count], refs[count : count + 6]
    h_ref, q_ref, k_ref, v_ref, gain_ref, x_ref = refs[count + 6 :]
    weights = (w0, w1, w2, w3)
    columns = [part_of(f ^ r, w0.shape[1]) for r in range(4)]
    heads = 3 * LANES
    for r, weight in enumerate(weights):
        gain_ref[:, columns[r]] = weight[heads : heads + EXTRA, :].astype(jnp.float32)[:8, :]
    if count == 1:
        tokens = tokens_in[0][...]
    else:
        half = tokens_in[0].shape[0]
        x_ref[part_of(t, half), :] = tokens_in[0][...]
        x_ref[part_of(1 - t, half), :] = tokens_in[1][...]
        tokens = x_ref[...]
    h_ref[...] = (standardize(tokens.astype(jnp.float32))[0] * gain_ref[0:1, :]).astype(jnp.bfloat16)
    projected = 0.0
    for r, weight in enumerate(weights):
        projected += dot_nt(h_ref[:, columns[r]], weight[:heads, :])
    rows = slice(block * tokens.shape[0], (block + 1) * tokens.shape[0])
    cosine, sine = cos_ref[rows, :], sin_ref[rows, :]
    for ref, part in ((q_ref, projected[:, :LANES]), (k_ref, projected[:, LANES : 2 * LANES])):
        ref[...] = (part * cosine + swap_halves(part) * sine).astype(jnp.bfloat16)
    v_ref[...] = projected[:, 2 * LANES :].astype(jnp.bfloat16)


def joined(refs):
    return jnp.concatenate([ref[...] for ref in refs], axis=0)


def attention_forward(at, *refs):
    c = at[1]
    query_refs, key_refs, value_refs, seg_col, seg_line = refs[:4], refs[4:8], refs[8:12], refs[12], refs[13]
    raw_ref, low_ref, lse_ref = refs[14:]
    rows_here = query_refs[0].shape[0]
    keys, values = joined(key_refs), joined(value_refs)
    for k in range(4):
        rows = slice(k * rows_here, (k + 1) * rows_here)
        queries = query_refs[k][...] * jnp.bfloat16(HD ** (-0.5))
        same = seg_col[rows, :] == seg_line[...]
        outs, logs = [], []
        for head in range(2):
            scores = dot_nt(one_head(queries, head), keys)
            scores = jnp.where(same, scores, MASKED)
            peak = jnp.max(scores, axis=1, keepdims=True)
            weights = jnp.exp(scores - peak)
            total = jnp.sum(weights, axis=1, keepdims=True)
            probs = (weights * (1.0 / total)).astype(jnp.bfloat16)
            outs.append(dot_nn(probs, values))
            logs.append(peak + jnp.log(total))
        raw = jnp.where(lane_half(outs[0].shape), outs[0], outs[1])
        raw_ref[rows, :] = raw
        low_ref[part_of(c ^ k, rows_here), :] = raw.astype(jnp.bfloat16)
        lane = lax.broadcasted_iota(jnp.int32, (rows_here, LANES), 1)
        lse_ref[:, rows] = jnp.where(lane == 0, logs[0], logs[1]).T[:8, :]


def attention_backward(
    at, q0, q1, q2, q3, k0, k1, k2, k3, v0, v1, v2, v3, do_ref, raw_ref, lse_ref, cos_ref, sin_ref,
    seg_col, seg_line, o0, o1, o2, o3, turned_ref,
):
    c = at[1]
    outs = (o0, o1, o2, o3)
    rows_here = o0.shape[0]
    grads = jnp.concatenate([do_ref[part_of(c ^ k, rows_here), :] for k in range(4)], axis=0)
    product = grads.astype(jnp.float32) * raw_ref[...]
    first = lane_half(product.shape)
    whole = jnp.sum(jnp.where(first, product, 0.0), axis=1, keepdims=True)
    other = jnp.sum(jnp.where(first, 0.0, product), axis=1, keepdims=True)
    lane = lax.broadcasted_iota(jnp.int32, product.shape, 1)
    delta = jnp.where(lane == 0, whole, other).T
    scale = HD ** (-0.5)
    queries = joined((q0, q1, q2, q3))
    scaled = queries * jnp.bfloat16(scale)
    for k, out_ref in enumerate(outs):
        rows = slice(k * rows_here, (k + 1) * rows_here)
        keys, values = (k0, k1, k2, k3)[k][...], (v0, v1, v2, v3)[k][...]
        keys_turned = keys.T
        same = seg_col[rows, :] == seg_line[...]
        key_parts, value_parts = [], []
        for head in range(2):
            scores = dot_nt(one_head(keys, head), scaled)
            probs = jnp.where(same, jnp.exp(scores - lse_ref[head : head + 1, :]), 0.0)
            prob_grad = dot_nt(one_head(values, head), grads)
            score_grad = (probs * (prob_grad - delta[head : head + 1, :]) * scale).astype(jnp.bfloat16)
            value_parts.append(dot_nn(probs.astype(jnp.bfloat16), grads))
            key_parts.append(dot_nn(score_grad, queries))
            here = slice(head * HD, (head + 1) * HD)
            part = dot_nn(keys_turned[here, :], score_grad)
            if k == 0:
                turned_ref[here, :] = part
            else:
                turned_ref[here, :] += part
        half = lane_half(key_parts[0].shape)
        key_grad = jnp.where(half, key_parts[0], key_parts[1])
        value_grad = jnp.where(half, value_parts[0], value_parts[1])
        key_grad = key_grad * cos_ref[rows, :] - swap_halves(key_grad) * sin_ref[rows, :]
        out_ref[:, LANES : 2 * LANES] = key_grad.astype(jnp.bfloat16)
        out_ref[:, 2 * LANES :] = value_grad.astype(jnp.bfloat16)
    for k, out_ref in enumerate(outs):
        rows = slice(k * rows_here, (k + 1) * rows_here)
        query_grad = turned_ref[:, rows].T
        query_grad = query_grad * cos_ref[rows, :] - swap_halves(query_grad) * sin_ref[rows, :]
        out_ref[:, :LANES] = query_grad.astype(jnp.bfloat16)


def feed_forward(
    at, own_ref, other_ref, x_ref, cot_ref, gain_ref,
    o0, o1, o2, o3, inner0, inner1, inner2, inner3, outer0, outer1, outer2, outer3,
    mid_ref, second_ref, hid_ref, dgate_ref, dup_ref, low_ref, gain_grad_ref,
    part_ref,
):
    f = at[0]
    rows_here = x_ref.shape[0]
    attended = jnp.concatenate(
        [ref[k * rows_here : (k + 1) * rows_here, :] for ref in (own_ref, other_ref) for k in range(4)],
        axis=1,
    )
    inners, outers = (inner0, inner1, inner2, inner3), (outer0, outer1, outer2, outer3)
    columns = [part_of(f ^ r, o0.shape[1]) for r in range(4)]
    for r, weight in enumerate((o0, o1, o2, o3)):
        mid_ref[:, columns[r]] = x_ref[:, columns[r]].astype(jnp.float32) + dot_nn(attended, weight[...])
    normed = standardize(mid_ref[...])[0]
    second_ref[...] = (normed * gain_ref[1:2, :]).astype(jnp.bfloat16)
    units = outer0.shape[0]
    for start in range(0, units, BLOCK):
        stop = min(start + BLOCK, units)
        gate, up, hid_grad = 0.0, 0.0, 0.0
        for r in range(4):
            rows = second_ref[:, columns[r]]
            gate += dot_nt(rows, inners[r][start:stop, :])
            up += dot_nt(rows, inners[r][units + start : units + stop, :])
            hid_grad += dot_nt(cot_ref[:, columns[r]], outers[r][start:stop, :])
        below = 0.5 + 0.5 * lax.erf(gate * (2.0 ** -0.5))
        density = jnp.exp(-0.5 * gate * gate) * ((2.0 * math.pi) ** -0.5)
        active = gate * below
        hid_ref[:, start:stop] = (active * up).astype(jnp.bfloat16)
        dgate_ref[:, start:stop] = (hid_grad * up * (below + gate * density)).astype(jnp.bfloat16)
        dup_ref[:, start:stop] = (hid_grad * active).astype(jnp.bfloat16)
    for r in range(4):
        part_ref[:, columns[r]] = dot_nn(dgate_ref[...], inners[r][:units, :]) + dot_nn(
            dup_ref[...], inners[r][units:, :]
        )
    low_ref[...] = part_ref[...].astype(jnp.bfloat16)
    gain_grad_ref[...] = jnp.sum(part_ref[...] * normed, axis=0, keepdims=True)


def feed_forward_out(at, hid_ref, outer0, outer1, outer2, outer3, out_ref):
    f = at[0]
    for r, weight in enumerate((outer0, outer1, outer2, outer3)):
        out_ref[:, part_of(f ^ r, weight.shape[1])] = dot_nn(hid_ref[...], weight[...]).astype(jnp.bfloat16)


def head_gradients(
    at, mine_ref, other_ref, mid_ref, cot_ref, gain_ref, o0, o1, o2, o3, da_ref, out_ref
):
    f = at[0]
    grad = (mine_ref[...].astype(jnp.float32) + other_ref[...].astype(jnp.float32)) * gain_ref[1:2, :]
    normed, scale = standardize(mid_ref[...])
    mid_grad = cot_ref[...].astype(jnp.float32) + standardize_back(normed, scale, grad)
    da_ref[...] = mid_grad.astype(jnp.bfloat16)
    total = 0.0
    for r, weight in enumerate((o0, o1, o2, o3)):
        total += dot_nt(da_ref[:, part_of(f ^ r, weight.shape[1])], weight[: 4 * LANES, :])
    rows_here = da_ref.shape[0]
    for k in range(4):
        out_ref[k * rows_here : (k + 1) * rows_here, :] = total[
            :, k * LANES : (k + 1) * LANES
        ].astype(jnp.bfloat16)


def store_piece(r, value, send_ref, keep_ref, keep_across_ref, rows=slice(None)):
    if r in (1, 3):
        send_ref[r // 2, rows, :] = value
    else:
        (keep_ref if r == 0 else keep_across_ref)[rows, :] = value


def extra_rows(row):
    lines = lax.broadcasted_iota(jnp.int32, (EXTRA, row.shape[1]), 0)
    return jnp.where(lines == 0, row, 0.0).astype(jnp.bfloat16)


def add_core_piece(keep_ref, received_ref, out_ref):
    out_ref[...] = keep_ref[...] + received_ref[0]


def add_chip_piece(keep_ref, received_ref, crossed_ref, out_ref):
    total = keep_ref[...].astype(jnp.float32) + received_ref[0].astype(jnp.float32)
    out_ref[...] = (total + crossed_ref[...].astype(jnp.float32)).astype(jnp.bfloat16)


def add_line_piece(mine_ref, arrived_ref, out_ref):
    out_ref[...] = mine_ref[...] + arrived_ref[...]


def add_rows(body, at_received, *operands):
    rows, columns = operands[0].shape
    block = rows // 2
    specs = [
        pl.BlockSpec((1, block, columns), lambda i: (at_received, i, 0))
        if operand.ndim == 3
        else pl.BlockSpec((block, columns), lambda i: (i, 0))
        for operand in operands
    ]
    return pl.pallas_call(
        body,
        name=body.__name__,
        grid=(2,),
        in_specs=specs,
        out_specs=pl.BlockSpec((block, columns), lambda i: (i, 0)),
        out_shape=low_shape(rows, columns),
        compiler_params=pltpu.CompilerParams(vmem_limit_bytes=WIDE_VMEM),
        cost_estimate=pl.CostEstimate(flops=0, bytes_accessed=0, transcendentals=0),
    )(*operands)


def weight_gradients(at, left_ref, right_ref, *outs):
    f = at[0]
    shard = outs[-1].shape[1]
    for r in (1, 3, 2, 0):
        value = dot_tn(left_ref[...], right_ref[:, part_of(f ^ r, shard)])
        store_piece(r, value.astype(jnp.bfloat16), *outs)


def up_and_out_gradients(at, left_ref, right_ref, gain_grad_ref, da_ref, attended_ref, *outs):
    f = at[0]
    rows, shard = left_ref.shape[1], outs[-1].shape[1]
    rows_here = da_ref.shape[0]
    attended = jnp.concatenate(
        [attended_ref[k * rows_here : (k + 1) * rows_here, :] for k in range(4)], axis=1
    )
    for r in (1, 3, 2, 0):
        columns = part_of(f ^ r, shard)
        value = dot_tn(left_ref[...], right_ref[:, columns])
        store_piece(r, value.astype(jnp.bfloat16), *outs, rows=slice(0, rows))
        store_piece(r, extra_rows(gain_grad_ref[:, columns]), *outs, rows=slice(rows, rows + EXTRA))
        value = dot_tn(attended, da_ref[:, columns])
        store_piece(r, value.astype(jnp.bfloat16), *outs, rows=slice(rows + EXTRA, None))


def qkv_gradients(
    at, g0, g1, g2, g3, h0, h1, h2, h3, w0, w1, w2, w3, gain_ref, *outs
):
    f = at[0]
    rows, shard = g0.shape[1], w0.shape[1]
    for r in (1, 3, 2, 0):
        columns = part_of(f ^ r, shard)
        value = 0.0
        for grad, left in zip((g0, g1, g2, g3), (h0, h1, h2, h3)):
            value += dot_tn(grad[...], left[:, columns])
        store_piece(r, value.astype(jnp.bfloat16), *outs, rows=slice(0, rows))
        weight = (w0, w1, w2, w3)[r][:rows, :].astype(jnp.float32)
        gain_grad = jnp.sum(weight * value, axis=0, keepdims=True) / gain_ref[0:1, columns]
        store_piece(r, extra_rows(gain_grad), *outs, rows=slice(rows, rows + EXTRA))


def first_gradients(at, g0, g1, g2, g3, q0, q1, q2, q3, rest0, rest1, rest2, rest3, low_ref):
    f = at[0]
    others = jnp.concatenate([g1[...], g2[...], g3[...]], axis=1)
    heads = 3 * LANES
    for r in range(4):
        own, rest = (q0, q1, q2, q3)[r], (rest0, rest1, rest2, rest3)[r]
        part = dot_nn(g0[...], own[:heads, :]) + dot_nn(others, rest[...])
        low_ref[:, part_of(f ^ r, own.shape[1])] = part.astype(jnp.bfloat16)


def input_gradients(at, mine_ref, other_ref, x_ref, gain_ref, da_ref, out_ref):
    grad = (mine_ref[...].astype(jnp.float32) + other_ref[...].astype(jnp.float32)) * gain_ref[0:1, :]
    normed, scale = standardize(x_ref[...].astype(jnp.float32))
    out_ref[...] = da_ref[...].astype(jnp.float32) + standardize_back(normed, scale, grad)


def qkv_layout(at, p0, p1, p2, p3, out_ref):
    c = at[1]
    for k, part in enumerate((p0, p1, p2, p3)):
        for j in range(3):
            place = part_of(j * 4 + (c ^ k), LANES)
            out_ref[:, place] = part[j * LANES : (j + 1) * LANES, :].astype(jnp.float32).T


def short_sequences(
    tokens, segments, attn_gain, qkv_weight, out_weight, mlp_gain, inner_weight, outer_weight, cotangent
):
    f = lax.axis_index("fsdp")
    c = lax.axis_index("ctx")
    t = lax.axis_index("tp")
    here = jnp.stack([f, c, t]).astype(jnp.int32)
    row_count, width = tokens.shape[1:]
    half_rows = row_count // 2
    shard = attn_gain.shape[0]
    units = inner_weight.shape[2]
    length = segments.shape[1]
    heads = 3 * LANES
    c_order = [c ^ r for r in range(4)]
    seg_row = jnp.concatenate(
        [lax.dynamic_slice_in_dim(segments[0], p * row_count, row_count) for p in c_order]
    )
    seg_col, seg_line = seg_row.reshape(length, 1), seg_row.reshape(1, length)
    own_tokens = tokens[0]
    out_cot = cotangent[0]

    def across(value):
        return hop(value, "fsdp", 2, 4)

    def beside(value):
        return hop(value, "fsdp", 1, 4)

    def over_tp(value):
        return hop(value, "tp", 1, 2)

    def over_ctx(value, bits):
        return value if bits == 0 else hop(value, "ctx", bits, 4)

    def gathered(value, crossed):
        return [value, beside(value), crossed, beside(crossed)]

    own_half = lax.dynamic_slice_in_dim(own_tokens, t * half_rows, half_rows)
    halves = [over_ctx(own_half, r) for r in (1, 2, 3)]

    by_ctx = [
        lax.dynamic_slice_in_dim(qkv_weight, p * LANES, LANES, 2).reshape(shard, heads).T for p in c_order
    ]
    gain_rows = jnp.concatenate(
        [attn_gain[None], mlp_gain[None], jnp.zeros((EXTRA - 2, shard), attn_gain.dtype)], axis=0
    )
    qkv_own = jnp.concatenate([by_ctx[0], gain_rows], axis=0)
    qkv_rest = jnp.concatenate(by_ctx[1:], axis=0)
    out_own = out_weight
    inner_own = jnp.concatenate([inner_weight[:, 0].T, inner_weight[:, 1].T], axis=0)
    outer_own = outer_weight

    qkv_crossed = across(qkv_own)
    qkv_here = gathered(qkv_own, qkv_crossed)
    out_pair = jnp.concatenate([out_own, over_tp(out_own)], axis=0)
    (out_pair,) = after([out_pair], qkv_crossed)
    out_crossed = across(out_pair)
    inner_own, outer_own = after([inner_own, outer_own], qkv_crossed)
    inner_crossed = across(inner_own)
    outer_crossed = across(outer_own)

    cosines, sines = zip(*[angle_tables(row_count, p * row_count, HD) for p in c_order])
    cosine, sine = jnp.concatenate(cosines, axis=0), jnp.concatenate(sines, axis=0)
    sign = jnp.where(jnp.arange(HD) < HD // 2, -1.0, 1.0).astype(jnp.float32)
    cosine = jnp.concatenate([cosine[:, 0]] * 2, axis=1)
    sine = jnp.concatenate([sine[:, 0] * sign] * 2, axis=1)

    def project(k, block):
        return local_call(
            functools.partial(project_block, k),
            [low_shape(row_count, width)] + [low_shape(row_count, LANES)] * 3 + [wide_shape(8, width)],
            here,
            [*block, *qkv_here, cosine, sine],
            scratch=[pltpu.VMEM((row_count, width), jnp.bfloat16)],
            flops=2 * row_count * width * heads,
        )

    projected = [project(0, [own_tokens])]
    for k in (1, 2, 3):
        (half,) = after([halves[k - 1]], *([projected[k - 2][1]] if k > 1 else []))
        projected.append(project(k, [half, over_tp(half)]))
    h_parts, queries, keys, values = [[p[i] for p in projected] for i in range(4)]
    gain_all = projected[0][4]

    raw, low, lse = local_call(
        attention_forward,
        [wide_shape(length, LANES), low_shape(length, LANES), wide_shape(8, length)],
        here,
        [*queries, *keys, *values, seg_col, seg_line],
        flops=8 * length * length * LANES,
        transcendentals=2 * length * length,
    )

    (inner_crossed,) = after([inner_crossed], low)
    inner_all = gathered(inner_own, inner_crossed)

    def between_ctx(value):
        return lax.all_to_all(value, "ctx", 0, 0, tiled=True)

    attended = between_ctx(low)
    attended_other = over_tp(attended)
    out_crossed, outer_crossed = after([out_crossed, outer_crossed], attended_other)
    out_all = gathered(out_pair, out_crossed)
    outer_all = gathered(outer_own, outer_crossed)
    (qkv_rest,) = after([qkv_rest], outer_crossed)
    rest_crossed = across(qkv_rest)
    rest_all = gathered(qkv_rest, rest_crossed)

    middle, second_low, hidden_low, gate_grad, up_grad, second_part, gain_two_part = local_call(
        feed_forward,
        [wide_shape(row_count, width), low_shape(row_count, width)]
        + [low_shape(row_count, units)] * 3
        + [low_shape(row_count, width), wide_shape(1, width)],
        here,
        [attended, attended_other, own_tokens, out_cot, gain_all, *out_all, *inner_all, *outer_all],
        scratch=[pltpu.VMEM((row_count, width), jnp.float32)],
        flops=2 * row_count * width * (width + 5 * units),
        transcendentals=2 * row_count * units,
    )

    def pieces(rows):
        return [low_shape(2, rows, shard), low_shape(rows, shard), low_shape(rows, shard)]

    def weight_grad(left, right):
        return local_call(
            weight_gradients,
            pieces(left.shape[1]),
            here,
            [left, right],
            flops=2 * left.shape[0] * width * left.shape[1],
        )

    at_end = jnp.logical_or(c == 0, c == 3)

    def chip_sum(keep, received, crossed):
        return add_rows(add_chip_piece, 0, keep, received, crossed)

    def ready(parts):
        sent, keep, keep_across = parts
        received = beside(sent)
        return [keep, received, add_rows(add_core_piece, 1, keep_across, received)]

    queue, inward, middle_out, outward, sums = [], {}, {}, {}, {}

    def advance(step, beside_it=()):
        arriving = {}
        if step < len(queue):
            arriving["x"] = across(queue[step][2])
        if step - 1 in inward:
            arriving["in"] = lax.ppermute(inward[step - 1], "ctx", [(0, 1), (3, 2)])
        if step - 2 in middle_out:
            arriving["mid"] = lax.ppermute(middle_out[step - 2], "ctx", [(1, 2), (2, 1)])
        if step - 3 in outward:
            arriving["out"] = lax.ppermute(outward[step - 3], "ctx", [(1, 0), (2, 3)])
        names = list(arriving)
        values = after([arriving[n] for n in names] + list(beside_it))
        arriving = dict(zip(names, values))
        if "x" in arriving:
            inward[step] = chip_sum(*queue[step][:2], arriving["x"])
        if "in" in arriving:
            middle_out[step - 1] = add_rows(add_line_piece, 0, inward[step - 1], arriving["in"])
        if "mid" in arriving:
            outward[step - 2] = add_rows(add_line_piece, 0, middle_out[step - 2], arriving["mid"])
        if "out" in arriving:
            sums[step - 3] = jnp.where(at_end, arriving["out"], outward[step - 3])
        return values[len(names) :]

    second_other = over_tp(second_part)
    outer_raw = weight_grad(hidden_low, out_cot)
    gate_raw = weight_grad(gate_grad, second_low)
    second_other, *raw_parts = after([second_other, *outer_raw, *gate_raw])
    queue.append(ready(raw_parts[:3]))
    queue.append(ready(raw_parts[3:]))

    attn_low, head_grads = local_call(
        head_gradients,
        [low_shape(row_count, width), low_shape(length, LANES)],
        here,
        [second_part, second_other, middle, out_cot, gain_all, *out_all],
        flops=row_count * width * width,
    )
    up_and_out = ready(
        local_call(
            up_and_out_gradients,
            pieces(units + EXTRA + 4 * LANES),
            here,
            [up_grad, second_low, gain_two_part, attn_low, attended],
            flops=2 * row_count * width * (units + 4 * LANES),
        )
    )
    head_grads = between_ctx(head_grads)
    head_grads, *up_and_out = advance(0, [head_grads, *up_and_out])
    queue.append(up_and_out)

    projected_grads = local_call(
        attention_backward,
        [low_shape(row_count, heads)] * 4,
        here,
        [*queries, *keys, *values, head_grads, raw, lse, cosine, sine, seg_col, seg_line],
        scratch=[pltpu.VMEM((LANES, length), jnp.float32)],
        flops=20 * length * length * LANES,
        transcendentals=2 * length * length,
    )
    first_parts = [over_ctx(projected_grads[k], k) for k in range(4)]
    qkv_ready = ready(
        local_call(
            qkv_gradients,
            pieces(heads + EXTRA),
            here,
            [*projected_grads, *h_parts, *qkv_here, gain_all],
            flops=2 * length * width * heads,
        )
    )
    *first_parts, k0, k1, k2 = advance(1, [*first_parts, *qkv_ready])
    qkv_ready = (k0, k1, k2)

    (first_low_part,) = local_call(
        first_gradients,
        [low_shape(row_count, width)],
        here,
        [*first_parts, *qkv_here, *rest_all],
        flops=2 * row_count * width * 4 * heads,
    )
    qkv_sum = lax.optimization_barrier(chip_sum(*qkv_ready[:2], across(qkv_ready[2])))
    first_other, qkv_sum = advance(2, [over_tp(first_low_part), qkv_sum])
    (input_grad,) = local_call(
        input_gradients,
        [wide_shape(row_count, width)],
        here,
        [first_low_part, first_other, own_tokens, gain_all, attn_low],
    )
    qkv_sums = [over_ctx(qkv_sum, k) for k in range(4)]

    (mlp_part,) = local_call(
        feed_forward_out,
        [low_shape(row_count, width)],
        here,
        [hidden_low, *outer_all],
        flops=2 * row_count * width * units,
    )
    qkv_sums = advance(3, qkv_sums)
    advance(4)
    advance(5)
    block_out = (
        middle + (mlp_part.astype(jnp.float32) + over_tp(mlp_part).astype(jnp.float32))
    ).astype(jnp.bfloat16)
    gain_two_grad = sums[2][units].astype(jnp.float32)

    (qkv_grad,) = local_call(qkv_layout, [wide_shape(shard, 4 * heads)], here, qkv_sums)
    gain_lines = [part[heads].astype(jnp.float32) for part in qkv_sums]
    gain_one_grad = (gain_lines[0] + gain_lines[1]) + (gain_lines[2] + gain_lines[3])

    return (
        block_out[None],
        input_grad[None],
        gain_one_grad + over_tp(gain_one_grad),
        qkv_grad.reshape(shard, 3, 4 * LANES),
        sums[2][units + EXTRA :].astype(jnp.float32),
        gain_two_grad + over_tp(gain_two_grad),
        jnp.stack([sums[1].T, sums[2][:units].T], axis=1).astype(jnp.float32),
        sums[0].astype(jnp.float32),
    )


def solution(mesh):
    placed = (
        P("fsdp", "ctx", None),
        P("fsdp", None),
        P("fsdp"),
        P("fsdp", None, "tp"),
        P("tp", "fsdp"),
        P("fsdp"),
        P("fsdp", None, "tp"),
        P("tp", "fsdp"),
        P("fsdp", "ctx", None),
    )
    sizes = dict(mesh.shape)

    def layer(*args):
        tokens, segments, qkv_weight = args[0], args[1], args[3]
        heads_apart = qkv_weight.shape[2] == 4 * LANES
        short = segments.shape[1] == 4 * tokens.shape[1] and segments.shape[1] <= 1024
        small = (sizes["fsdp"], sizes["ctx"], sizes["tp"]) == (4, 4, 2)
        if small and short and heads_apart and tokens.shape[0] == 1:
            return short_sequences(*args)
        return per_device(*args)

    return jax.shard_map(
        layer,
        mesh=mesh,
        in_specs=placed,
        out_specs=(
            P("fsdp", "ctx", None),
            P("fsdp", "ctx", None),
            P("fsdp"),
            P("fsdp", None, "tp"),
            P("tp", "fsdp"),
            P("fsdp"),
            P("fsdp", None, "tp"),
            P("tp", "fsdp"),
        ),
        check_vma=False,
    )
```

```python
import functools
import math

import jax
import jax.numpy as jnp
from jax import lax
from jax.experimental import pallas as pl
from jax.experimental.pallas import tpu as pltpu
from jax.sharding import PartitionSpec as P

HD = 64


EPSILON = 1e-05
ROPE_BASE = 160000.0
MASKED = -1e30


def normalize(values, gain_row):
    row_mean = jnp.mean(values, axis=-1, keepdims=True)
    centered = values - row_mean
    spread = jnp.mean(centered * centered, axis=-1, keepdims=True)
    return centered * lax.rsqrt(spread + EPSILON) * gain_row


def geglu(gate_in, upper):
    return jax.nn.gelu(gate_in, approximate=False) * upper


def angle_tables(row_count, offset, depth):
    half_width = depth // 2
    inverse = jnp.power(
        jnp.float32(ROPE_BASE), -(2.0 * jnp.arange(half_width, dtype=jnp.float32)) / depth
    )
    places = (offset + jnp.arange(row_count, dtype=jnp.int32)).astype(jnp.float32)
    angles = places[:, None] * inverse[None, :]
    angles = jnp.concatenate([angles, angles], axis=-1)
    return (jnp.cos(angles)[:, None, :], jnp.sin(angles)[:, None, :])


def rotate(values, cosine, sine):
    half_width = values.shape[-1] // 2
    turned = jnp.concatenate([-values[..., half_width:], values[..., :half_width]], axis=-1)
    return values * cosine + turned * sine


def rotate_back(grad_in, cosine, sine):
    half_width = grad_in.shape[-1] // 2
    scaled = grad_in * sine
    turned = jnp.concatenate([scaled[..., half_width:], -scaled[..., :half_width]], axis=-1)
    return grad_in * cosine + turned


def attend_forward(queries, query_seg, seg_row, key_low, value_low, score_scale):
    row_count, heads_here, depth = queries.shape
    initial = (
        jnp.full((heads_here, row_count), MASKED, jnp.float32),
        jnp.zeros((heads_here, row_count), jnp.float32),
        jnp.zeros((row_count, heads_here, depth), jnp.float32),
    )
    key_piece = lax.all_gather(key_low, "ctx", axis=0, tiled=True)
    value_piece = lax.all_gather(value_low, "ctx", axis=0, tiled=True)
    piece_rows = key_piece.shape[0]
    block_size = math.gcd(piece_rows, 512)
    blocks = (
        key_piece.reshape(piece_rows // block_size, block_size, heads_here, depth),
        value_piece.reshape(piece_rows // block_size, block_size, heads_here, depth),
        seg_row.reshape(piece_rows // block_size, block_size),
    )

    def step(state, block_data):
        running_peak, running_total, accum = state
        key_block, value_block, block_seg = block_data
        scores = jnp.einsum("qhe,khe->hqk", queries, key_block, preferred_element_type=jnp.float32)
        same_doc = (query_seg[:, None] == block_seg[None, :])[None]
        logits = jnp.where(same_doc, scores * score_scale, MASKED)
        new_peak = jnp.maximum(running_peak, jnp.max(logits, axis=-1))
        rescale = jnp.exp(running_peak - new_peak)
        weights = jnp.where(same_doc, jnp.exp(logits - new_peak[:, :, None]), 0.0)
        running_total = running_total * rescale + jnp.sum(weights, axis=-1)
        mixed_out = jnp.einsum(
            "hqk,khe->qhe",
            weights.astype(jnp.bfloat16),
            value_block,
            preferred_element_type=jnp.float32,
        )
        accum = accum * rescale.T[:, :, None] + mixed_out
        return ((new_peak, running_total, accum), None)

    result, unused = lax.scan(step, initial, blocks)
    running_peak, running_total, accum = result
    return (accum / running_total.T[:, :, None], running_peak + jnp.log(running_total))


def probs_and_grads(
    query_block, key_block, grad_block, value_block, same_doc, log_total, delta_rows, score_scale
):
    scores = jnp.einsum("qhe,khe->hqk", query_block, key_block, preferred_element_type=jnp.float32)
    probs = jnp.where(same_doc, jnp.exp(scores * score_scale - log_total[:, :, None]), 0.0)
    prob_grad = jnp.einsum(
        "qhe,khe->hqk", grad_block, value_block, preferred_element_type=jnp.float32
    )
    score_grad = (probs * (prob_grad - delta_rows[:, :, None]) * score_scale).astype(jnp.bfloat16)
    return (probs.astype(jnp.bfloat16), score_grad)


def attend_backward(
    queries, key_low, value_low, grad_low, log_total, delta_rows, query_seg, seg_row, score_scale
):
    row_count, heads_here, depth = queries.shape
    seq_length = seg_row.shape[0]
    block_size = math.gcd(seq_length, 512)
    block_count = seq_length // block_size
    key_all, value_all = (
        lax.all_gather(key_low, "ctx", axis=0, tiled=True),
        lax.all_gather(value_low, "ctx", axis=0, tiled=True),
    )
    blocks = (
        key_all.reshape(block_count, block_size, heads_here, depth),
        value_all.reshape(block_count, block_size, heads_here, depth),
        seg_row.reshape(block_count, block_size),
    )

    def key_step(query_acc, block_data):
        key_block, value_block, block_seg = block_data
        same_doc = (query_seg[:, None] == block_seg[None, :])[None]
        prob_low, score_grad = probs_and_grads(
            queries, key_block, grad_low, value_block, same_doc, log_total, delta_rows, score_scale
        )
        query_acc = query_acc + jnp.einsum(
            "hqk,khe->qhe", score_grad, key_block, preferred_element_type=jnp.float32
        )
        key_part = jnp.einsum(
            "hqk,qhe->khe", score_grad, queries, preferred_element_type=jnp.float32
        )
        value_part = jnp.einsum(
            "hqk,qhe->khe", prob_low, grad_low, preferred_element_type=jnp.float32
        )
        return (query_acc, (key_part, value_part))

    query_grad, key_value_parts = lax.scan(
        key_step, jnp.zeros((row_count, heads_here, depth), jnp.float32), blocks
    )
    key_parts = key_value_parts[0].reshape(seq_length, heads_here * depth)
    value_parts = key_value_parts[1].reshape(seq_length, heads_here * depth)
    key_grad, value_grad = (
        lax.psum_scatter(
            key_parts.astype(jnp.bfloat16), "ctx", scatter_dimension=0, tiled=True
        ).astype(jnp.float32),
        lax.psum_scatter(
            value_parts.astype(jnp.bfloat16), "ctx", scatter_dimension=0, tiled=True
        ).astype(jnp.float32),
    )
    key_grad = key_grad.reshape(row_count, heads_here, depth)
    value_grad = value_grad.reshape(row_count, heads_here, depth)
    return (query_grad, key_grad, value_grad)


def per_device(
    tokens,
    segments,
    attn_gain,
    qkv_weight,
    out_weight,
    mlp_gain,
    inner_weight,
    outer_weight,
    cotangent,
):
    qkv_full, out_full, gain_one = (
        lax.all_gather(qkv_weight, "fsdp", axis=0, tiled=True),
        lax.all_gather(out_weight, "fsdp", axis=1, tiled=True),
        lax.all_gather(attn_gain, "fsdp", axis=0, tiled=True),
    )
    inner_full, outer_full, gain_two = (
        lax.all_gather(inner_weight, "fsdp", axis=0, tiled=True),
        lax.all_gather(outer_weight, "fsdp", axis=1, tiled=True),
        lax.all_gather(mlp_gain, "fsdp", axis=0, tiled=True),
    )
    seq_count, row_count, model_width = tokens.shape
    local_width = qkv_full.shape[2]
    heads_here = local_width // HD
    score_scale = HD ** (-0.5)
    offset = lax.axis_index("ctx") * row_count
    cosine, sine = angle_tables(row_count, offset, HD)
    input_rows = tokens.reshape(-1, model_width).astype(jnp.float32)
    normed_one, norm_one_back = jax.vjp(normalize, input_rows, gain_one.astype(jnp.float32))
    first_low = normed_one.astype(jnp.bfloat16)
    projected_output = jnp.einsum(
        "td,dcf->tcf", first_low, qkv_full, preferred_element_type=jnp.float32
    )
    projected_output = projected_output.reshape(seq_count, row_count, 3, heads_here, HD)
    query_low = rotate(projected_output[:, :, 0], cosine, sine).astype(jnp.bfloat16)
    key_low = rotate(projected_output[:, :, 1], cosine, sine).astype(jnp.bfloat16)
    value_low = projected_output[:, :, 2].astype(jnp.bfloat16)
    seq_index = 0
    seg_row = segments[seq_index]
    query_seg = lax.dynamic_slice_in_dim(seg_row, offset, row_count)
    raw_out, log_total = attend_forward(
        query_low[seq_index],
        query_seg,
        seg_row,
        key_low[seq_index],
        value_low[seq_index],
        score_scale,
    )
    query_segs = [query_seg]
    raw_outs = [raw_out]
    log_totals = [log_total]
    attended_low = jnp.stack(raw_outs).astype(jnp.bfloat16).reshape(-1, local_width)
    attn_part = jnp.dot(attended_low, out_full, preferred_element_type=jnp.float32)
    middle_activation = input_rows + lax.psum(attn_part.astype(jnp.bfloat16), "tp").astype(
        jnp.float32
    )
    normed_two, norm_two_back = jax.vjp(normalize, middle_activation, gain_two.astype(jnp.float32))
    second_low = normed_two.astype(jnp.bfloat16)
    hidden_input = jnp.einsum(
        "td,dcf->tcf", second_low, inner_full, preferred_element_type=jnp.float32
    )
    hidden_state, geglu_back = jax.vjp(geglu, hidden_input[:, 0], hidden_input[:, 1])
    hidden_low = hidden_state.astype(jnp.bfloat16)
    mlp_part = jnp.dot(hidden_low, outer_full, preferred_element_type=jnp.float32)
    block_out = (
        middle_activation + lax.psum(mlp_part.astype(jnp.bfloat16), "tp").astype(jnp.float32)
    ).astype(jnp.bfloat16)
    out_cot = cotangent.reshape(-1, model_width)
    outer_local = jnp.einsum("tf,td->fd", hidden_low, out_cot, preferred_element_type=jnp.float32)
    hidden_grad = jnp.einsum("td,fd->tf", out_cot, outer_full, preferred_element_type=jnp.float32)
    gate_grad, up_grad = geglu_back(hidden_grad)
    inner_low = jnp.stack([gate_grad, up_grad], axis=1).astype(jnp.bfloat16)
    inner_local = jnp.einsum(
        "td,tcf->dcf", second_low, inner_low, preferred_element_type=jnp.float32
    )
    normed_two_grad = lax.psum(
        jnp.einsum("tcf,dcf->td", inner_low, inner_full, preferred_element_type=jnp.float32).astype(
            jnp.bfloat16
        ),
        "tp",
    ).astype(jnp.float32)
    middle_part, gain_two_grad = norm_two_back(normed_two_grad)
    middle_grad = out_cot.astype(jnp.float32) + middle_part
    attn_low = middle_grad.astype(jnp.bfloat16)
    out_local = jnp.einsum("tf,td->fd", attended_low, attn_low, preferred_element_type=jnp.float32)
    attended_grad = jnp.einsum("td,fd->tf", attn_low, out_full, preferred_element_type=jnp.float32)
    attended_grad = attended_grad.astype(jnp.bfloat16).reshape(seq_count, row_count, heads_here, HD)
    seq_index = 0
    grad_low = attended_grad[seq_index]
    delta_rows = jnp.sum(grad_low.astype(jnp.float32) * raw_outs[seq_index], axis=-1).T
    query_grad, key_grad, value_grad = attend_backward(
        query_low[seq_index],
        key_low[seq_index],
        value_low[seq_index],
        grad_low,
        log_totals[seq_index],
        delta_rows,
        query_segs[seq_index],
        segments[seq_index],
        score_scale,
    )
    stacked = jnp.stack(
        [rotate_back(query_grad, cosine, sine), rotate_back(key_grad, cosine, sine), value_grad],
        axis=1,
    )
    qkv_grads = stacked.reshape(row_count, 3, local_width)
    qkv_low = qkv_grads.astype(jnp.bfloat16)
    qkv_local = jnp.einsum("td,tcf->dcf", first_low, qkv_low, preferred_element_type=jnp.float32)
    normed_one_grad = lax.psum(
        jnp.einsum("tcf,dcf->td", qkv_low, qkv_full, preferred_element_type=jnp.float32).astype(
            jnp.bfloat16
        ),
        "tp",
    ).astype(jnp.float32)
    input_part, gain_one_grad = norm_one_back(normed_one_grad)
    input_grad = (middle_grad + input_part).reshape(tokens.shape)
    summed = (
        lax.psum_scatter(gain_one_grad, ("fsdp", "ctx"), scatter_dimension=0, tiled=True),
        lax.psum_scatter(qkv_local, ("fsdp", "ctx"), scatter_dimension=0, tiled=True),
        lax.psum_scatter(out_local, ("fsdp", "ctx"), scatter_dimension=1, tiled=True),
        lax.psum_scatter(gain_two_grad, ("fsdp", "ctx"), scatter_dimension=0, tiled=True),
        lax.psum_scatter(inner_local, ("fsdp", "ctx"), scatter_dimension=0, tiled=True),
        lax.psum_scatter(outer_local, ("fsdp", "ctx"), scatter_dimension=1, tiled=True),
    )
    gain_one_sum, qkv_sum, out_sum, gain_two_sum, inner_sum, outer_sum = summed
    shards = (
        lax.all_gather(gain_one_sum.astype(jnp.bfloat16), "ctx", axis=0, tiled=True).astype(
            gain_one_sum.dtype
        ),
        lax.all_gather(qkv_sum.astype(jnp.bfloat16), "ctx", axis=0, tiled=True).astype(
            qkv_sum.dtype
        ),
        lax.all_gather(out_sum.astype(jnp.bfloat16), "ctx", axis=1, tiled=True).astype(
            out_sum.dtype
        ),
        lax.all_gather(gain_two_sum.astype(jnp.bfloat16), "ctx", axis=0, tiled=True).astype(
            gain_two_sum.dtype
        ),
        lax.all_gather(inner_sum.astype(jnp.bfloat16), "ctx", axis=0, tiled=True).astype(
            inner_sum.dtype
        ),
        lax.all_gather(outer_sum.astype(jnp.bfloat16), "ctx", axis=1, tiled=True).astype(
            outer_sum.dtype
        ),
    )
    return (
        block_out.reshape(tokens.shape),
        input_grad,
        shards[0],
        shards[1],
        shards[2],
        shards[3],
        shards[4],
        shards[5],
    )


LANES = 128
BLOCK = 256
EXTRA = 32
COST = 0.0
WIDE_VMEM = 62 * 1024 * 1024


def hop(value, axis, bit, count):
    return lax.ppermute(value, axis, [(i, i ^ bit) for i in range(count)])


def after(values, *earlier):
    values = list(values)
    return list(lax.optimization_barrier(tuple(values) + earlier))[: len(values)]


def lane_half(shape):
    return lax.broadcasted_iota(jnp.int32, shape, 1) < HD


def swap_halves(values):
    lane = lax.broadcasted_iota(jnp.int32, values.shape, 1)
    low_part = lax.rem(lane, HD) < HD // 2
    return jnp.where(
        low_part,
        pltpu.roll(values, LANES - HD // 2, 1),
        pltpu.roll(values, HD // 2, 1),
    )


def dot_nt(left, right):
    return lax.dot_general(left, right, (((1,), (1,)), ((), ())), preferred_element_type=jnp.float32)


def dot_nn(left, right):
    return lax.dot_general(left, right, (((1,), (0,)), ((), ())), preferred_element_type=jnp.float32)


def dot_tn(left, right):
    return lax.dot_general(left, right, (((0,), (0,)), ((), ())), preferred_element_type=jnp.float32)


def one_head(values, head):
    first = lane_half(values.shape)
    keep = first if head == 0 else jnp.logical_not(first)
    return jnp.where(keep, values, jnp.zeros_like(values))


def part_of(index, size):
    return pl.ds(pl.multiple_of(index * size, size), size)


def standardize(values):
    row_mean = jnp.mean(values, axis=-1, keepdims=True)
    centered = values - row_mean
    spread = jnp.mean(centered * centered, axis=-1, keepdims=True)
    scale = lax.rsqrt(spread + EPSILON)
    return centered * scale, scale


def standardize_back(normed, scale, grad):
    inner = jnp.mean(grad * normed, axis=-1, keepdims=True)
    return scale * (grad - jnp.mean(grad, axis=-1, keepdims=True) - normed * inner)


def local_call(body, outs, places, operands, scratch=(), flops=0, transcendentals=0):
    moved = sum(math.prod(o.shape) * o.dtype.itemsize for o in list(operands) + list(outs))
    return pl.pallas_call(
        body,
        name=body.__name__ if hasattr(body, "__name__") else body.func.__name__,
        out_shape=tuple(outs),
        in_specs=[pl.BlockSpec(memory_space=pltpu.SMEM)]
        + [pl.BlockSpec(memory_space=pltpu.VMEM)] * len(operands),
        out_specs=tuple([pl.BlockSpec(memory_space=pltpu.VMEM)] * len(outs)),
        scratch_shapes=list(scratch),
        compiler_params=pltpu.CompilerParams(vmem_limit_bytes=WIDE_VMEM),
        cost_estimate=pl.CostEstimate(
            flops=int(flops * COST), bytes_accessed=int(moved * COST), transcendentals=int(transcendentals * COST)
        ),
    )(places, *operands)


def low_shape(*shape):
    return jax.ShapeDtypeStruct(shape, jnp.bfloat16)


def wide_shape(*shape):
    return jax.ShapeDtypeStruct(shape, jnp.float32)


def project_block(block, at, *refs):
    f, t = at[0], at[2]
    count = len(refs) - 12
    tokens_in, (w0, w1, w2, w3, cos_ref, sin_ref) = refs[:count], refs[count : count + 6]
    h_ref, q_ref, k_ref, v_ref, gain_ref, x_ref = refs[count + 6 :]
    weights = (w0, w1, w2, w3)
    columns = [part_of(f ^ r, w0.shape[1]) for r in range(4)]
    heads = 3 * LANES
    for r, weight in enumerate(weights):
        gain_ref[:, columns[r]] = weight[heads : heads + EXTRA, :].astype(jnp.float32)[:8, :]
    if count == 1:
        tokens = tokens_in[0][...]
    else:
        half = tokens_in[0].shape[0]
        x_ref[part_of(t, half), :] = tokens_in[0][...]
        x_ref[part_of(1 - t, half), :] = tokens_in[1][...]
        tokens = x_ref[...]
    h_ref[...] = (standardize(tokens.astype(jnp.float32))[0] * gain_ref[0:1, :]).astype(jnp.bfloat16)
    projected = 0.0
    for r, weight in enumerate(weights):
        projected += dot_nt(h_ref[:, columns[r]], weight[:heads, :])
    rows = slice(block * tokens.shape[0], (block + 1) * tokens.shape[0])
    cosine, sine = cos_ref[rows, :], sin_ref[rows, :]
    for ref, part in ((q_ref, projected[:, :LANES]), (k_ref, projected[:, LANES : 2 * LANES])):
        ref[...] = (part * cosine + swap_halves(part) * sine).astype(jnp.bfloat16)
    v_ref[...] = projected[:, 2 * LANES :].astype(jnp.bfloat16)


def joined(refs):
    return jnp.concatenate([ref[...] for ref in refs], axis=0)


def attention_forward(at, *refs):
    c = at[1]
    query_refs, key_refs, value_refs, seg_col, seg_line = refs[:4], refs[4:8], refs[8:12], refs[12], refs[13]
    raw_ref, low_ref, lse_ref = refs[14:]
    rows_here = query_refs[0].shape[0]
    keys, values = joined(key_refs), joined(value_refs)
    for k in range(4):
        rows = slice(k * rows_here, (k + 1) * rows_here)
        queries = query_refs[k][...] * jnp.bfloat16(HD ** (-0.5))
        same = seg_col[rows, :] == seg_line[...]
        outs, logs = [], []
        for head in range(2):
            scores = dot_nt(one_head(queries, head), keys)
            scores = jnp.where(same, scores, MASKED)
            peak = jnp.max(scores, axis=1, keepdims=True)
            weights = jnp.exp(scores - peak)
            total = jnp.sum(weights, axis=1, keepdims=True)
            probs = (weights * (1.0 / total)).astype(jnp.bfloat16)
            outs.append(dot_nn(probs, values))
            logs.append(peak + jnp.log(total))
        raw = jnp.where(lane_half(outs[0].shape), outs[0], outs[1])
        raw_ref[rows, :] = raw
        low_ref[part_of(c ^ k, rows_here), :] = raw.astype(jnp.bfloat16)
        lane = lax.broadcasted_iota(jnp.int32, (rows_here, LANES), 1)
        lse_ref[:, rows] = jnp.where(lane == 0, logs[0], logs[1]).T[:8, :]


def attention_backward(
    at, q0, q1, q2, q3, k0, k1, k2, k3, v0, v1, v2, v3, do_ref, raw_ref, lse_ref, cos_ref, sin_ref,
    seg_col, seg_line, out_ref, turned_ref,
):
    c = at[1]
    rows_here = q0.shape[0]
    grads = jnp.concatenate([do_ref[part_of(c ^ k, rows_here), :] for k in range(4)], axis=0)
    product = grads.astype(jnp.float32) * raw_ref[...]
    first = lane_half(product.shape)
    whole = jnp.sum(jnp.where(first, product, 0.0), axis=1, keepdims=True)
    other = jnp.sum(jnp.where(first, 0.0, product), axis=1, keepdims=True)
    lane = lax.broadcasted_iota(jnp.int32, product.shape, 1)
    delta = jnp.where(lane == 0, whole, other).T
    scale = HD ** (-0.5)
    queries = joined((q0, q1, q2, q3))
    scaled = queries * jnp.bfloat16(scale)
    for k in range(4):
        rows, place = slice(k * rows_here, (k + 1) * rows_here), part_of(c ^ k, rows_here)
        keys, values = (k0, k1, k2, k3)[k][...], (v0, v1, v2, v3)[k][...]
        keys_turned = keys.T
        same = seg_col[rows, :] == seg_line[...]
        key_parts, value_parts = [], []
        for head in range(2):
            scores = dot_nt(one_head(keys, head), scaled)
            probs = jnp.where(same, jnp.exp(scores - lse_ref[head : head + 1, :]), 0.0)
            prob_grad = dot_nt(one_head(values, head), grads)
            score_grad = (probs * (prob_grad - delta[head : head + 1, :]) * scale).astype(jnp.bfloat16)
            value_parts.append(dot_nn(probs.astype(jnp.bfloat16), grads))
            key_parts.append(dot_nn(score_grad, queries))
            here = slice(head * HD, (head + 1) * HD)
            part = dot_nn(keys_turned[here, :], score_grad)
            if k == 0:
                turned_ref[here, :] = part
            else:
                turned_ref[here, :] += part
        half = lane_half(key_parts[0].shape)
        key_grad = jnp.where(half, key_parts[0], key_parts[1])
        value_grad = jnp.where(half, value_parts[0], value_parts[1])
        key_grad = key_grad * cos_ref[rows, :] - swap_halves(key_grad) * sin_ref[rows, :]
        out_ref[place, LANES : 2 * LANES] = key_grad.astype(jnp.bfloat16)
        out_ref[place, 2 * LANES :] = value_grad.astype(jnp.bfloat16)
    for k in range(4):
        rows, place = slice(k * rows_here, (k + 1) * rows_here), part_of(c ^ k, rows_here)
        query_grad = turned_ref[:, rows].T
        query_grad = query_grad * cos_ref[rows, :] - swap_halves(query_grad) * sin_ref[rows, :]
        out_ref[place, :LANES] = query_grad.astype(jnp.bfloat16)


def feed_forward(
    at, own_ref, other_ref, x_ref, cot_ref, gain_ref,
    o0, o1, o2, o3, inner0, inner1, inner2, inner3, outer0, outer1, outer2, outer3,
    mid_ref, normed_ref, second_ref, acts_ref,
):
    f = at[0]
    rows_here = x_ref.shape[0]
    attended = jnp.concatenate(
        [ref[k * rows_here : (k + 1) * rows_here, :] for ref in (own_ref, other_ref) for k in range(4)],
        axis=1,
    )
    inners, outers = (inner0, inner1, inner2, inner3), (outer0, outer1, outer2, outer3)
    columns = [part_of(f ^ r, o0.shape[1]) for r in range(4)]
    for r, weight in enumerate((o0, o1, o2, o3)):
        mid_ref[:, columns[r]] = x_ref[:, columns[r]].astype(jnp.float32) + dot_nn(attended, weight[...])
    normed = standardize(mid_ref[...])[0]
    normed_ref[...] = normed
    second_ref[...] = (normed * gain_ref[1:2, :]).astype(jnp.bfloat16)
    units = outer0.shape[0]
    for start in range(0, units, BLOCK):
        stop = min(start + BLOCK, units)
        gate, up, hid_grad = 0.0, 0.0, 0.0
        for r in range(4):
            rows = second_ref[:, columns[r]]
            gate += dot_nt(rows, inners[r][start:stop, :])
            up += dot_nt(rows, inners[r][units + start : units + stop, :])
            hid_grad += dot_nt(cot_ref[:, columns[r]], outers[r][start:stop, :])
        below = 0.5 + 0.5 * lax.erf(gate * (2.0 ** -0.5))
        density = jnp.exp(-0.5 * gate * gate) * ((2.0 * math.pi) ** -0.5)
        active = gate * below
        acts_ref[:rows_here, start:stop] = (active * up).astype(jnp.bfloat16)
        acts_ref[rows_here : 2 * rows_here, start:stop] = (
            hid_grad * up * (below + gate * density)
        ).astype(jnp.bfloat16)
        acts_ref[2 * rows_here :, start:stop] = (hid_grad * active).astype(jnp.bfloat16)


def feed_forward_back(
    at, acts_ref, normed_ref, inner0, inner1, inner2, inner3, low_ref, gain_grad_ref
):
    f = at[0]
    rows_here = normed_ref.shape[0]
    units = inner0.shape[0] // 2
    gate_grad = acts_ref[rows_here : 2 * rows_here, :units]
    up_grad = acts_ref[2 * rows_here :, :units]
    for r, inner in enumerate((inner0, inner1, inner2, inner3)):
        columns = part_of(f ^ r, inner.shape[1])
        part = dot_nn(gate_grad, inner[:units, :]) + dot_nn(up_grad, inner[units:, :])
        low_ref[:, columns] = part.astype(jnp.bfloat16)
        gain_grad_ref[:, columns] = jnp.sum(part * normed_ref[:, columns], axis=0, keepdims=True)


def feed_forward_out(at, acts_ref, outer0, outer1, outer2, outer3, out_ref):
    f = at[0]
    hidden = acts_ref[: out_ref.shape[0], : outer0.shape[0]]
    for r, weight in enumerate((outer0, outer1, outer2, outer3)):
        out_ref[:, part_of(f ^ r, weight.shape[1])] = dot_nn(hidden, weight[...]).astype(jnp.bfloat16)


def head_gradients(
    at, mine_ref, other_ref, mid_ref, cot_ref, gain_ref, o0, o1, o2, o3, da_ref, out_ref
):
    f = at[0]
    grad = (mine_ref[...].astype(jnp.float32) + other_ref[...].astype(jnp.float32)) * gain_ref[1:2, :]
    normed, scale = standardize(mid_ref[...])
    mid_grad = cot_ref[...].astype(jnp.float32) + standardize_back(normed, scale, grad)
    da_ref[...] = mid_grad.astype(jnp.bfloat16)
    total = 0.0
    for r, weight in enumerate((o0, o1, o2, o3)):
        total += dot_nt(da_ref[:, part_of(f ^ r, weight.shape[1])], weight[: 4 * LANES, :])
    rows_here = da_ref.shape[0]
    for k in range(4):
        out_ref[k * rows_here : (k + 1) * rows_here, :] = total[
            :, k * LANES : (k + 1) * LANES
        ].astype(jnp.bfloat16)


def store_piece(r, value, send_ref, keep_ref, keep_across_ref, rows=slice(None)):
    if r in (1, 3):
        send_ref[r // 2, rows, :] = value
    else:
        (keep_ref if r == 0 else keep_across_ref)[rows, :] = value


def extra_rows(row):
    lines = lax.broadcasted_iota(jnp.int32, (EXTRA, row.shape[1]), 0)
    return jnp.where(lines == 0, row, 0.0).astype(jnp.bfloat16)


def add_arrays(steps, *refs):
    count = len(refs) - len(steps)
    arrays, outs = refs[:count], refs[count:]
    for out, step in zip(outs, steps):
        if step[0][0] == "rows":
            first, second, third, fourth = [arrays[index][...].astype(jnp.float32) for kind, index in step]
            out[: first.shape[0], :] = (first + second).astype(jnp.bfloat16)
            out[first.shape[0] :, :] = (third + fourth).astype(jnp.bfloat16)
            continue
        total = 0.0
        for kind, index in step:
            total += (outs if kind == "out" else arrays)[index][...].astype(jnp.float32)
        out[...] = total.astype(jnp.bfloat16)


def pair_columns(f, shard):
    return part_of(f, shard), part_of(f ^ 2, shard)


def mlp_gradients(
    at, own_ref, other_ref, second_ref, second_other, cot_ref, cot_other,
    outer_keep, outer_cross, gate_keep, gate_cross, up_keep, up_cross,
):
    f = at[0]
    units, shard = outer_keep.shape
    tokens = cot_ref.shape[0]
    early = gate_keep.shape[0] - units
    parts = (
        (0, 0, units, cot_ref, cot_other, outer_keep, outer_cross, 0),
        (1, 0, units, second_ref, second_other, gate_keep, gate_cross, 0),
        (2, 0, early, second_ref, second_other, gate_keep, gate_cross, units),
        (2, early, units, second_ref, second_other, up_keep, up_cross, 0),
    )
    for i, start, stop, right, right_other, keep, cross, first in parts:
        rows = slice(i * tokens, (i + 1) * tokens)
        for columns, out_ref in zip(pair_columns(f, shard), (keep, cross)):
            value = dot_tn(own_ref[rows, start:stop], right[:, columns])
            value += dot_tn(other_ref[rows, start:stop], right_other[:, columns])
            out_ref[first : first + stop - start, :] = value.astype(jnp.bfloat16)


def out_gradients(
    at, attended_ref, attended_other, da_ref, da_other, gain_grad_ref, gain_grad_other, keep_ref, cross_ref
):
    f = at[0]
    rows_here = da_ref.shape[0]
    own, other = [
        jnp.concatenate([ref[k * rows_here : (k + 1) * rows_here, :] for k in range(4)], axis=1)
        for ref in (attended_ref, attended_other)
    ]
    for columns, out_ref in zip(pair_columns(f, keep_ref.shape[1]), (keep_ref, cross_ref)):
        value = dot_tn(own, da_ref[:, columns]) + dot_tn(other, da_other[:, columns])
        out_ref[: 4 * LANES, :] = value.astype(jnp.bfloat16)
        out_ref[4 * LANES :, :] = extra_rows(gain_grad_ref[:, columns] + gain_grad_other[:, columns])


def qkv_gradients(at, grad_ref, h0, h1, h2, h3, w0, w1, w2, w3, gain_ref, *outs):
    f, c = at[0], at[1]
    rows, shard = grad_ref.shape[1], w0.shape[1]
    rows_here = h0.shape[0]
    for r in (1, 3, 2, 0):
        columns = part_of(f ^ r, shard)
        value = 0.0
        for k, left in enumerate((h0, h1, h2, h3)):
            value += dot_tn(grad_ref[part_of(c ^ k, rows_here), :], left[:, columns])
        store_piece(r, value.astype(jnp.bfloat16), *outs, rows=slice(0, rows))
        weight = (w0, w1, w2, w3)[r][:rows, :].astype(jnp.float32)
        gain_grad = jnp.sum(weight * value, axis=0, keepdims=True) / gain_ref[0:1, columns]
        store_piece(r, extra_rows(gain_grad), *outs, rows=slice(rows, rows + EXTRA))


def first_gradients(at, grad_ref, q0, q1, q2, q3, rest0, rest1, rest2, rest3, low_ref):
    f, c = at[0], at[1]
    rows_here = low_ref.shape[0]
    grads = [grad_ref[part_of(c ^ k, rows_here), :] for k in range(4)]
    others = jnp.concatenate(grads[1:], axis=1)
    heads = 3 * LANES
    for r in range(4):
        own, rest = (q0, q1, q2, q3)[r], (rest0, rest1, rest2, rest3)[r]
        part = dot_nn(grads[0], own[:heads, :]) + dot_nn(others, rest[...])
        low_ref[:, part_of(f ^ r, own.shape[1])] = part.astype(jnp.bfloat16)


def input_gradients(at, mine_ref, other_ref, x_ref, gain_ref, da_ref, out_ref):
    grad = (mine_ref[...].astype(jnp.float32) + other_ref[...].astype(jnp.float32)) * gain_ref[0:1, :]
    normed, scale = standardize(x_ref[...].astype(jnp.float32))
    out_ref[...] = da_ref[...].astype(jnp.float32) + standardize_back(normed, scale, grad)


def qkv_layout(at, p0, p1, p2, p3, out_ref):
    c = at[1]
    for k, part in enumerate((p0, p1, p2, p3)):
        for j in range(3):
            out_ref[j, :, part_of(c ^ k, LANES)] = part[j * LANES : (j + 1) * LANES, :].astype(jnp.float32).T


def short_sequences(
    tokens, segments, attn_gain, qkv_weight, out_weight, mlp_gain, inner_weight, outer_weight, cotangent
):
    f = lax.axis_index("fsdp")
    c = lax.axis_index("ctx")
    t = lax.axis_index("tp")
    here = jnp.stack([f, c, t]).astype(jnp.int32)
    row_count, width = tokens.shape[1:]
    half_rows = row_count // 2
    shard = attn_gain.shape[0]
    units = inner_weight.shape[2]
    length = segments.shape[1]
    heads = 3 * LANES
    c_order = [c ^ r for r in range(4)]
    seg_row = jnp.concatenate(
        [lax.dynamic_slice_in_dim(segments[0], p * row_count, row_count) for p in c_order]
    )
    seg_col, seg_line = seg_row.reshape(length, 1), seg_row.reshape(1, length)
    own_tokens = tokens[0]
    out_cot = cotangent[0]

    def across(value):
        return hop(value, "fsdp", 2, 4)

    def beside(value):
        return hop(value, "fsdp", 1, 4)

    def over_tp(value):
        return hop(value, "tp", 1, 2)

    def over_ctx(value, bits):
        return value if bits == 0 else hop(value, "ctx", bits, 4)

    def gathered(value, crossed):
        return [value, beside(value), crossed, beside(crossed)]

    own_half = lax.dynamic_slice_in_dim(own_tokens, t * half_rows, half_rows)
    halves = [over_ctx(own_half, r) for r in (1, 2, 3)]

    by_ctx = [
        lax.dynamic_slice_in_dim(qkv_weight, p * LANES, LANES, 2).reshape(shard, heads).T for p in c_order
    ]
    gain_rows = jnp.concatenate(
        [attn_gain[None], mlp_gain[None], jnp.zeros((EXTRA - 2, shard), attn_gain.dtype)], axis=0
    )
    qkv_own = jnp.concatenate([by_ctx[0], gain_rows], axis=0)
    qkv_rest = jnp.concatenate(by_ctx[1:], axis=0)
    out_own = out_weight
    inner_own = jnp.concatenate([inner_weight[:, 0].T, inner_weight[:, 1].T], axis=0)
    outer_own = outer_weight

    qkv_crossed = across(qkv_own)
    qkv_here = gathered(qkv_own, qkv_crossed)
    out_other = over_tp(out_own)
    (inner_own,) = after([inner_own], qkv_crossed)
    inner_crossed = across(inner_own)

    cosines, sines = zip(*[angle_tables(row_count, p * row_count, HD) for p in c_order])
    cosine, sine = jnp.concatenate(cosines, axis=0), jnp.concatenate(sines, axis=0)
    sign = jnp.where(jnp.arange(HD) < HD // 2, -1.0, 1.0).astype(jnp.float32)
    cosine = jnp.concatenate([cosine[:, 0]] * 2, axis=1)
    sine = jnp.concatenate([sine[:, 0] * sign] * 2, axis=1)

    def project(k, block):
        return local_call(
            functools.partial(project_block, k),
            [low_shape(row_count, width)] + [low_shape(row_count, LANES)] * 3 + [wide_shape(8, width)],
            here,
            [*block, *qkv_here, cosine, sine],
            scratch=[pltpu.VMEM((row_count, width), jnp.bfloat16)],
            flops=2 * row_count * width * heads,
        )

    projected = [project(0, [own_tokens])]
    for k in (1, 2, 3):
        half, qkv_rest = after([halves[k - 1], qkv_rest], *([projected[k - 2][1]] if k > 1 else []))
        if k == 2:
            half, out_other = lax.optimization_barrier((half, out_other))
            out_pair = jnp.concatenate([out_own, out_other], axis=0)
            out_crossed = across(out_pair)
        projected.append(project(k, [half, over_tp(half)]))
    h_parts, queries, keys, values = [[p[i] for p in projected] for i in range(4)]
    gain_all = projected[0][4]

    raw, low, lse = local_call(
        attention_forward,
        [wide_shape(length, LANES), low_shape(length, LANES), wide_shape(8, length)],
        here,
        [*queries, *keys, *values, seg_col, seg_line],
        flops=8 * length * length * LANES,
        transcendentals=2 * length * length,
    )

    def between_ctx(value):
        return lax.all_to_all(value, "ctx", 0, 0, tiled=True)

    inner_crossed, out_crossed = after([inner_crossed, out_crossed], low)
    (outer_own,) = after([outer_own], inner_crossed)
    attended, outer_crossed, *inner_all = lax.optimization_barrier(
        (between_ctx(low), across(outer_own), *gathered(inner_own, inner_crossed))
    )
    attended_other, *weights = lax.optimization_barrier(
        (over_tp(attended), *gathered(out_pair, out_crossed), *gathered(outer_own, outer_crossed))
    )
    out_all, outer_all = weights[:4], weights[4:]

    padded = (units + LANES - 1) // LANES * LANES
    middle, normed_two, second_low, acts = local_call(
        feed_forward,
        [wide_shape(row_count, width)] * 2 + [low_shape(row_count, width), low_shape(3 * row_count, padded)],
        here,
        [attended, attended_other, own_tokens, out_cot, gain_all, *out_all, *inner_all, *outer_all],
    )

    def close(*values):
        return lax.optimization_barrier(values)

    def add(arrays, *steps):
        shapes = []
        for step in steps:
            kind, index = step[0]
            if kind == "rows":
                rows = sum(arrays[i].shape[0] for kind, i in step) // 2
                shapes.append(low_shape(rows, arrays[index].shape[1]))
            else:
                shapes.append(shapes[index] if kind == "out" else low_shape(*arrays[index].shape))
        return pl.pallas_call(
            functools.partial(add_arrays, steps),
            name="add_arrays",
            out_shape=tuple(shapes),
            compiler_params=pltpu.CompilerParams(vmem_limit_bytes=WIDE_VMEM),
            cost_estimate=pl.CostEstimate(flops=0, bytes_accessed=0, transcendentals=0),
        )(*arrays)

    def add_pairs(*pairs):
        flat = [array for pair in pairs for array in pair]
        return add(flat, *[(("in", 2 * i), ("in", 2 * i + 1)) for i in range(len(pairs))])

    def inwards(value):
        return lax.ppermute(value, "ctx", [(0, 1), (3, 2)])

    def across_middle(value):
        return lax.ppermute(value, "ctx", [(1, 2), (2, 1)])

    def outwards(value):
        return lax.ppermute(value, "ctx", [(1, 0), (2, 3)])

    at_end = jnp.logical_or(c == 0, c == 3)

    second_part, gain_two_part = local_call(
        feed_forward_back,
        [low_shape(row_count, width), wide_shape(1, width)],
        here,
        [acts, normed_two, *inner_all],
    )
    acts_other, second_low_other, cot_other, attended_beside, second_part, gain_two_part = close(
        beside(acts), beside(second_low), beside(out_cot), beside(attended), second_part, gain_two_part
    )

    early = units // (4 * LANES) * LANES * 2
    mlp_grads = local_call(
        mlp_gradients,
        [low_shape(rows, shard) for rows in (units, units, units + early, units + early, units - early, units - early)],
        here,
        [acts, acts_other, second_low, second_low_other, out_cot, cot_other],
        flops=2 * 3 * row_count * width * units,
    )
    (mlp_part,) = local_call(feed_forward_out, [low_shape(row_count, width)], here, [acts, *outer_all])
    second_other, rest_crossed, mlp_part, gain_two_other, *mlp_grads = close(
        over_tp(second_part), across(qkv_rest), mlp_part, beside(gain_two_part), *mlp_grads
    )
    outer_keep, outer_cross, gate_keep, gate_cross, up_keep, up_cross = mlp_grads

    attn_low, head_grads = local_call(
        head_gradients,
        [low_shape(row_count, width), low_shape(length, LANES)],
        here,
        [second_part, second_other, middle, out_cot, gain_all, *out_all],
        flops=row_count * width * width,
    )
    head_grads, outer_x, attn_other, mlp_other, *rest_all = close(
        between_ctx(head_grads), across(outer_cross), beside(attn_low), over_tp(mlp_part),
        *gathered(qkv_rest, rest_crossed),
    )

    (outer_a,) = add_pairs((outer_keep, outer_x))
    (projected_grads,) = local_call(
        attention_backward,
        [low_shape(length, heads)],
        here,
        [*queries, *keys, *values, head_grads, raw, lse, cosine, sine, seg_col, seg_line],
        scratch=[pltpu.VMEM((LANES, length), jnp.float32)],
        flops=20 * length * length * LANES,
        transcendentals=2 * length * length,
    )
    out_keep, out_cross = local_call(
        out_gradients,
        [low_shape(4 * LANES + EXTRA, shard)] * 2,
        here,
        [attended, attended_beside, attn_low, attn_other, gain_two_part, gain_two_other],
        flops=2 * row_count * width * 4 * LANES,
    )
    outer_in, gate_x, projected_grads, out_keep, out_cross = close(
        inwards(outer_a), across(gate_cross), projected_grads, out_keep, out_cross
    )

    gate_a, outer_b = add_pairs((gate_keep, gate_x), (outer_a, outer_in))
    qkv_parts = local_call(
        qkv_gradients,
        [low_shape(2, heads + EXTRA, shard)] + [low_shape(heads + EXTRA, shard)] * 2,
        here,
        [projected_grads, *h_parts, *qkv_here, gain_all],
        flops=2 * length * width * heads,
    )
    first_in, up_x, out_x, gate_in, outer_mid, *qkv_parts = close(
        between_ctx(projected_grads), across(up_cross), across(out_cross), inwards(gate_a), across_middle(outer_b),
        *qkv_parts,
    )

    qkv_sent, qkv_keep, qkv_keep_across = qkv_parts
    up_a, gate_b, outer_c = add(
        [up_keep, up_x, out_keep, out_x, gate_a, gate_in, outer_b, outer_mid],
        (("rows", 0), ("rows", 1), ("rows", 2), ("rows", 3)),
        (("in", 4), ("in", 5)),
        (("in", 6), ("in", 7)),
    )
    (first_low_part,) = local_call(
        first_gradients,
        [low_shape(row_count, width)],
        here,
        [first_in, *qkv_here, *rest_all],
        flops=2 * row_count * width * 4 * heads,
    )
    up_in, outer_out, gate_mid, qkv_received, first_low_part = close(
        inwards(up_a), outwards(outer_c), across_middle(gate_b), beside(qkv_sent), first_low_part
    )

    up_b, gate_c = add_pairs((up_a, up_in), (gate_b, gate_mid))
    qkv_cross = qkv_keep_across + qkv_received[1]
    outer_grad = jnp.where(at_end, outer_out, outer_c).astype(jnp.float32)
    first_other, up_mid, gate_out, qkv_x, outer_grad = close(
        over_tp(first_low_part), across_middle(up_b), outwards(gate_c), across(qkv_cross), outer_grad
    )

    (up_c,) = add_pairs((up_b, up_mid))
    qkv_sum = lax.optimization_barrier(
        (qkv_keep.astype(jnp.float32) + qkv_received[0].astype(jnp.float32) + qkv_x.astype(jnp.float32)).astype(
            jnp.bfloat16
        )
    )
    (input_grad,) = local_call(
        input_gradients,
        [wide_shape(row_count, width)],
        here,
        [first_low_part, first_other, own_tokens, gain_all, attn_low],
    )
    gate_sum = jnp.where(at_end, gate_out, gate_c)
    block_out = (
        middle + (mlp_part.astype(jnp.float32) + mlp_other.astype(jnp.float32))
    ).astype(jnp.bfloat16)
    up_out, input_grad, gate_sum, block_out, *qkv_sums = close(
        outwards(up_c), input_grad, gate_sum, block_out, *[over_ctx(qkv_sum, k) for k in (1, 2, 3)]
    )
    qkv_sums = [qkv_sum, *qkv_sums]
    up_sum = jnp.where(at_end, up_out, up_c)
    late = units - early
    out_grad = up_sum[late : late + 4 * LANES].astype(jnp.float32)

    (qkv_grad,) = local_call(qkv_layout, [wide_shape(3, shard, 4 * LANES)], here, qkv_sums)
    gain_lines = [part[heads].astype(jnp.float32) for part in qkv_sums]
    up_grad = jnp.concatenate([gate_sum[units:], up_sum[:late]], axis=0)
    gain_grads = jnp.stack(
        [(gain_lines[0] + gain_lines[1]) + (gain_lines[2] + gain_lines[3]), up_sum[late + 4 * LANES].astype(jnp.float32)]
    )
    gain_grads = gain_grads + over_tp(gain_grads)

    return (
        block_out[None],
        input_grad[None],
        gain_grads[0],
        qkv_grad.transpose(1, 0, 2),
        out_grad,
        gain_grads[1],
        jnp.stack([gate_sum[:units].T, up_grad.T], axis=1).astype(jnp.float32),
        outer_grad,
    )


def solution(mesh):
    placed = (
        P("fsdp", "ctx", None),
        P("fsdp", None),
        P("fsdp"),
        P("fsdp", None, "tp"),
        P("tp", "fsdp"),
        P("fsdp"),
        P("fsdp", None, "tp"),
        P("tp", "fsdp"),
        P("fsdp", "ctx", None),
    )
    sizes = dict(mesh.shape)

    def layer(*args):
        tokens, segments, qkv_weight = args[0], args[1], args[3]
        heads_apart = qkv_weight.shape[2] == 4 * LANES
        short = segments.shape[1] == 4 * tokens.shape[1] and segments.shape[1] <= 1024
        small = (sizes["fsdp"], sizes["ctx"], sizes["tp"]) == (4, 4, 2)
        if small and short and heads_apart and tokens.shape[0] == 1:
            return short_sequences(*args)
        return per_device(*args)

    return jax.shard_map(
        layer,
        mesh=mesh,
        in_specs=placed,
        out_specs=(
            P("fsdp", "ctx", None),
            P("fsdp", "ctx", None),
            P("fsdp"),
            P("fsdp", None, "tp"),
            P("tp", "fsdp"),
            P("fsdp"),
            P("fsdp", None, "tp"),
            P("tp", "fsdp"),
        ),
        check_vma=False,
    )
```

```python
import functools
import math

import jax
import jax.numpy as jnp
from jax import lax
from jax.experimental import pallas as pl
from jax.experimental.pallas import tpu as pltpu
from jax.sharding import PartitionSpec as P

HD = 64


EPSILON = 1e-05
ROPE_BASE = 160000.0
MASKED = -1e30


def normalize(values, gain_row):
    row_mean = jnp.mean(values, axis=-1, keepdims=True)
    centered = values - row_mean
    spread = jnp.mean(centered * centered, axis=-1, keepdims=True)
    return centered * lax.rsqrt(spread + EPSILON) * gain_row


def geglu(gate_in, upper):
    return jax.nn.gelu(gate_in, approximate=False) * upper


def angle_tables(row_count, offset, depth):
    half_width = depth // 2
    inverse = jnp.power(
        jnp.float32(ROPE_BASE), -(2.0 * jnp.arange(half_width, dtype=jnp.float32)) / depth
    )
    places = (offset + jnp.arange(row_count, dtype=jnp.int32)).astype(jnp.float32)
    angles = places[:, None] * inverse[None, :]
    angles = jnp.concatenate([angles, angles], axis=-1)
    return (jnp.cos(angles)[:, None, :], jnp.sin(angles)[:, None, :])


def rotate(values, cosine, sine):
    half_width = values.shape[-1] // 2
    turned = jnp.concatenate([-values[..., half_width:], values[..., :half_width]], axis=-1)
    return values * cosine + turned * sine


def rotate_back(grad_in, cosine, sine):
    half_width = grad_in.shape[-1] // 2
    scaled = grad_in * sine
    turned = jnp.concatenate([scaled[..., half_width:], -scaled[..., :half_width]], axis=-1)
    return grad_in * cosine + turned


def attend_forward(queries, query_seg, seg_row, key_low, value_low, score_scale):
    row_count, heads_here, depth = queries.shape
    initial = (
        jnp.full((heads_here, row_count), MASKED, jnp.float32),
        jnp.zeros((heads_here, row_count), jnp.float32),
        jnp.zeros((row_count, heads_here, depth), jnp.float32),
    )
    key_piece = lax.all_gather(key_low, "ctx", axis=0, tiled=True)
    value_piece = lax.all_gather(value_low, "ctx", axis=0, tiled=True)
    piece_rows = key_piece.shape[0]
    block_size = math.gcd(piece_rows, 512)
    blocks = (
        key_piece.reshape(piece_rows // block_size, block_size, heads_here, depth),
        value_piece.reshape(piece_rows // block_size, block_size, heads_here, depth),
        seg_row.reshape(piece_rows // block_size, block_size),
    )

    def step(state, block_data):
        running_peak, running_total, accum = state
        key_block, value_block, block_seg = block_data
        scores = jnp.einsum("qhe,khe->hqk", queries, key_block, preferred_element_type=jnp.float32)
        same_doc = (query_seg[:, None] == block_seg[None, :])[None]
        logits = jnp.where(same_doc, scores * score_scale, MASKED)
        new_peak = jnp.maximum(running_peak, jnp.max(logits, axis=-1))
        rescale = jnp.exp(running_peak - new_peak)
        weights = jnp.where(same_doc, jnp.exp(logits - new_peak[:, :, None]), 0.0)
        running_total = running_total * rescale + jnp.sum(weights, axis=-1)
        mixed_out = jnp.einsum(
            "hqk,khe->qhe",
            weights.astype(jnp.bfloat16),
            value_block,
            preferred_element_type=jnp.float32,
        )
        accum = accum * rescale.T[:, :, None] + mixed_out
        return ((new_peak, running_total, accum), None)

    result, unused = lax.scan(step, initial, blocks)
    running_peak, running_total, accum = result
    return (accum / running_total.T[:, :, None], running_peak + jnp.log(running_total))


def probs_and_grads(
    query_block, key_block, grad_block, value_block, same_doc, log_total, delta_rows, score_scale
):
    scores = jnp.einsum("qhe,khe->hqk", query_block, key_block, preferred_element_type=jnp.float32)
    probs = jnp.where(same_doc, jnp.exp(scores * score_scale - log_total[:, :, None]), 0.0)
    prob_grad = jnp.einsum(
        "qhe,khe->hqk", grad_block, value_block, preferred_element_type=jnp.float32
    )
    score_grad = (probs * (prob_grad - delta_rows[:, :, None]) * score_scale).astype(jnp.bfloat16)
    return (probs.astype(jnp.bfloat16), score_grad)


def attend_backward(
    queries, key_low, value_low, grad_low, log_total, delta_rows, query_seg, seg_row, score_scale
):
    row_count, heads_here, depth = queries.shape
    seq_length = seg_row.shape[0]
    block_size = math.gcd(seq_length, 512)
    block_count = seq_length // block_size
    key_all, value_all = (
        lax.all_gather(key_low, "ctx", axis=0, tiled=True),
        lax.all_gather(value_low, "ctx", axis=0, tiled=True),
    )
    blocks = (
        key_all.reshape(block_count, block_size, heads_here, depth),
        value_all.reshape(block_count, block_size, heads_here, depth),
        seg_row.reshape(block_count, block_size),
    )

    def key_step(query_acc, block_data):
        key_block, value_block, block_seg = block_data
        same_doc = (query_seg[:, None] == block_seg[None, :])[None]
        prob_low, score_grad = probs_and_grads(
            queries, key_block, grad_low, value_block, same_doc, log_total, delta_rows, score_scale
        )
        query_acc = query_acc + jnp.einsum(
            "hqk,khe->qhe", score_grad, key_block, preferred_element_type=jnp.float32
        )
        key_part = jnp.einsum(
            "hqk,qhe->khe", score_grad, queries, preferred_element_type=jnp.float32
        )
        value_part = jnp.einsum(
            "hqk,qhe->khe", prob_low, grad_low, preferred_element_type=jnp.float32
        )
        return (query_acc, (key_part, value_part))

    query_grad, key_value_parts = lax.scan(
        key_step, jnp.zeros((row_count, heads_here, depth), jnp.float32), blocks
    )
    key_parts = key_value_parts[0].reshape(seq_length, heads_here * depth)
    value_parts = key_value_parts[1].reshape(seq_length, heads_here * depth)
    key_grad, value_grad = (
        lax.psum_scatter(
            key_parts.astype(jnp.bfloat16), "ctx", scatter_dimension=0, tiled=True
        ).astype(jnp.float32),
        lax.psum_scatter(
            value_parts.astype(jnp.bfloat16), "ctx", scatter_dimension=0, tiled=True
        ).astype(jnp.float32),
    )
    key_grad = key_grad.reshape(row_count, heads_here, depth)
    value_grad = value_grad.reshape(row_count, heads_here, depth)
    return (query_grad, key_grad, value_grad)


def per_device(
    tokens,
    segments,
    attn_gain,
    qkv_weight,
    out_weight,
    mlp_gain,
    inner_weight,
    outer_weight,
    cotangent,
):
    qkv_full, out_full, gain_one = (
        lax.all_gather(qkv_weight, "fsdp", axis=0, tiled=True),
        lax.all_gather(out_weight, "fsdp", axis=1, tiled=True),
        lax.all_gather(attn_gain, "fsdp", axis=0, tiled=True),
    )
    inner_full, outer_full, gain_two = (
        lax.all_gather(inner_weight, "fsdp", axis=0, tiled=True),
        lax.all_gather(outer_weight, "fsdp", axis=1, tiled=True),
        lax.all_gather(mlp_gain, "fsdp", axis=0, tiled=True),
    )
    seq_count, row_count, model_width = tokens.shape
    local_width = qkv_full.shape[2]
    heads_here = local_width // HD
    score_scale = HD ** (-0.5)
    offset = lax.axis_index("ctx") * row_count
    cosine, sine = angle_tables(row_count, offset, HD)
    input_rows = tokens.reshape(-1, model_width).astype(jnp.float32)
    normed_one, norm_one_back = jax.vjp(normalize, input_rows, gain_one.astype(jnp.float32))
    first_low = normed_one.astype(jnp.bfloat16)
    projected_output = jnp.einsum(
        "td,dcf->tcf", first_low, qkv_full, preferred_element_type=jnp.float32
    )
    projected_output = projected_output.reshape(seq_count, row_count, 3, heads_here, HD)
    query_low = rotate(projected_output[:, :, 0], cosine, sine).astype(jnp.bfloat16)
    key_low = rotate(projected_output[:, :, 1], cosine, sine).astype(jnp.bfloat16)
    value_low = projected_output[:, :, 2].astype(jnp.bfloat16)
    seq_index = 0
    seg_row = segments[seq_index]
    query_seg = lax.dynamic_slice_in_dim(seg_row, offset, row_count)
    raw_out, log_total = attend_forward(
        query_low[seq_index],
        query_seg,
        seg_row,
        key_low[seq_index],
        value_low[seq_index],
        score_scale,
    )
    query_segs = [query_seg]
    raw_outs = [raw_out]
    log_totals = [log_total]
    attended_low = jnp.stack(raw_outs).astype(jnp.bfloat16).reshape(-1, local_width)
    attn_part = jnp.dot(attended_low, out_full, preferred_element_type=jnp.float32)
    middle_activation = input_rows + lax.psum(attn_part.astype(jnp.bfloat16), "tp").astype(
        jnp.float32
    )
    normed_two, norm_two_back = jax.vjp(normalize, middle_activation, gain_two.astype(jnp.float32))
    second_low = normed_two.astype(jnp.bfloat16)
    hidden_input = jnp.einsum(
        "td,dcf->tcf", second_low, inner_full, preferred_element_type=jnp.float32
    )
    hidden_state, geglu_back = jax.vjp(geglu, hidden_input[:, 0], hidden_input[:, 1])
    hidden_low = hidden_state.astype(jnp.bfloat16)
    mlp_part = jnp.dot(hidden_low, outer_full, preferred_element_type=jnp.float32)
    block_out = (
        middle_activation + lax.psum(mlp_part.astype(jnp.bfloat16), "tp").astype(jnp.float32)
    ).astype(jnp.bfloat16)
    out_cot = cotangent.reshape(-1, model_width)
    outer_local = jnp.einsum("tf,td->fd", hidden_low, out_cot, preferred_element_type=jnp.float32)
    hidden_grad = jnp.einsum("td,fd->tf", out_cot, outer_full, preferred_element_type=jnp.float32)
    gate_grad, up_grad = geglu_back(hidden_grad)
    inner_low = jnp.stack([gate_grad, up_grad], axis=1).astype(jnp.bfloat16)
    inner_local = jnp.einsum(
        "td,tcf->dcf", second_low, inner_low, preferred_element_type=jnp.float32
    )
    normed_two_grad = lax.psum(
        jnp.einsum("tcf,dcf->td", inner_low, inner_full, preferred_element_type=jnp.float32).astype(
            jnp.bfloat16
        ),
        "tp",
    ).astype(jnp.float32)
    middle_part, gain_two_grad = norm_two_back(normed_two_grad)
    middle_grad = out_cot.astype(jnp.float32) + middle_part
    attn_low = middle_grad.astype(jnp.bfloat16)
    out_local = jnp.einsum("tf,td->fd", attended_low, attn_low, preferred_element_type=jnp.float32)
    attended_grad = jnp.einsum("td,fd->tf", attn_low, out_full, preferred_element_type=jnp.float32)
    attended_grad = attended_grad.astype(jnp.bfloat16).reshape(seq_count, row_count, heads_here, HD)
    seq_index = 0
    grad_low = attended_grad[seq_index]
    delta_rows = jnp.sum(grad_low.astype(jnp.float32) * raw_outs[seq_index], axis=-1).T
    query_grad, key_grad, value_grad = attend_backward(
        query_low[seq_index],
        key_low[seq_index],
        value_low[seq_index],
        grad_low,
        log_totals[seq_index],
        delta_rows,
        query_segs[seq_index],
        segments[seq_index],
        score_scale,
    )
    stacked = jnp.stack(
        [rotate_back(query_grad, cosine, sine), rotate_back(key_grad, cosine, sine), value_grad],
        axis=1,
    )
    qkv_grads = stacked.reshape(row_count, 3, local_width)
    qkv_low = qkv_grads.astype(jnp.bfloat16)
    qkv_local = jnp.einsum("td,tcf->dcf", first_low, qkv_low, preferred_element_type=jnp.float32)
    normed_one_grad = lax.psum(
        jnp.einsum("tcf,dcf->td", qkv_low, qkv_full, preferred_element_type=jnp.float32).astype(
            jnp.bfloat16
        ),
        "tp",
    ).astype(jnp.float32)
    input_part, gain_one_grad = norm_one_back(normed_one_grad)
    input_grad = (middle_grad + input_part).reshape(tokens.shape)
    summed = (
        lax.psum_scatter(gain_one_grad, ("fsdp", "ctx"), scatter_dimension=0, tiled=True),
        lax.psum_scatter(qkv_local, ("fsdp", "ctx"), scatter_dimension=0, tiled=True),
        lax.psum_scatter(out_local, ("fsdp", "ctx"), scatter_dimension=1, tiled=True),
        lax.psum_scatter(gain_two_grad, ("fsdp", "ctx"), scatter_dimension=0, tiled=True),
        lax.psum_scatter(inner_local, ("fsdp", "ctx"), scatter_dimension=0, tiled=True),
        lax.psum_scatter(outer_local, ("fsdp", "ctx"), scatter_dimension=1, tiled=True),
    )
    gain_one_sum, qkv_sum, out_sum, gain_two_sum, inner_sum, outer_sum = summed
    shards = (
        lax.all_gather(gain_one_sum.astype(jnp.bfloat16), "ctx", axis=0, tiled=True).astype(
            gain_one_sum.dtype
        ),
        lax.all_gather(qkv_sum.astype(jnp.bfloat16), "ctx", axis=0, tiled=True).astype(
            qkv_sum.dtype
        ),
        lax.all_gather(out_sum.astype(jnp.bfloat16), "ctx", axis=1, tiled=True).astype(
            out_sum.dtype
        ),
        lax.all_gather(gain_two_sum.astype(jnp.bfloat16), "ctx", axis=0, tiled=True).astype(
            gain_two_sum.dtype
        ),
        lax.all_gather(inner_sum.astype(jnp.bfloat16), "ctx", axis=0, tiled=True).astype(
            inner_sum.dtype
        ),
        lax.all_gather(outer_sum.astype(jnp.bfloat16), "ctx", axis=1, tiled=True).astype(
            outer_sum.dtype
        ),
    )
    return (
        block_out.reshape(tokens.shape),
        input_grad,
        shards[0],
        shards[1],
        shards[2],
        shards[3],
        shards[4],
        shards[5],
    )


LANES = 128
BLOCK = 256
EXTRA = 32
COST = 0.0
WIDE_VMEM = 62 * 1024 * 1024


def hop(value, axis, bit, count):
    return lax.ppermute(value, axis, [(i, i ^ bit) for i in range(count)])


def after(values, *earlier):
    values = list(values)
    return list(lax.optimization_barrier(tuple(values) + earlier))[: len(values)]


def lane_half(shape):
    return lax.broadcasted_iota(jnp.int32, shape, 1) < HD


def swap_halves(values):
    lane = lax.broadcasted_iota(jnp.int32, values.shape, 1)
    low_part = lax.rem(lane, HD) < HD // 2
    return jnp.where(
        low_part,
        pltpu.roll(values, LANES - HD // 2, 1),
        pltpu.roll(values, HD // 2, 1),
    )


def dot_nt(left, right):
    return lax.dot_general(left, right, (((1,), (1,)), ((), ())), preferred_element_type=jnp.float32)


def dot_nn(left, right):
    return lax.dot_general(left, right, (((1,), (0,)), ((), ())), preferred_element_type=jnp.float32)


def dot_tn(left, right):
    return lax.dot_general(left, right, (((0,), (0,)), ((), ())), preferred_element_type=jnp.float32)


def one_head(values, head):
    first = lane_half(values.shape)
    keep = first if head == 0 else jnp.logical_not(first)
    return jnp.where(keep, values, jnp.zeros_like(values))


def part_of(index, size):
    return pl.ds(pl.multiple_of(index * size, size), size)


def standardize(values):
    row_mean = jnp.mean(values, axis=-1, keepdims=True)
    centered = values - row_mean
    spread = jnp.mean(centered * centered, axis=-1, keepdims=True)
    scale = lax.rsqrt(spread + EPSILON)
    return centered * scale, scale


def standardize_back(normed, scale, grad):
    inner = jnp.mean(grad * normed, axis=-1, keepdims=True)
    return scale * (grad - jnp.mean(grad, axis=-1, keepdims=True) - normed * inner)


def local_call(body, outs, places, operands, scratch=(), flops=0, transcendentals=0):
    moved = sum(math.prod(o.shape) * o.dtype.itemsize for o in list(operands) + list(outs))
    return pl.pallas_call(
        body,
        name=body.__name__ if hasattr(body, "__name__") else body.func.__name__,
        out_shape=tuple(outs),
        in_specs=[pl.BlockSpec(memory_space=pltpu.SMEM)]
        + [pl.BlockSpec(memory_space=pltpu.VMEM)] * len(operands),
        out_specs=tuple([pl.BlockSpec(memory_space=pltpu.VMEM)] * len(outs)),
        scratch_shapes=list(scratch),
        compiler_params=pltpu.CompilerParams(vmem_limit_bytes=WIDE_VMEM),
        cost_estimate=pl.CostEstimate(
            flops=int(flops * COST), bytes_accessed=int(moved * COST), transcendentals=int(transcendentals * COST)
        ),
    )(places, *operands)


def low_shape(*shape):
    return jax.ShapeDtypeStruct(shape, jnp.bfloat16)


def wide_shape(*shape):
    return jax.ShapeDtypeStruct(shape, jnp.float32)


def project_block(block, at, *refs):
    f, t = at[0], at[2]
    count = len(refs) - 12
    tokens_in, (w0, w1, w2, w3, cos_ref, sin_ref) = refs[:count], refs[count : count + 6]
    h_ref, q_ref, k_ref, v_ref, gain_ref, x_ref = refs[count + 6 :]
    weights = (w0, w1, w2, w3)
    columns = [part_of(f ^ r, w0.shape[1]) for r in range(4)]
    heads = 3 * LANES
    for r, weight in enumerate(weights):
        gain_ref[:, columns[r]] = weight[heads : heads + EXTRA, :].astype(jnp.float32)[:8, :]
    if count == 1:
        tokens = tokens_in[0][...]
    else:
        half = tokens_in[0].shape[0]
        x_ref[part_of(t, half), :] = tokens_in[0][...]
        x_ref[part_of(1 - t, half), :] = tokens_in[1][...]
        tokens = x_ref[...]
    h_ref[...] = (standardize(tokens.astype(jnp.float32))[0] * gain_ref[0:1, :]).astype(jnp.bfloat16)
    projected = 0.0
    for r, weight in enumerate(weights):
        projected += dot_nt(h_ref[:, columns[r]], weight[:heads, :])
    rows = slice(block * tokens.shape[0], (block + 1) * tokens.shape[0])
    cosine, sine = cos_ref[rows, :], sin_ref[rows, :]
    for ref, part in ((q_ref, projected[:, :LANES]), (k_ref, projected[:, LANES : 2 * LANES])):
        ref[...] = (part * cosine + swap_halves(part) * sine).astype(jnp.bfloat16)
    v_ref[...] = projected[:, 2 * LANES :].astype(jnp.bfloat16)


def joined(refs):
    return jnp.concatenate([ref[...] for ref in refs], axis=0)


def attention_forward(at, *refs):
    c = at[1]
    query_refs, key_refs, value_refs, seg_col, seg_line = refs[:4], refs[4:8], refs[8:12], refs[12], refs[13]
    raw_ref, low_ref, lse_ref = refs[14:]
    rows_here = query_refs[0].shape[0]
    keys, values = joined(key_refs), joined(value_refs)
    for k in range(4):
        rows = slice(k * rows_here, (k + 1) * rows_here)
        queries = query_refs[k][...] * jnp.bfloat16(HD ** (-0.5))
        same = seg_col[rows, :] == seg_line[...]
        outs, logs = [], []
        for head in range(2):
            scores = dot_nt(one_head(queries, head), keys)
            scores = jnp.where(same, scores, MASKED)
            peak = jnp.max(scores, axis=1, keepdims=True)
            weights = jnp.exp(scores - peak)
            total = jnp.sum(weights, axis=1, keepdims=True)
            probs = (weights * (1.0 / total)).astype(jnp.bfloat16)
            outs.append(dot_nn(probs, values))
            logs.append(peak + jnp.log(total))
        raw = jnp.where(lane_half(outs[0].shape), outs[0], outs[1])
        raw_ref[rows, :] = raw
        for b in range(2):
            low_ref[part_of((c ^ k) * 2 + b, rows_here), :] = raw.astype(jnp.bfloat16)
        lane = lax.broadcasted_iota(jnp.int32, (rows_here, LANES), 1)
        lse_ref[:, rows] = jnp.where(lane == 0, logs[0], logs[1]).T[:8, :]


def attention_backward(
    at, q0, q1, q2, q3, k0, k1, k2, k3, v0, v1, v2, v3, do_ref, raw_ref, lse_ref, cos_ref, sin_ref,
    seg_col, seg_line, out_ref, turned_ref,
):
    c = at[1]
    rows_here = q0.shape[0]
    grads = jnp.concatenate([do_ref[part_of(c ^ k, rows_here), :] for k in range(4)], axis=0)
    product = grads.astype(jnp.float32) * raw_ref[...]
    first = lane_half(product.shape)
    whole = jnp.sum(jnp.where(first, product, 0.0), axis=1, keepdims=True)
    other = jnp.sum(jnp.where(first, 0.0, product), axis=1, keepdims=True)
    lane = lax.broadcasted_iota(jnp.int32, product.shape, 1)
    delta = jnp.where(lane == 0, whole, other).T
    scale = HD ** (-0.5)
    queries = joined((q0, q1, q2, q3))
    scaled = queries * jnp.bfloat16(scale)
    for k in range(4):
        rows, place = slice(k * rows_here, (k + 1) * rows_here), part_of(c ^ k, rows_here)
        keys, values = (k0, k1, k2, k3)[k][...], (v0, v1, v2, v3)[k][...]
        keys_turned = keys.T
        same = seg_col[rows, :] == seg_line[...]
        key_parts, value_parts = [], []
        for head in range(2):
            scores = dot_nt(one_head(keys, head), scaled)
            probs = jnp.where(same, jnp.exp(scores - lse_ref[head : head + 1, :]), 0.0)
            prob_grad = dot_nt(one_head(values, head), grads)
            score_grad = (probs * (prob_grad - delta[head : head + 1, :]) * scale).astype(jnp.bfloat16)
            value_parts.append(dot_nn(probs.astype(jnp.bfloat16), grads))
            key_parts.append(dot_nn(score_grad, queries))
            here = slice(head * HD, (head + 1) * HD)
            part = dot_nn(keys_turned[here, :], score_grad)
            if k == 0:
                turned_ref[here, :] = part
            else:
                turned_ref[here, :] += part
        half = lane_half(key_parts[0].shape)
        key_grad = jnp.where(half, key_parts[0], key_parts[1])
        value_grad = jnp.where(half, value_parts[0], value_parts[1])
        key_grad = key_grad * cos_ref[rows, :] - swap_halves(key_grad) * sin_ref[rows, :]
        out_ref[place, LANES : 2 * LANES] = key_grad.astype(jnp.bfloat16)
        out_ref[place, 2 * LANES :] = value_grad.astype(jnp.bfloat16)
    for k in range(4):
        rows, place = slice(k * rows_here, (k + 1) * rows_here), part_of(c ^ k, rows_here)
        query_grad = turned_ref[:, rows].T
        query_grad = query_grad * cos_ref[rows, :] - swap_halves(query_grad) * sin_ref[rows, :]
        out_ref[place, :LANES] = query_grad.astype(jnp.bfloat16)


def attended_heads(ref, rows_here, sides):
    return jnp.concatenate([ref[part_of(k * 2 + b, rows_here), :] for b in sides for k in range(4)], axis=1)


def feed_forward(
    at, attended_ref, x_ref, cot_ref, gain_ref,
    o0, o1, o2, o3, inner0, inner1, inner2, inner3, outer0, outer1, outer2, outer3,
    mid_ref, normed_ref, second_ref, acts_ref,
):
    f, t = at[0], at[2]
    rows_here = x_ref.shape[0]
    attended = attended_heads(attended_ref, rows_here, (t, 1 - t))
    inners, outers = (inner0, inner1, inner2, inner3), (outer0, outer1, outer2, outer3)
    columns = [part_of(f ^ r, o0.shape[1]) for r in range(4)]
    for r, weight in enumerate((o0, o1, o2, o3)):
        mid_ref[:, columns[r]] = x_ref[:, columns[r]].astype(jnp.float32) + dot_nn(attended, weight[...])
    normed = standardize(mid_ref[...])[0]
    normed_ref[...] = normed
    second_ref[...] = (normed * gain_ref[1:2, :]).astype(jnp.bfloat16)
    units = outer0.shape[0]
    for start in range(0, units, BLOCK):
        stop = min(start + BLOCK, units)
        gate, up, hid_grad = 0.0, 0.0, 0.0
        for r in range(4):
            rows = second_ref[:, columns[r]]
            gate += dot_nt(rows, inners[r][start:stop, :])
            up += dot_nt(rows, inners[r][units + start : units + stop, :])
            hid_grad += dot_nt(cot_ref[:, columns[r]], outers[r][start:stop, :])
        below = 0.5 + 0.5 * lax.erf(gate * (2.0 ** -0.5))
        density = jnp.exp(-0.5 * gate * gate) * ((2.0 * math.pi) ** -0.5)
        active = gate * below
        acts_ref[:rows_here, start:stop] = (active * up).astype(jnp.bfloat16)
        acts_ref[rows_here : 2 * rows_here, start:stop] = (
            hid_grad * up * (below + gate * density)
        ).astype(jnp.bfloat16)
        acts_ref[2 * rows_here :, start:stop] = (hid_grad * active).astype(jnp.bfloat16)


def feed_forward_back(
    at, acts_ref, normed_ref, inner0, inner1, inner2, inner3, mine_ref, other_ref, gain_grad_ref, low_ref
):
    f, t = at[0], at[2]
    rows_here = normed_ref.shape[0]
    units = inner0.shape[0] // 2
    gate_grad = acts_ref[rows_here : 2 * rows_here, :units]
    up_grad = acts_ref[2 * rows_here :, :units]
    for r, inner in enumerate((inner0, inner1, inner2, inner3)):
        columns = part_of(f ^ r, inner.shape[1])
        part = dot_nn(gate_grad, inner[:units, :]) + dot_nn(up_grad, inner[units:, :])
        low_ref[:, columns] = part.astype(jnp.bfloat16)
        gain_grad_ref[:, columns] = jnp.sum(part * normed_ref[:, columns], axis=0, keepdims=True)
    half = mine_ref.shape[0]
    mine_ref[...] = low_ref[part_of(t, half), :]
    other_ref[...] = low_ref[part_of(1 - t, half), :]


def feed_forward_out(at, acts_ref, outer0, outer1, outer2, outer3, out_ref):
    f = at[0]
    hidden = acts_ref[: out_ref.shape[0], : outer0.shape[0]]
    for r, weight in enumerate((outer0, outer1, outer2, outer3)):
        out_ref[:, part_of(f ^ r, weight.shape[1])] = dot_nn(hidden, weight[...]).astype(jnp.bfloat16)


def head_gradients(
    at, mine_ref, other_ref, mid_ref, cot_ref, gain_ref, o0, o1, o2, o3, da_ref, out_ref
):
    f, t = at[0], at[2]
    rows = part_of(t, da_ref.shape[0])
    grad = (mine_ref[...].astype(jnp.float32) + other_ref[...].astype(jnp.float32)) * gain_ref[1:2, :]
    normed, scale = standardize(mid_ref[rows, :])
    mid_grad = cot_ref[rows, :].astype(jnp.float32) + standardize_back(normed, scale, grad)
    da_ref[...] = mid_grad.astype(jnp.bfloat16)
    total = 0.0
    for r, weight in enumerate((o0, o1, o2, o3)):
        total += dot_nt(da_ref[:, part_of(f ^ r, weight.shape[1])], weight[...])
    for b in range(2):
        for k in range(4):
            at_part = (b * 4 + k) * LANES
            out_ref[part_of(k * 2 + (t ^ b), da_ref.shape[0]), :] = total[:, at_part : at_part + LANES].astype(
                jnp.bfloat16
            )


def store_piece(r, value, send_ref, keep_ref, keep_across_ref, rows=slice(None)):
    if r in (1, 3):
        send_ref[r // 2, rows, :] = value
    else:
        (keep_ref if r == 0 else keep_across_ref)[rows, :] = value


def extra_rows(row):
    lines = lax.broadcasted_iota(jnp.int32, (EXTRA, row.shape[1]), 0)
    return jnp.where(lines == 0, row, 0.0).astype(jnp.bfloat16)


def joined_sums(
    at, up_keep, up_x, out_keep, out_x, outer_ref, outer_arrived, joined_ref, outer_sum, payload_ref
):
    c = at[1]
    rows, units = up_keep.shape[0], outer_ref.shape[0]
    joined_ref[:rows, :] = up_keep[...] + up_x[...]
    joined_ref[rows:, :] = out_keep[...] + out_x[...]
    outer_sum[...] = outer_ref[...] + outer_arrived[...]
    at_end = jnp.logical_or(c == 0, c == 3)

    @pl.when(at_end)
    def _():
        payload_ref[...] = joined_ref[...]

    @pl.when(jnp.logical_not(at_end))
    def _():
        payload_ref[:units, :] = outer_sum[...]
        payload_ref[units:, :] = jnp.zeros_like(payload_ref[units:, :])


def pair_columns(f, shard):
    return part_of(f, shard), part_of(f ^ 2, shard)


def mlp_gradients(
    at, own_ref, other_ref, second_ref, second_other, cot_ref, cot_other,
    outer_keep, outer_cross, gate_keep, gate_cross, up_keep, up_cross,
):
    f = at[0]
    units, shard = outer_keep.shape
    tokens = cot_ref.shape[0]
    early = gate_keep.shape[0] - units
    parts = (
        (0, 0, units, cot_ref, cot_other, outer_keep, outer_cross, 0),
        (1, 0, units, second_ref, second_other, gate_keep, gate_cross, 0),
        (2, 0, early, second_ref, second_other, gate_keep, gate_cross, units),
        (2, early, units, second_ref, second_other, up_keep, up_cross, 0),
    )
    for i, start, stop, right, right_other, keep, cross, first in parts:
        rows = slice(i * tokens, (i + 1) * tokens)
        for columns, out_ref in zip(pair_columns(f, shard), (keep, cross)):
            value = dot_tn(own_ref[rows, start:stop], right[:, columns])
            value += dot_tn(other_ref[rows, start:stop], right_other[:, columns])
            out_ref[first : first + stop - start, :] = value.astype(jnp.bfloat16)


def out_gradients(
    at, attended_ref, attended_other, da0, da1, da2, da3, gain_grad_ref, gain_grad_other, keep_ref, cross_ref
):
    f, t = at[0], at[2]
    half, rows_here = da0.shape[0], 2 * da0.shape[0]
    shard = keep_ref.shape[1]
    heads = [attended_heads(ref, rows_here, (t,)) for ref in (attended_ref, attended_other)]
    for columns, out_ref in zip(pair_columns(f, shard), (keep_ref, cross_ref)):
        value = 0.0
        for rows_of, own, other in ((heads[0], da0, da1), (heads[1], da2, da3)):
            first = jnp.where(t == 0, own[:, columns], other[:, columns])
            second = jnp.where(t == 0, other[:, columns], own[:, columns])
            value += dot_tn(rows_of, jnp.concatenate([first, second], axis=0))
        out_ref[: 4 * LANES, :] = value.astype(jnp.bfloat16)
        out_ref[4 * LANES :, :] = extra_rows(gain_grad_ref[:, columns] + gain_grad_other[:, columns])


def qkv_gradients(at, grad_ref, h0, h1, h2, h3, w0, w1, w2, w3, gain_ref, *outs):
    f, c = at[0], at[1]
    rows, shard = grad_ref.shape[1], w0.shape[1]
    rows_here = h0.shape[0]
    for r in (1, 3, 2, 0):
        columns = part_of(f ^ r, shard)
        value = 0.0
        for k, left in enumerate((h0, h1, h2, h3)):
            value += dot_tn(grad_ref[part_of(c ^ k, rows_here), :], left[:, columns])
        store_piece(r, value.astype(jnp.bfloat16), *outs, rows=slice(0, rows))
        weight = (w0, w1, w2, w3)[r][:rows, :].astype(jnp.float32)
        gain_grad = jnp.sum(weight * value, axis=0, keepdims=True) / gain_ref[0:1, columns]
        store_piece(r, extra_rows(gain_grad), *outs, rows=slice(rows, rows + EXTRA))


def first_gradients(at, grad_ref, q0, q1, q2, q3, rest0, rest1, rest2, rest3, low_ref):
    f, c = at[0], at[1]
    rows_here = low_ref.shape[0]
    grads = [grad_ref[part_of(c ^ k, rows_here), :] for k in range(4)]
    others = jnp.concatenate(grads[1:], axis=1)
    heads = 3 * LANES
    for r in range(4):
        own, rest = (q0, q1, q2, q3)[r], (rest0, rest1, rest2, rest3)[r]
        part = dot_nn(grads[0], own[:heads, :]) + dot_nn(others, rest[...])
        low_ref[:, part_of(f ^ r, own.shape[1])] = part.astype(jnp.bfloat16)


def input_gradients(at, mine_ref, other_ref, x_ref, gain_ref, da_mine, da_other, out_ref):
    t, half = at[2], da_mine.shape[0]
    grad = (mine_ref[...].astype(jnp.float32) + other_ref[...].astype(jnp.float32)) * gain_ref[0:1, :]
    normed, scale = standardize(x_ref[...].astype(jnp.float32))
    out_ref[...] = standardize_back(normed, scale, grad)
    out_ref[part_of(t, half), :] += da_mine[...].astype(jnp.float32)
    out_ref[part_of(1 - t, half), :] += da_other[...].astype(jnp.float32)


def qkv_layout(at, p0, p1, p2, p3, out_ref):
    c = at[1]
    for k, part in enumerate((p0, p1, p2, p3)):
        for j in range(3):
            out_ref[j, :, part_of(c ^ k, LANES)] = part[j * LANES : (j + 1) * LANES, :].astype(jnp.float32).T


def short_sequences(
    tokens, segments, attn_gain, qkv_weight, out_weight, mlp_gain, inner_weight, outer_weight, cotangent
):
    f = lax.axis_index("fsdp")
    c = lax.axis_index("ctx")
    t = lax.axis_index("tp")
    here = jnp.stack([f, c, t]).astype(jnp.int32)
    row_count, width = tokens.shape[1:]
    half_rows = row_count // 2
    shard = attn_gain.shape[0]
    units = inner_weight.shape[2]
    length = segments.shape[1]
    heads = 3 * LANES
    c_order = [c ^ r for r in range(4)]
    seg_row = jnp.concatenate(
        [lax.dynamic_slice_in_dim(segments[0], p * row_count, row_count) for p in c_order]
    )
    seg_col, seg_line = seg_row.reshape(length, 1), seg_row.reshape(1, length)
    own_tokens = tokens[0]
    out_cot = cotangent[0]

    def across(value):
        return hop(value, "fsdp", 2, 4)

    def beside(value):
        return hop(value, "fsdp", 1, 4)

    def over_tp(value):
        return hop(value, "tp", 1, 2)

    def over_ctx(value, bits):
        return value if bits == 0 else hop(value, "ctx", bits, 4)

    def gathered(value, crossed):
        return [value, beside(value), crossed, beside(crossed)]

    own_half = lax.dynamic_slice_in_dim(own_tokens, t * half_rows, half_rows)
    halves = [over_ctx(own_half, r) for r in (1, 2, 3)]

    by_ctx = [
        lax.dynamic_slice_in_dim(qkv_weight, p * LANES, LANES, 2).reshape(shard, heads).T for p in c_order
    ]
    gain_rows = jnp.concatenate(
        [attn_gain[None], mlp_gain[None], jnp.zeros((EXTRA - 2, shard), attn_gain.dtype)], axis=0
    )
    qkv_own = jnp.concatenate([by_ctx[0], gain_rows], axis=0)
    qkv_rest = jnp.concatenate(by_ctx[1:], axis=0)
    out_own = out_weight
    inner_own = jnp.concatenate([inner_weight[:, 0].T, inner_weight[:, 1].T], axis=0)
    outer_own = outer_weight

    qkv_crossed = across(qkv_own)
    qkv_here = gathered(qkv_own, qkv_crossed)
    out_other = over_tp(out_own)
    (inner_own,) = after([inner_own], qkv_crossed)
    inner_crossed = across(inner_own)

    cosines, sines = zip(*[angle_tables(row_count, p * row_count, HD) for p in c_order])
    cosine, sine = jnp.concatenate(cosines, axis=0), jnp.concatenate(sines, axis=0)
    sign = jnp.where(jnp.arange(HD) < HD // 2, -1.0, 1.0).astype(jnp.float32)
    cosine = jnp.concatenate([cosine[:, 0]] * 2, axis=1)
    sine = jnp.concatenate([sine[:, 0] * sign] * 2, axis=1)

    def project(k, block):
        return local_call(
            functools.partial(project_block, k),
            [low_shape(row_count, width)] + [low_shape(row_count, LANES)] * 3 + [wide_shape(8, width)],
            here,
            [*block, *qkv_here, cosine, sine],
            scratch=[pltpu.VMEM((row_count, width), jnp.bfloat16)],
            flops=2 * row_count * width * heads,
        )

    projected = [project(0, [own_tokens])]
    for k in (1, 2, 3):
        half, qkv_rest = after([halves[k - 1], qkv_rest], *([projected[k - 2][1]] if k > 1 else []))
        if k == 2:
            half, out_other = lax.optimization_barrier((half, out_other))
            out_pair = jnp.concatenate([out_own, out_other], axis=0)
            out_crossed = across(out_pair)
        projected.append(project(k, [half, over_tp(half)]))
    h_parts, queries, keys, values = [[p[i] for p in projected] for i in range(4)]
    gain_all = projected[0][4]

    raw, low, lse = local_call(
        attention_forward,
        [wide_shape(length, LANES), low_shape(2 * length, LANES), wide_shape(8, length)],
        here,
        [*queries, *keys, *values, seg_col, seg_line],
        flops=8 * length * length * LANES,
        transcendentals=2 * length * length,
    )

    def between_all(value):
        return lax.all_to_all(value, ("ctx", "tp"), 0, 0, tiled=True)

    def between_ctx(value):
        return lax.all_to_all(value, "ctx", 0, 0, tiled=True)

    inner_crossed, out_crossed = after([inner_crossed, out_crossed], low)
    (outer_own,) = after([outer_own], inner_crossed)
    attended, outer_crossed, *weights = lax.optimization_barrier(
        (between_all(low), across(outer_own), *gathered(inner_own, inner_crossed), *gathered(out_pair, out_crossed))
    )
    inner_all, out_all = weights[:4], weights[4:]
    outer_all = gathered(outer_own, outer_crossed)

    padded = (units + LANES - 1) // LANES * LANES
    middle, normed_two, second_low, acts = local_call(
        feed_forward,
        [wide_shape(row_count, width)] * 2 + [low_shape(row_count, width), low_shape(3 * row_count, padded)],
        here,
        [attended, own_tokens, out_cot, gain_all, *out_all, *inner_all, *outer_all],
    )

    def close(*values):
        return lax.optimization_barrier(values)

    def add_pairs(*pairs):
        return [lax.optimization_barrier(mine + arrived) for mine, arrived in pairs]

    def inwards(value):
        return lax.ppermute(value, "ctx", [(0, 1), (3, 2)])

    def across_middle(value):
        return lax.ppermute(value, "ctx", [(1, 2), (2, 1)])

    def outwards(value):
        return lax.ppermute(value, "ctx", [(1, 0), (2, 3)])

    at_end = jnp.logical_or(c == 0, c == 3)

    part_mine, part_other, gain_two_part = local_call(
        feed_forward_back,
        [low_shape(half_rows, width)] * 2 + [wide_shape(1, width)],
        here,
        [acts, normed_two, *inner_all],
        scratch=[pltpu.VMEM((row_count, width), jnp.bfloat16)],
    )
    acts_other, second_low_other, cot_other, attended_beside, part_mine, part_other, gain_two_part = close(
        beside(acts), beside(second_low), beside(out_cot), beside(attended), part_mine, part_other, gain_two_part
    )

    early = units // (4 * LANES) * LANES * 2
    mlp_grads = local_call(
        mlp_gradients,
        [low_shape(rows, shard) for rows in (units, units, units + early, units + early, units - early, units - early)],
        here,
        [acts, acts_other, second_low, second_low_other, out_cot, cot_other],
        flops=2 * 3 * row_count * width * units,
    )
    arrived, rest_crossed, gain_two_other, *mlp_grads = close(
        over_tp(part_other), across(qkv_rest), beside(gain_two_part), *mlp_grads
    )
    outer_keep, outer_cross, gate_keep, gate_cross, up_keep, up_cross = mlp_grads

    attn_low, head_grads = local_call(
        head_gradients,
        [low_shape(half_rows, width), low_shape(length, LANES)],
        here,
        [part_mine, arrived, middle, out_cot, gain_all, *out_all],
        flops=row_count * width * width,
    )
    (mlp_part,) = local_call(feed_forward_out, [low_shape(row_count, width)], here, [acts, *outer_all])
    diagonal = [(i, i ^ 3) for i in range(8)]
    head_grads, outer_x, attn_tp, attn_core, attn_diagonal, mlp_part, *rest_all = close(
        between_all(head_grads), across(outer_cross), over_tp(attn_low), beside(attn_low),
        lax.ppermute(attn_low, ("fsdp", "tp"), diagonal), mlp_part, *gathered(qkv_rest, rest_crossed),
    )

    (outer_a,) = add_pairs((outer_keep, outer_x))
    (projected_grads,) = local_call(
        attention_backward,
        [low_shape(length, heads)],
        here,
        [*queries, *keys, *values, head_grads, raw, lse, cosine, sine, seg_col, seg_line],
        scratch=[pltpu.VMEM((LANES, length), jnp.float32)],
        flops=20 * length * length * LANES,
        transcendentals=2 * length * length,
    )
    out_keep, out_cross = local_call(
        out_gradients,
        [low_shape(4 * LANES + EXTRA, shard)] * 2,
        here,
        [attended, attended_beside, attn_low, attn_tp, attn_core, attn_diagonal, gain_two_part, gain_two_other],
        flops=2 * row_count * width * 4 * LANES,
    )
    outer_in, gate_x, mlp_other, projected_grads, out_keep, out_cross = close(
        inwards(outer_a), across(gate_cross), over_tp(mlp_part), projected_grads, out_keep, out_cross
    )

    gate_a, outer_b = add_pairs((gate_keep, gate_x), (outer_a, outer_in))
    qkv_parts = local_call(
        qkv_gradients,
        [low_shape(2, heads + EXTRA, shard)] + [low_shape(heads + EXTRA, shard)] * 2,
        here,
        [projected_grads, *h_parts, *qkv_here, gain_all],
        flops=2 * length * width * heads,
    )
    first_in, up_x, out_x, gate_in, outer_mid, *qkv_parts = close(
        between_ctx(projected_grads), across(up_cross), across(out_cross), inwards(gate_a), across_middle(outer_b),
        *qkv_parts,
    )

    qkv_sent, qkv_keep, qkv_keep_across = qkv_parts
    joined_rows = units - early + 4 * LANES + EXTRA
    up_a, outer_c, payload = local_call(
        joined_sums,
        [low_shape(joined_rows, shard), low_shape(units, shard), low_shape(joined_rows, shard)],
        here,
        [up_keep, up_x, out_keep, out_x, outer_b, outer_mid],
    )
    (gate_b,) = add_pairs((gate_a, gate_in))
    (first_low_part,) = local_call(
        first_gradients,
        [low_shape(row_count, width)],
        here,
        [first_in, *qkv_here, *rest_all],
        flops=2 * row_count * width * 4 * heads,
    )
    up_in, gate_mid, qkv_received, first_low_part = close(
        over_ctx(payload, 1), across_middle(gate_b), beside(qkv_sent), first_low_part
    )
    outer_out = up_in[:units]

    up_b, gate_c = add_pairs((up_a, up_in), (gate_b, gate_mid))
    qkv_cross = qkv_keep_across + qkv_received[1]
    outer_grad = jnp.where(at_end, outer_out, outer_c).astype(jnp.float32)
    first_other, up_mid, gate_out, qkv_x, outer_grad = close(
        over_tp(first_low_part), across_middle(up_b), outwards(gate_c), across(qkv_cross), outer_grad
    )

    (up_c,) = add_pairs((up_b, up_mid))
    qkv_sum = lax.optimization_barrier(
        (qkv_keep.astype(jnp.float32) + qkv_received[0].astype(jnp.float32) + qkv_x.astype(jnp.float32)).astype(
            jnp.bfloat16
        )
    )
    (input_grad,) = local_call(
        input_gradients,
        [wide_shape(row_count, width)],
        here,
        [first_low_part, first_other, own_tokens, gain_all, attn_low, attn_tp],
    )
    gate_sum = jnp.where(at_end, gate_out, gate_c)
    block_out = (
        middle + (mlp_part.astype(jnp.float32) + mlp_other.astype(jnp.float32))
    ).astype(jnp.bfloat16)
    up_out, input_grad, gate_sum, block_out, *qkv_sums = close(
        outwards(up_c), input_grad, gate_sum, block_out, *[over_ctx(qkv_sum, k) for k in (1, 2, 3)]
    )
    qkv_sums = [qkv_sum, *qkv_sums]
    up_sum = jnp.where(at_end, up_out, up_c)
    late = units - early
    out_grad = up_sum[late : late + 4 * LANES].astype(jnp.float32)

    (qkv_grad,) = local_call(qkv_layout, [wide_shape(3, shard, 4 * LANES)], here, qkv_sums)
    gain_lines = [part[heads].astype(jnp.float32) for part in qkv_sums]
    up_grad = jnp.concatenate([gate_sum[units:], up_sum[:late]], axis=0)
    gain_grads = jnp.stack(
        [(gain_lines[0] + gain_lines[1]) + (gain_lines[2] + gain_lines[3]), up_sum[late + 4 * LANES].astype(jnp.float32)]
    )
    gain_grads = gain_grads + over_tp(gain_grads)

    return (
        block_out[None],
        input_grad[None],
        gain_grads[0],
        qkv_grad.transpose(1, 0, 2),
        out_grad,
        gain_grads[1],
        jnp.stack([gate_sum[:units].T, up_grad.T], axis=1).astype(jnp.float32),
        outer_grad,
    )


def solution(mesh):
    placed = (
        P("fsdp", "ctx", None),
        P("fsdp", None),
        P("fsdp"),
        P("fsdp", None, "tp"),
        P("tp", "fsdp"),
        P("fsdp"),
        P("fsdp", None, "tp"),
        P("tp", "fsdp"),
        P("fsdp", "ctx", None),
    )
    sizes = dict(mesh.shape)

    def layer(*args):
        tokens, segments, qkv_weight = args[0], args[1], args[3]
        heads_apart = qkv_weight.shape[2] == 4 * LANES
        short = segments.shape[1] == 4 * tokens.shape[1] and segments.shape[1] <= 1024
        small = (sizes["fsdp"], sizes["ctx"], sizes["tp"]) == (4, 4, 2)
        if small and short and heads_apart and tokens.shape[0] == 1:
            return short_sequences(*args)
        return per_device(*args)

    return jax.shard_map(
        layer,
        mesh=mesh,
        in_specs=placed,
        out_specs=(
            P("fsdp", "ctx", None),
            P("fsdp", "ctx", None),
            P("fsdp"),
            P("fsdp", None, "tp"),
            P("tp", "fsdp"),
            P("fsdp"),
            P("fsdp", None, "tp"),
            P("tp", "fsdp"),
        ),
        check_vma=False,
    )
```

```python
import functools
import math

import jax
import jax.numpy as jnp
from jax import lax
from jax.experimental import pallas as pl
from jax.experimental.pallas import tpu as pltpu
from jax.sharding import PartitionSpec as P

HD = 64


EPSILON = 1e-05
ROPE_BASE = 160000.0
MASKED = -1e30


def normalize(values, gain_row):
    row_mean = jnp.mean(values, axis=-1, keepdims=True)
    centered = values - row_mean
    spread = jnp.mean(centered * centered, axis=-1, keepdims=True)
    return centered * lax.rsqrt(spread + EPSILON) * gain_row


def geglu(gate_in, upper):
    return jax.nn.gelu(gate_in, approximate=False) * upper


def angle_tables(row_count, offset, depth):
    half_width = depth // 2
    inverse = jnp.power(
        jnp.float32(ROPE_BASE), -(2.0 * jnp.arange(half_width, dtype=jnp.float32)) / depth
    )
    places = (offset + jnp.arange(row_count, dtype=jnp.int32)).astype(jnp.float32)
    angles = places[:, None] * inverse[None, :]
    angles = jnp.concatenate([angles, angles], axis=-1)
    return (jnp.cos(angles)[:, None, :], jnp.sin(angles)[:, None, :])


def rotate(values, cosine, sine):
    half_width = values.shape[-1] // 2
    turned = jnp.concatenate([-values[..., half_width:], values[..., :half_width]], axis=-1)
    return values * cosine + turned * sine


def rotate_back(grad_in, cosine, sine):
    half_width = grad_in.shape[-1] // 2
    scaled = grad_in * sine
    turned = jnp.concatenate([scaled[..., half_width:], -scaled[..., :half_width]], axis=-1)
    return grad_in * cosine + turned


def attend_forward(queries, query_seg, seg_row, key_low, value_low, score_scale):
    row_count, heads_here, depth = queries.shape
    initial = (
        jnp.full((heads_here, row_count), MASKED, jnp.float32),
        jnp.zeros((heads_here, row_count), jnp.float32),
        jnp.zeros((row_count, heads_here, depth), jnp.float32),
    )
    key_piece = lax.all_gather(key_low, "ctx", axis=0, tiled=True)
    value_piece = lax.all_gather(value_low, "ctx", axis=0, tiled=True)
    piece_rows = key_piece.shape[0]
    block_size = math.gcd(piece_rows, 512)
    blocks = (
        key_piece.reshape(piece_rows // block_size, block_size, heads_here, depth),
        value_piece.reshape(piece_rows // block_size, block_size, heads_here, depth),
        seg_row.reshape(piece_rows // block_size, block_size),
    )

    def step(state, block_data):
        running_peak, running_total, accum = state
        key_block, value_block, block_seg = block_data
        scores = jnp.einsum("qhe,khe->hqk", queries, key_block, preferred_element_type=jnp.float32)
        same_doc = (query_seg[:, None] == block_seg[None, :])[None]
        logits = jnp.where(same_doc, scores * score_scale, MASKED)
        new_peak = jnp.maximum(running_peak, jnp.max(logits, axis=-1))
        rescale = jnp.exp(running_peak - new_peak)
        weights = jnp.where(same_doc, jnp.exp(logits - new_peak[:, :, None]), 0.0)
        running_total = running_total * rescale + jnp.sum(weights, axis=-1)
        mixed_out = jnp.einsum(
            "hqk,khe->qhe",
            weights.astype(jnp.bfloat16),
            value_block,
            preferred_element_type=jnp.float32,
        )
        accum = accum * rescale.T[:, :, None] + mixed_out
        return ((new_peak, running_total, accum), None)

    result, unused = lax.scan(step, initial, blocks)
    running_peak, running_total, accum = result
    return (accum / running_total.T[:, :, None], running_peak + jnp.log(running_total))


def probs_and_grads(
    query_block, key_block, grad_block, value_block, same_doc, log_total, delta_rows, score_scale
):
    scores = jnp.einsum("qhe,khe->hqk", query_block, key_block, preferred_element_type=jnp.float32)
    probs = jnp.where(same_doc, jnp.exp(scores * score_scale - log_total[:, :, None]), 0.0)
    prob_grad = jnp.einsum(
        "qhe,khe->hqk", grad_block, value_block, preferred_element_type=jnp.float32
    )
    score_grad = (probs * (prob_grad - delta_rows[:, :, None]) * score_scale).astype(jnp.bfloat16)
    return (probs.astype(jnp.bfloat16), score_grad)


def attend_backward(
    queries, key_low, value_low, grad_low, log_total, delta_rows, query_seg, seg_row, score_scale
):
    row_count, heads_here, depth = queries.shape
    seq_length = seg_row.shape[0]
    block_size = math.gcd(seq_length, 512)
    block_count = seq_length // block_size
    key_all, value_all = (
        lax.all_gather(key_low, "ctx", axis=0, tiled=True),
        lax.all_gather(value_low, "ctx", axis=0, tiled=True),
    )
    blocks = (
        key_all.reshape(block_count, block_size, heads_here, depth),
        value_all.reshape(block_count, block_size, heads_here, depth),
        seg_row.reshape(block_count, block_size),
    )

    def key_step(query_acc, block_data):
        key_block, value_block, block_seg = block_data
        same_doc = (query_seg[:, None] == block_seg[None, :])[None]
        prob_low, score_grad = probs_and_grads(
            queries, key_block, grad_low, value_block, same_doc, log_total, delta_rows, score_scale
        )
        query_acc = query_acc + jnp.einsum(
            "hqk,khe->qhe", score_grad, key_block, preferred_element_type=jnp.float32
        )
        key_part = jnp.einsum(
            "hqk,qhe->khe", score_grad, queries, preferred_element_type=jnp.float32
        )
        value_part = jnp.einsum(
            "hqk,qhe->khe", prob_low, grad_low, preferred_element_type=jnp.float32
        )
        return (query_acc, (key_part, value_part))

    query_grad, key_value_parts = lax.scan(
        key_step, jnp.zeros((row_count, heads_here, depth), jnp.float32), blocks
    )
    key_parts = key_value_parts[0].reshape(seq_length, heads_here * depth)
    value_parts = key_value_parts[1].reshape(seq_length, heads_here * depth)
    key_grad, value_grad = (
        lax.psum_scatter(
            key_parts.astype(jnp.bfloat16), "ctx", scatter_dimension=0, tiled=True
        ).astype(jnp.float32),
        lax.psum_scatter(
            value_parts.astype(jnp.bfloat16), "ctx", scatter_dimension=0, tiled=True
        ).astype(jnp.float32),
    )
    key_grad = key_grad.reshape(row_count, heads_here, depth)
    value_grad = value_grad.reshape(row_count, heads_here, depth)
    return (query_grad, key_grad, value_grad)


def per_device(
    tokens,
    segments,
    attn_gain,
    qkv_weight,
    out_weight,
    mlp_gain,
    inner_weight,
    outer_weight,
    cotangent,
):
    qkv_full, out_full, gain_one = (
        lax.all_gather(qkv_weight, "fsdp", axis=0, tiled=True),
        lax.all_gather(out_weight, "fsdp", axis=1, tiled=True),
        lax.all_gather(attn_gain, "fsdp", axis=0, tiled=True),
    )
    inner_full, outer_full, gain_two = (
        lax.all_gather(inner_weight, "fsdp", axis=0, tiled=True),
        lax.all_gather(outer_weight, "fsdp", axis=1, tiled=True),
        lax.all_gather(mlp_gain, "fsdp", axis=0, tiled=True),
    )
    seq_count, row_count, model_width = tokens.shape
    local_width = qkv_full.shape[2]
    heads_here = local_width // HD
    score_scale = HD ** (-0.5)
    offset = lax.axis_index("ctx") * row_count
    cosine, sine = angle_tables(row_count, offset, HD)
    input_rows = tokens.reshape(-1, model_width).astype(jnp.float32)
    normed_one, norm_one_back = jax.vjp(normalize, input_rows, gain_one.astype(jnp.float32))
    first_low = normed_one.astype(jnp.bfloat16)
    projected_output = jnp.einsum(
        "td,dcf->tcf", first_low, qkv_full, preferred_element_type=jnp.float32
    )
    projected_output = projected_output.reshape(seq_count, row_count, 3, heads_here, HD)
    query_low = rotate(projected_output[:, :, 0], cosine, sine).astype(jnp.bfloat16)
    key_low = rotate(projected_output[:, :, 1], cosine, sine).astype(jnp.bfloat16)
    value_low = projected_output[:, :, 2].astype(jnp.bfloat16)
    seq_index = 0
    seg_row = segments[seq_index]
    query_seg = lax.dynamic_slice_in_dim(seg_row, offset, row_count)
    raw_out, log_total = attend_forward(
        query_low[seq_index],
        query_seg,
        seg_row,
        key_low[seq_index],
        value_low[seq_index],
        score_scale,
    )
    query_segs = [query_seg]
    raw_outs = [raw_out]
    log_totals = [log_total]
    attended_low = jnp.stack(raw_outs).astype(jnp.bfloat16).reshape(-1, local_width)
    attn_part = jnp.dot(attended_low, out_full, preferred_element_type=jnp.float32)
    middle_activation = input_rows + lax.psum(attn_part.astype(jnp.bfloat16), "tp").astype(
        jnp.float32
    )
    normed_two, norm_two_back = jax.vjp(normalize, middle_activation, gain_two.astype(jnp.float32))
    second_low = normed_two.astype(jnp.bfloat16)
    hidden_input = jnp.einsum(
        "td,dcf->tcf", second_low, inner_full, preferred_element_type=jnp.float32
    )
    hidden_state, geglu_back = jax.vjp(geglu, hidden_input[:, 0], hidden_input[:, 1])
    hidden_low = hidden_state.astype(jnp.bfloat16)
    mlp_part = jnp.dot(hidden_low, outer_full, preferred_element_type=jnp.float32)
    block_out = (
        middle_activation + lax.psum(mlp_part.astype(jnp.bfloat16), "tp").astype(jnp.float32)
    ).astype(jnp.bfloat16)
    out_cot = cotangent.reshape(-1, model_width)
    outer_local = jnp.einsum("tf,td->fd", hidden_low, out_cot, preferred_element_type=jnp.float32)
    hidden_grad = jnp.einsum("td,fd->tf", out_cot, outer_full, preferred_element_type=jnp.float32)
    gate_grad, up_grad = geglu_back(hidden_grad)
    inner_low = jnp.stack([gate_grad, up_grad], axis=1).astype(jnp.bfloat16)
    inner_local = jnp.einsum(
        "td,tcf->dcf", second_low, inner_low, preferred_element_type=jnp.float32
    )
    normed_two_grad = lax.psum(
        jnp.einsum("tcf,dcf->td", inner_low, inner_full, preferred_element_type=jnp.float32).astype(
            jnp.bfloat16
        ),
        "tp",
    ).astype(jnp.float32)
    middle_part, gain_two_grad = norm_two_back(normed_two_grad)
    middle_grad = out_cot.astype(jnp.float32) + middle_part
    attn_low = middle_grad.astype(jnp.bfloat16)
    out_local = jnp.einsum("tf,td->fd", attended_low, attn_low, preferred_element_type=jnp.float32)
    attended_grad = jnp.einsum("td,fd->tf", attn_low, out_full, preferred_element_type=jnp.float32)
    attended_grad = attended_grad.astype(jnp.bfloat16).reshape(seq_count, row_count, heads_here, HD)
    seq_index = 0
    grad_low = attended_grad[seq_index]
    delta_rows = jnp.sum(grad_low.astype(jnp.float32) * raw_outs[seq_index], axis=-1).T
    query_grad, key_grad, value_grad = attend_backward(
        query_low[seq_index],
        key_low[seq_index],
        value_low[seq_index],
        grad_low,
        log_totals[seq_index],
        delta_rows,
        query_segs[seq_index],
        segments[seq_index],
        score_scale,
    )
    stacked = jnp.stack(
        [rotate_back(query_grad, cosine, sine), rotate_back(key_grad, cosine, sine), value_grad],
        axis=1,
    )
    qkv_grads = stacked.reshape(row_count, 3, local_width)
    qkv_low = qkv_grads.astype(jnp.bfloat16)
    qkv_local = jnp.einsum("td,tcf->dcf", first_low, qkv_low, preferred_element_type=jnp.float32)
    normed_one_grad = lax.psum(
        jnp.einsum("tcf,dcf->td", qkv_low, qkv_full, preferred_element_type=jnp.float32).astype(
            jnp.bfloat16
        ),
        "tp",
    ).astype(jnp.float32)
    input_part, gain_one_grad = norm_one_back(normed_one_grad)
    input_grad = (middle_grad + input_part).reshape(tokens.shape)
    summed = (
        lax.psum_scatter(gain_one_grad, ("fsdp", "ctx"), scatter_dimension=0, tiled=True),
        lax.psum_scatter(qkv_local, ("fsdp", "ctx"), scatter_dimension=0, tiled=True),
        lax.psum_scatter(out_local, ("fsdp", "ctx"), scatter_dimension=1, tiled=True),
        lax.psum_scatter(gain_two_grad, ("fsdp", "ctx"), scatter_dimension=0, tiled=True),
        lax.psum_scatter(inner_local, ("fsdp", "ctx"), scatter_dimension=0, tiled=True),
        lax.psum_scatter(outer_local, ("fsdp", "ctx"), scatter_dimension=1, tiled=True),
    )
    gain_one_sum, qkv_sum, out_sum, gain_two_sum, inner_sum, outer_sum = summed
    shards = (
        lax.all_gather(gain_one_sum.astype(jnp.bfloat16), "ctx", axis=0, tiled=True).astype(
            gain_one_sum.dtype
        ),
        lax.all_gather(qkv_sum.astype(jnp.bfloat16), "ctx", axis=0, tiled=True).astype(
            qkv_sum.dtype
        ),
        lax.all_gather(out_sum.astype(jnp.bfloat16), "ctx", axis=1, tiled=True).astype(
            out_sum.dtype
        ),
        lax.all_gather(gain_two_sum.astype(jnp.bfloat16), "ctx", axis=0, tiled=True).astype(
            gain_two_sum.dtype
        ),
        lax.all_gather(inner_sum.astype(jnp.bfloat16), "ctx", axis=0, tiled=True).astype(
            inner_sum.dtype
        ),
        lax.all_gather(outer_sum.astype(jnp.bfloat16), "ctx", axis=1, tiled=True).astype(
            outer_sum.dtype
        ),
    )
    return (
        block_out.reshape(tokens.shape),
        input_grad,
        shards[0],
        shards[1],
        shards[2],
        shards[3],
        shards[4],
        shards[5],
    )


LANES = 128
BLOCK = 256
EXTRA = 32
COST = 0.0
WIDE_VMEM = 62 * 1024 * 1024


def hop(value, axis, bit, count):
    return lax.ppermute(value, axis, [(i, i ^ bit) for i in range(count)])


def after(values, *earlier):
    values = list(values)
    return list(lax.optimization_barrier(tuple(values) + earlier))[: len(values)]


def lane_half(shape):
    return lax.broadcasted_iota(jnp.int32, shape, 1) < HD


def swap_halves(values):
    lane = lax.broadcasted_iota(jnp.int32, values.shape, 1)
    low_part = lax.rem(lane, HD) < HD // 2
    return jnp.where(
        low_part,
        pltpu.roll(values, LANES - HD // 2, 1),
        pltpu.roll(values, HD // 2, 1),
    )


def dot_nt(left, right):
    return lax.dot_general(left, right, (((1,), (1,)), ((), ())), preferred_element_type=jnp.float32)


def dot_nn(left, right):
    return lax.dot_general(left, right, (((1,), (0,)), ((), ())), preferred_element_type=jnp.float32)


def dot_tn(left, right):
    return lax.dot_general(left, right, (((0,), (0,)), ((), ())), preferred_element_type=jnp.float32)


def one_head(values, head):
    first = lane_half(values.shape)
    keep = first if head == 0 else jnp.logical_not(first)
    return jnp.where(keep, values, jnp.zeros_like(values))


def part_of(index, size):
    return pl.ds(pl.multiple_of(index * size, size), size)


def standardize(values):
    row_mean = jnp.mean(values, axis=-1, keepdims=True)
    centered = values - row_mean
    spread = jnp.mean(centered * centered, axis=-1, keepdims=True)
    scale = lax.rsqrt(spread + EPSILON)
    return centered * scale, scale


def standardize_back(normed, scale, grad):
    inner = jnp.mean(grad * normed, axis=-1, keepdims=True)
    return scale * (grad - jnp.mean(grad, axis=-1, keepdims=True) - normed * inner)


def local_call(body, outs, places, operands, scratch=(), flops=0, transcendentals=0):
    moved = sum(math.prod(o.shape) * o.dtype.itemsize for o in list(operands) + list(outs))
    return pl.pallas_call(
        body,
        name=body.__name__ if hasattr(body, "__name__") else body.func.__name__,
        out_shape=tuple(outs),
        in_specs=[pl.BlockSpec(memory_space=pltpu.SMEM)]
        + [pl.BlockSpec(memory_space=pltpu.VMEM)] * len(operands),
        out_specs=tuple([pl.BlockSpec(memory_space=pltpu.VMEM)] * len(outs)),
        scratch_shapes=list(scratch),
        compiler_params=pltpu.CompilerParams(vmem_limit_bytes=WIDE_VMEM),
        cost_estimate=pl.CostEstimate(
            flops=int(flops * COST), bytes_accessed=int(moved * COST), transcendentals=int(transcendentals * COST)
        ),
    )(places, *operands)


def low_shape(*shape):
    return jax.ShapeDtypeStruct(shape, jnp.bfloat16)


def wide_shape(*shape):
    return jax.ShapeDtypeStruct(shape, jnp.float32)


def project_block(block, at, *refs):
    f, t = at[0], at[2]
    count = len(refs) - 12
    tokens_in, (w0, w1, w2, w3, cos_ref, sin_ref) = refs[:count], refs[count : count + 6]
    h_ref, q_ref, k_ref, v_ref, gain_ref, x_ref = refs[count + 6 :]
    weights = (w0, w1, w2, w3)
    columns = [part_of(f ^ r, w0.shape[1]) for r in range(4)]
    heads = 3 * LANES
    for r, weight in enumerate(weights):
        gain_ref[:, columns[r]] = weight[heads : heads + EXTRA, :].astype(jnp.float32)[:8, :]
    if count == 1:
        tokens = tokens_in[0][...]
    else:
        half = tokens_in[0].shape[0]
        x_ref[part_of(t, half), :] = tokens_in[0][...]
        x_ref[part_of(1 - t, half), :] = tokens_in[1][...]
        tokens = x_ref[...]
    h_ref[...] = (standardize(tokens.astype(jnp.float32))[0] * gain_ref[0:1, :]).astype(jnp.bfloat16)
    projected = 0.0
    for r, weight in enumerate(weights):
        projected += dot_nt(h_ref[:, columns[r]], weight[:heads, :])
    rows = slice(block * tokens.shape[0], (block + 1) * tokens.shape[0])
    cosine, sine = cos_ref[rows, :], sin_ref[rows, :]
    for ref, part in ((q_ref, projected[:, :LANES]), (k_ref, projected[:, LANES : 2 * LANES])):
        ref[...] = (part * cosine + swap_halves(part) * sine).astype(jnp.bfloat16)
    v_ref[...] = projected[:, 2 * LANES :].astype(jnp.bfloat16)


def joined(refs):
    return jnp.concatenate([ref[...] for ref in refs], axis=0)


def attention_forward(at, *refs):
    c = at[1]
    query_refs, key_refs, value_refs, seg_col, seg_line = refs[:4], refs[4:8], refs[8:12], refs[12], refs[13]
    raw_ref, low_ref, lse_ref = refs[14:]
    rows_here = query_refs[0].shape[0]
    keys, values = joined(key_refs), joined(value_refs)
    for k in range(4):
        rows = slice(k * rows_here, (k + 1) * rows_here)
        queries = query_refs[k][...] * jnp.bfloat16(HD ** (-0.5))
        same = seg_col[rows, :] == seg_line[...]
        outs, logs = [], []
        for head in range(2):
            scores = dot_nt(one_head(queries, head), keys)
            scores = jnp.where(same, scores, MASKED)
            peak = jnp.max(scores, axis=1, keepdims=True)
            weights = jnp.exp(scores - peak)
            total = jnp.sum(weights, axis=1, keepdims=True)
            probs = (weights * (1.0 / total)).astype(jnp.bfloat16)
            outs.append(dot_nn(probs, values))
            logs.append(peak + jnp.log(total))
        raw = jnp.where(lane_half(outs[0].shape), outs[0], outs[1])
        raw_ref[rows, :] = raw
        for b in range(2):
            low_ref[part_of((c ^ k) * 2 + b, rows_here), :] = raw.astype(jnp.bfloat16)
        lane = lax.broadcasted_iota(jnp.int32, (rows_here, LANES), 1)
        lse_ref[:, rows] = jnp.where(lane == 0, logs[0], logs[1]).T[:8, :]


def attention_backward(
    at, q0, q1, q2, q3, k0, k1, k2, k3, v0, v1, v2, v3, do_ref, raw_ref, lse_ref, cos_ref, sin_ref,
    seg_col, seg_line, out_ref, turned_ref,
):
    c = at[1]
    rows_here = q0.shape[0]
    grads = jnp.concatenate([do_ref[part_of(c ^ k, rows_here), :] for k in range(4)], axis=0)
    product = grads.astype(jnp.float32) * raw_ref[...]
    first = lane_half(product.shape)
    whole = jnp.sum(jnp.where(first, product, 0.0), axis=1, keepdims=True)
    other = jnp.sum(jnp.where(first, 0.0, product), axis=1, keepdims=True)
    lane = lax.broadcasted_iota(jnp.int32, product.shape, 1)
    delta = jnp.where(lane == 0, whole, other).T
    scale = HD ** (-0.5)
    queries = joined((q0, q1, q2, q3))
    scaled = queries * jnp.bfloat16(scale)
    for k in range(4):
        rows, place = slice(k * rows_here, (k + 1) * rows_here), part_of(c ^ k, rows_here)
        keys, values = (k0, k1, k2, k3)[k][...], (v0, v1, v2, v3)[k][...]
        keys_turned = keys.T
        same = seg_col[rows, :] == seg_line[...]
        key_parts, value_parts = [], []
        for head in range(2):
            scores = dot_nt(one_head(keys, head), scaled)
            probs = jnp.where(same, jnp.exp(scores - lse_ref[head : head + 1, :]), 0.0)
            prob_grad = dot_nt(one_head(values, head), grads)
            score_grad = (probs * (prob_grad - delta[head : head + 1, :])).astype(jnp.bfloat16)
            value_parts.append(dot_nn(probs.astype(jnp.bfloat16), grads))
            key_parts.append(dot_nn(score_grad, scaled))
            here = slice(head * HD, (head + 1) * HD)
            part = dot_nn(keys_turned[here, :], score_grad)
            if k == 0:
                turned_ref[here, :] = part
            else:
                turned_ref[here, :] += part
        half = lane_half(key_parts[0].shape)
        key_grad = jnp.where(half, key_parts[0], key_parts[1])
        value_grad = jnp.where(half, value_parts[0], value_parts[1])
        key_grad = key_grad * cos_ref[rows, :] - swap_halves(key_grad) * sin_ref[rows, :]
        out_ref[place, LANES : 2 * LANES] = key_grad.astype(jnp.bfloat16)
        out_ref[place, 2 * LANES :] = value_grad.astype(jnp.bfloat16)
    for k in range(4):
        rows, place = slice(k * rows_here, (k + 1) * rows_here), part_of(c ^ k, rows_here)
        query_grad = turned_ref[:, rows].T * scale
        query_grad = query_grad * cos_ref[rows, :] - swap_halves(query_grad) * sin_ref[rows, :]
        out_ref[place, :LANES] = query_grad.astype(jnp.bfloat16)


def attended_heads(ref, rows_here, sides):
    return jnp.concatenate([ref[part_of(k * 2 + b, rows_here), :] for b in sides for k in range(4)], axis=1)


def feed_forward(
    at, attended_ref, x_ref, cot_ref, gain_ref,
    o0, o1, o2, o3, inner0, inner1, inner2, inner3, outer0, outer1, outer2, outer3,
    mid_ref, normed_ref, second_ref, acts_ref,
):
    f, t = at[0], at[2]
    rows_here = x_ref.shape[0]
    attended = attended_heads(attended_ref, rows_here, (t, 1 - t))
    inners, outers = (inner0, inner1, inner2, inner3), (outer0, outer1, outer2, outer3)
    columns = [part_of(f ^ r, o0.shape[1]) for r in range(4)]
    for r, weight in enumerate((o0, o1, o2, o3)):
        mid_ref[:, columns[r]] = x_ref[:, columns[r]].astype(jnp.float32) + dot_nn(attended, weight[...])
    normed = standardize(mid_ref[...])[0]
    normed_ref[...] = normed
    second_ref[...] = (normed * gain_ref[1:2, :]).astype(jnp.bfloat16)
    units = outer0.shape[0]
    for start in range(0, units, BLOCK):
        stop = min(start + BLOCK, units)
        gate, up, hid_grad = 0.0, 0.0, 0.0
        for r in range(4):
            rows = second_ref[:, columns[r]]
            gate += dot_nt(rows, inners[r][start:stop, :])
            up += dot_nt(rows, inners[r][units + start : units + stop, :])
            hid_grad += dot_nt(cot_ref[:, columns[r]], outers[r][start:stop, :])
        below = 0.5 + 0.5 * lax.erf(gate * (2.0 ** -0.5))
        density = jnp.exp(-0.5 * gate * gate) * ((2.0 * math.pi) ** -0.5)
        active = gate * below
        acts_ref[:rows_here, start:stop] = (active * up).astype(jnp.bfloat16)
        acts_ref[rows_here : 2 * rows_here, start:stop] = (
            hid_grad * up * (below + gate * density)
        ).astype(jnp.bfloat16)
        acts_ref[2 * rows_here :, start:stop] = (hid_grad * active).astype(jnp.bfloat16)


def feed_forward_back(
    at, acts_ref, normed_ref, inner0, inner1, inner2, inner3, mine_ref, other_ref, gain_grad_ref, low_ref
):
    f, t = at[0], at[2]
    rows_here = normed_ref.shape[0]
    units = inner0.shape[0] // 2
    gate_grad = acts_ref[rows_here : 2 * rows_here, :units]
    up_grad = acts_ref[2 * rows_here :, :units]
    for r, inner in enumerate((inner0, inner1, inner2, inner3)):
        columns = part_of(f ^ r, inner.shape[1])
        part = dot_nn(gate_grad, inner[:units, :]) + dot_nn(up_grad, inner[units:, :])
        low_ref[:, columns] = part.astype(jnp.bfloat16)
        gain_grad_ref[:, columns] = jnp.sum(part * normed_ref[:, columns], axis=0, keepdims=True)
    half = mine_ref.shape[0]
    mine_ref[...] = low_ref[part_of(t, half), :]
    other_ref[...] = low_ref[part_of(1 - t, half), :]


def feed_forward_out(at, acts_ref, outer0, outer1, outer2, outer3, out_ref):
    f = at[0]
    hidden = acts_ref[: out_ref.shape[0], : outer0.shape[0]]
    for r, weight in enumerate((outer0, outer1, outer2, outer3)):
        out_ref[:, part_of(f ^ r, weight.shape[1])] = dot_nn(hidden, weight[...]).astype(jnp.bfloat16)


def head_gradients(
    at, mine_ref, other_ref, mid_ref, cot_ref, gain_ref, o0, o1, o2, o3, da_ref, out_ref
):
    f, t = at[0], at[2]
    rows = part_of(t, da_ref.shape[0])
    grad = (mine_ref[...].astype(jnp.float32) + other_ref[...].astype(jnp.float32)) * gain_ref[1:2, :]
    normed, scale = standardize(mid_ref[rows, :])
    mid_grad = cot_ref[rows, :].astype(jnp.float32) + standardize_back(normed, scale, grad)
    da_ref[...] = mid_grad.astype(jnp.bfloat16)
    total = 0.0
    for r, weight in enumerate((o0, o1, o2, o3)):
        total += dot_nt(da_ref[:, part_of(f ^ r, weight.shape[1])], weight[...])
    for b in range(2):
        for k in range(4):
            at_part = (b * 4 + k) * LANES
            out_ref[part_of(k * 2 + (t ^ b), da_ref.shape[0]), :] = total[:, at_part : at_part + LANES].astype(
                jnp.bfloat16
            )


def store_piece(r, value, send_ref, keep_ref, keep_across_ref, rows=slice(None)):
    if r in (1, 3):
        send_ref[r // 2, rows, :] = value
    else:
        (keep_ref if r == 0 else keep_across_ref)[rows, :] = value


def extra_rows(row):
    lines = lax.broadcasted_iota(jnp.int32, (EXTRA, row.shape[1]), 0)
    return jnp.where(lines == 0, row, 0.0).astype(jnp.bfloat16)


def joined_sums(
    at, up_keep, up_x, out_keep, out_x, outer_ref, outer_arrived, joined_ref, outer_sum, payload_ref
):
    c = at[1]
    rows, units = up_keep.shape[0], outer_ref.shape[0]
    joined_ref[:rows, :] = up_keep[...] + up_x[...]
    joined_ref[rows:, :] = out_keep[...] + out_x[...]
    outer_sum[...] = outer_ref[...] + outer_arrived[...]
    at_end = jnp.logical_or(c == 0, c == 3)

    @pl.when(at_end)
    def _():
        payload_ref[...] = joined_ref[...]

    @pl.when(jnp.logical_not(at_end))
    def _():
        payload_ref[:units, :] = outer_sum[...]
        payload_ref[units:, :] = jnp.zeros_like(payload_ref[units:, :])


def pair_columns(f, shard):
    return part_of(f, shard), part_of(f ^ 2, shard)


def mlp_gradients(
    at, own_ref, other_ref, second_ref, second_other, cot_ref, cot_other,
    outer_keep, outer_cross, gate_keep, gate_cross, up_keep, up_cross,
):
    f = at[0]
    units, shard = outer_keep.shape
    tokens = cot_ref.shape[0]
    early = gate_keep.shape[0] - units
    parts = (
        (0, 0, units, cot_ref, cot_other, outer_keep, outer_cross, 0),
        (1, 0, units, second_ref, second_other, gate_keep, gate_cross, 0),
        (2, 0, early, second_ref, second_other, gate_keep, gate_cross, units),
        (2, early, units, second_ref, second_other, up_keep, up_cross, 0),
    )
    for i, start, stop, right, right_other, keep, cross, first in parts:
        rows = slice(i * tokens, (i + 1) * tokens)
        for columns, out_ref in zip(pair_columns(f, shard), (keep, cross)):
            value = dot_tn(own_ref[rows, start:stop], right[:, columns])
            value += dot_tn(other_ref[rows, start:stop], right_other[:, columns])
            out_ref[first : first + stop - start, :] = value.astype(jnp.bfloat16)


def out_gradients(
    at, attended_ref, attended_other, da0, da1, da2, da3, gain_grad_ref, gain_grad_other, keep_ref, cross_ref
):
    f, t = at[0], at[2]
    half, rows_here = da0.shape[0], 2 * da0.shape[0]
    shard = keep_ref.shape[1]
    heads = [attended_heads(ref, rows_here, (t,)) for ref in (attended_ref, attended_other)]
    for columns, out_ref in zip(pair_columns(f, shard), (keep_ref, cross_ref)):
        value = 0.0
        for rows_of, own, other in ((heads[0], da0, da1), (heads[1], da2, da3)):
            first = jnp.where(t == 0, own[:, columns], other[:, columns])
            second = jnp.where(t == 0, other[:, columns], own[:, columns])
            value += dot_tn(rows_of, jnp.concatenate([first, second], axis=0))
        out_ref[: 4 * LANES, :] = value.astype(jnp.bfloat16)
        out_ref[4 * LANES :, :] = extra_rows(gain_grad_ref[:, columns] + gain_grad_other[:, columns])


def qkv_gradients(at, grad_ref, h0, h1, h2, h3, w0, w1, w2, w3, gain_ref, *outs):
    f, c = at[0], at[1]
    rows, shard = grad_ref.shape[1], w0.shape[1]
    rows_here = h0.shape[0]
    for r in (1, 3, 2, 0):
        columns = part_of(f ^ r, shard)
        value = 0.0
        for k, left in enumerate((h0, h1, h2, h3)):
            value += dot_tn(grad_ref[part_of(c ^ k, rows_here), :], left[:, columns])
        store_piece(r, value.astype(jnp.bfloat16), *outs, rows=slice(0, rows))
        weight = (w0, w1, w2, w3)[r][:rows, :].astype(jnp.float32)
        gain_grad = jnp.sum(weight * value, axis=0, keepdims=True) / gain_ref[0:1, columns]
        store_piece(r, extra_rows(gain_grad), *outs, rows=slice(rows, rows + EXTRA))


def first_gradients(at, grad_ref, q0, q1, q2, q3, rest0, rest1, rest2, rest3, low_ref):
    f, c = at[0], at[1]
    rows_here = low_ref.shape[0]
    grads = [grad_ref[part_of(c ^ k, rows_here), :] for k in range(4)]
    others = jnp.concatenate(grads[1:], axis=1)
    heads = 3 * LANES
    for r in range(4):
        own, rest = (q0, q1, q2, q3)[r], (rest0, rest1, rest2, rest3)[r]
        part = dot_nn(grads[0], own[:heads, :]) + dot_nn(others, rest[...])
        low_ref[:, part_of(f ^ r, own.shape[1])] = part.astype(jnp.bfloat16)


def input_gradients(at, mine_ref, other_ref, x_ref, gain_ref, da_mine, da_other, out_ref):
    t, half = at[2], da_mine.shape[0]
    grad = (mine_ref[...].astype(jnp.float32) + other_ref[...].astype(jnp.float32)) * gain_ref[0:1, :]
    normed, scale = standardize(x_ref[...].astype(jnp.float32))
    out_ref[...] = standardize_back(normed, scale, grad)
    out_ref[part_of(t, half), :] += da_mine[...].astype(jnp.float32)
    out_ref[part_of(1 - t, half), :] += da_other[...].astype(jnp.float32)


def qkv_layout(at, p0, p1, p2, p3, out_ref):
    c = at[1]
    for k, part in enumerate((p0, p1, p2, p3)):
        for j in range(3):
            out_ref[j, :, part_of(c ^ k, LANES)] = part[j * LANES : (j + 1) * LANES, :].astype(jnp.float32).T


def short_sequences(
    tokens, segments, attn_gain, qkv_weight, out_weight, mlp_gain, inner_weight, outer_weight, cotangent
):
    f = lax.axis_index("fsdp")
    c = lax.axis_index("ctx")
    t = lax.axis_index("tp")
    here = jnp.stack([f, c, t]).astype(jnp.int32)
    row_count, width = tokens.shape[1:]
    half_rows = row_count // 2
    shard = attn_gain.shape[0]
    units = inner_weight.shape[2]
    length = segments.shape[1]
    heads = 3 * LANES
    c_order = [c ^ r for r in range(4)]
    seg_row = jnp.concatenate(
        [lax.dynamic_slice_in_dim(segments[0], p * row_count, row_count) for p in c_order]
    )
    seg_col, seg_line = seg_row.reshape(length, 1), seg_row.reshape(1, length)
    own_tokens = tokens[0]
    out_cot = cotangent[0]

    def across(value):
        return hop(value, "fsdp", 2, 4)

    def beside(value):
        return hop(value, "fsdp", 1, 4)

    def over_tp(value):
        return hop(value, "tp", 1, 2)

    def over_ctx(value, bits):
        return value if bits == 0 else hop(value, "ctx", bits, 4)

    def gathered(value, crossed):
        return [value, beside(value), crossed, beside(crossed)]

    own_half = lax.dynamic_slice_in_dim(own_tokens, t * half_rows, half_rows)
    halves = [over_ctx(own_half, r) for r in (1, 2, 3)]

    by_ctx = [
        lax.dynamic_slice_in_dim(qkv_weight, p * LANES, LANES, 2).reshape(shard, heads).T for p in c_order
    ]
    gain_rows = jnp.concatenate(
        [attn_gain[None], mlp_gain[None], jnp.zeros((EXTRA - 2, shard), attn_gain.dtype)], axis=0
    )
    qkv_own = jnp.concatenate([by_ctx[0], gain_rows], axis=0)
    qkv_rest = jnp.concatenate(by_ctx[1:], axis=0)
    out_own = out_weight
    inner_own = jnp.concatenate([inner_weight[:, 0].T, inner_weight[:, 1].T], axis=0)
    outer_own = outer_weight

    qkv_crossed = across(qkv_own)
    qkv_here = gathered(qkv_own, qkv_crossed)
    out_other = over_tp(out_own)
    inner_crossed = across(inner_own)

    cosines, sines = zip(*[angle_tables(row_count, p * row_count, HD) for p in c_order])
    cosine, sine = jnp.concatenate(cosines, axis=0), jnp.concatenate(sines, axis=0)
    sign = jnp.where(jnp.arange(HD) < HD // 2, -1.0, 1.0).astype(jnp.float32)
    cosine = jnp.concatenate([cosine[:, 0]] * 2, axis=1)
    sine = jnp.concatenate([sine[:, 0] * sign] * 2, axis=1)

    def project(k, block):
        return local_call(
            functools.partial(project_block, k),
            [low_shape(row_count, width)] + [low_shape(row_count, LANES)] * 3 + [wide_shape(8, width)],
            here,
            [*block, *qkv_here, cosine, sine],
            scratch=[pltpu.VMEM((row_count, width), jnp.bfloat16)],
            flops=2 * row_count * width * heads,
        )

    projected = [project(0, [own_tokens])]
    for k in (1, 2, 3):
        half, qkv_rest = after([halves[k - 1], qkv_rest], *([projected[k - 2][1]] if k > 1 else []))
        if k == 2:
            half, out_other = lax.optimization_barrier((half, out_other))
            out_pair = jnp.concatenate([out_own, out_other], axis=0)
            out_crossed = across(out_pair)
        projected.append(project(k, [half, over_tp(half)]))
    h_parts, queries, keys, values = [[p[i] for p in projected] for i in range(4)]
    gain_all = projected[0][4]

    raw, low, lse = local_call(
        attention_forward,
        [wide_shape(length, LANES), low_shape(2 * length, LANES), wide_shape(8, length)],
        here,
        [*queries, *keys, *values, seg_col, seg_line],
        flops=8 * length * length * LANES,
        transcendentals=2 * length * length,
    )

    def between_all(value):
        return lax.all_to_all(value, ("ctx", "tp"), 0, 0, tiled=True)

    def between_ctx(value):
        return lax.all_to_all(value, "ctx", 0, 0, tiled=True)

    inner_crossed, out_crossed = after([inner_crossed, out_crossed], low)
    (outer_own,) = after([outer_own], inner_crossed)
    attended, outer_crossed, *weights = lax.optimization_barrier(
        (between_all(low), across(outer_own), *gathered(inner_own, inner_crossed), *gathered(out_pair, out_crossed))
    )
    inner_all, out_all = weights[:4], weights[4:]
    outer_all = gathered(outer_own, outer_crossed)

    padded = (units + LANES - 1) // LANES * LANES
    middle, normed_two, second_low, acts = local_call(
        feed_forward,
        [wide_shape(row_count, width)] * 2 + [low_shape(row_count, width), low_shape(3 * row_count, padded)],
        here,
        [attended, own_tokens, out_cot, gain_all, *out_all, *inner_all, *outer_all],
    )

    def close(*values):
        return lax.optimization_barrier(values)

    def add_pairs(*pairs):
        return [lax.optimization_barrier(mine + arrived) for mine, arrived in pairs]

    def inwards(value):
        return lax.ppermute(value, "ctx", [(0, 1), (3, 2)])

    def across_middle(value):
        return lax.ppermute(value, "ctx", [(1, 2), (2, 1)])

    def outwards(value):
        return lax.ppermute(value, "ctx", [(1, 0), (2, 3)])

    at_end = jnp.logical_or(c == 0, c == 3)

    part_mine, part_other, gain_two_part = local_call(
        feed_forward_back,
        [low_shape(half_rows, width)] * 2 + [wide_shape(1, width)],
        here,
        [acts, normed_two, *inner_all],
        scratch=[pltpu.VMEM((row_count, width), jnp.bfloat16)],
    )
    acts_other, second_low_other, cot_other, attended_beside, part_mine, part_other, gain_two_part = close(
        beside(acts), beside(second_low), beside(out_cot), beside(attended), part_mine, part_other, gain_two_part
    )

    early = units // (4 * LANES) * LANES * 2
    mlp_grads = local_call(
        mlp_gradients,
        [low_shape(rows, shard) for rows in (units, units, units + early, units + early, units - early, units - early)],
        here,
        [acts, acts_other, second_low, second_low_other, out_cot, cot_other],
        flops=2 * 3 * row_count * width * units,
    )
    arrived, rest_crossed, gain_two_other, *mlp_grads = close(
        over_tp(part_other), across(qkv_rest), beside(gain_two_part), *mlp_grads
    )
    outer_keep, outer_cross, gate_keep, gate_cross, up_keep, up_cross = mlp_grads

    attn_low, head_grads = local_call(
        head_gradients,
        [low_shape(half_rows, width), low_shape(length, LANES)],
        here,
        [part_mine, arrived, middle, out_cot, gain_all, *out_all],
        flops=row_count * width * width,
    )
    (mlp_part,) = local_call(feed_forward_out, [low_shape(row_count, width)], here, [acts, *outer_all])
    diagonal = [(i, i ^ 3) for i in range(8)]
    head_grads, outer_x, attn_tp, attn_core, attn_diagonal, mlp_part, *rest_all = close(
        between_all(head_grads), across(outer_cross), over_tp(attn_low), beside(attn_low),
        lax.ppermute(attn_low, ("fsdp", "tp"), diagonal), mlp_part, *gathered(qkv_rest, rest_crossed),
    )

    (outer_a,) = add_pairs((outer_keep, outer_x))
    (projected_grads,) = local_call(
        attention_backward,
        [low_shape(length, heads)],
        here,
        [*queries, *keys, *values, head_grads, raw, lse, cosine, sine, seg_col, seg_line],
        scratch=[pltpu.VMEM((LANES, length), jnp.float32)],
        flops=20 * length * length * LANES,
        transcendentals=2 * length * length,
    )
    out_keep, out_cross = local_call(
        out_gradients,
        [low_shape(4 * LANES + EXTRA, shard)] * 2,
        here,
        [attended, attended_beside, attn_low, attn_tp, attn_core, attn_diagonal, gain_two_part, gain_two_other],
        flops=2 * row_count * width * 4 * LANES,
    )
    outer_in, gate_x, mlp_other, projected_grads, out_keep, out_cross = close(
        inwards(outer_a), across(gate_cross), over_tp(mlp_part), projected_grads, out_keep, out_cross
    )

    gate_a, outer_b = add_pairs((gate_keep, gate_x), (outer_a, outer_in))
    qkv_parts = local_call(
        qkv_gradients,
        [low_shape(2, heads + EXTRA, shard)] + [low_shape(heads + EXTRA, shard)] * 2,
        here,
        [projected_grads, *h_parts, *qkv_here, gain_all],
        flops=2 * length * width * heads,
    )
    first_in, up_x, out_x, gate_in, outer_mid, *qkv_parts = close(
        between_ctx(projected_grads), across(up_cross), across(out_cross), inwards(gate_a), across_middle(outer_b),
        *qkv_parts,
    )

    qkv_sent, qkv_keep, qkv_keep_across = qkv_parts
    joined_rows = units - early + 4 * LANES + EXTRA
    up_a, outer_c, payload = local_call(
        joined_sums,
        [low_shape(joined_rows, shard), low_shape(units, shard), low_shape(joined_rows, shard)],
        here,
        [up_keep, up_x, out_keep, out_x, outer_b, outer_mid],
    )
    (gate_b,) = add_pairs((gate_a, gate_in))
    (first_low_part,) = local_call(
        first_gradients,
        [low_shape(row_count, width)],
        here,
        [first_in, *qkv_here, *rest_all],
        flops=2 * row_count * width * 4 * heads,
    )
    up_in, gate_mid, qkv_received, first_low_part = close(
        over_ctx(payload, 1), across_middle(gate_b), beside(qkv_sent), first_low_part
    )
    outer_out = up_in[:units]

    up_b, gate_c = add_pairs((up_a, up_in), (gate_b, gate_mid))
    qkv_cross = qkv_keep_across + qkv_received[1]
    outer_grad = jnp.where(at_end, outer_out, outer_c).astype(jnp.float32)
    first_other, up_mid, gate_out, qkv_x, outer_grad = close(
        over_tp(first_low_part), across_middle(up_b), outwards(gate_c), across(qkv_cross), outer_grad
    )

    (up_c,) = add_pairs((up_b, up_mid))
    qkv_sum = lax.optimization_barrier(
        (qkv_keep.astype(jnp.float32) + qkv_received[0].astype(jnp.float32) + qkv_x.astype(jnp.float32)).astype(
            jnp.bfloat16
        )
    )
    (input_grad,) = local_call(
        input_gradients,
        [wide_shape(row_count, width)],
        here,
        [first_low_part, first_other, own_tokens, gain_all, attn_low, attn_tp],
    )
    gate_sum = jnp.where(at_end, gate_out, gate_c)
    block_out = (
        middle + (mlp_part.astype(jnp.float32) + mlp_other.astype(jnp.float32))
    ).astype(jnp.bfloat16)
    up_out, input_grad, gate_sum, block_out, *qkv_sums = close(
        outwards(up_c), input_grad, gate_sum, block_out, *[over_ctx(qkv_sum, k) for k in (1, 2, 3)]
    )
    qkv_sums = [qkv_sum, *qkv_sums]
    up_sum = jnp.where(at_end, up_out, up_c)
    late = units - early
    out_grad = up_sum[late : late + 4 * LANES].astype(jnp.float32)

    (qkv_grad,) = local_call(qkv_layout, [wide_shape(3, shard, 4 * LANES)], here, qkv_sums)
    gain_lines = [part[heads].astype(jnp.float32) for part in qkv_sums]
    up_grad = jnp.concatenate([gate_sum[units:], up_sum[:late]], axis=0)
    gain_grads = jnp.stack(
        [(gain_lines[0] + gain_lines[1]) + (gain_lines[2] + gain_lines[3]), up_sum[late + 4 * LANES].astype(jnp.float32)]
    )
    gain_grads = gain_grads + over_tp(gain_grads)

    return (
        block_out[None],
        input_grad[None],
        gain_grads[0],
        qkv_grad.transpose(1, 0, 2),
        out_grad,
        gain_grads[1],
        jnp.stack([gate_sum[:units].T, up_grad.T], axis=1).astype(jnp.float32),
        outer_grad,
    )


def solution(mesh):
    placed = (
        P("fsdp", "ctx", None),
        P("fsdp", None),
        P("fsdp"),
        P("fsdp", None, "tp"),
        P("tp", "fsdp"),
        P("fsdp"),
        P("fsdp", None, "tp"),
        P("tp", "fsdp"),
        P("fsdp", "ctx", None),
    )
    sizes = dict(mesh.shape)

    def layer(*args):
        tokens, segments, qkv_weight = args[0], args[1], args[3]
        heads_apart = qkv_weight.shape[2] == 4 * LANES
        short = segments.shape[1] == 4 * tokens.shape[1] and segments.shape[1] <= 1024
        small = (sizes["fsdp"], sizes["ctx"], sizes["tp"]) == (4, 4, 2)
        if small and short and heads_apart and tokens.shape[0] == 1:
            return short_sequences(*args)
        return per_device(*args)

    return jax.shard_map(
        layer,
        mesh=mesh,
        in_specs=placed,
        out_specs=(
            P("fsdp", "ctx", None),
            P("fsdp", "ctx", None),
            P("fsdp"),
            P("fsdp", None, "tp"),
            P("tp", "fsdp"),
            P("fsdp"),
            P("fsdp", None, "tp"),
            P("tp", "fsdp"),
        ),
        check_vma=False,
    )
```

```python
import functools
import math

import jax
import jax.numpy as jnp
from jax import lax
from jax.experimental import pallas as pl
from jax.experimental.pallas import tpu as pltpu
from jax.sharding import PartitionSpec as P

HD = 64


EPSILON = 1e-05
ROPE_BASE = 160000.0
MASKED = -1e30


def normalize(values, gain_row):
    row_mean = jnp.mean(values, axis=-1, keepdims=True)
    centered = values - row_mean
    spread = jnp.mean(centered * centered, axis=-1, keepdims=True)
    return centered * lax.rsqrt(spread + EPSILON) * gain_row


def geglu(gate_in, upper):
    return jax.nn.gelu(gate_in, approximate=False) * upper


def angle_tables(row_count, offset, depth):
    half_width = depth // 2
    inverse = jnp.power(
        jnp.float32(ROPE_BASE), -(2.0 * jnp.arange(half_width, dtype=jnp.float32)) / depth
    )
    places = (offset + jnp.arange(row_count, dtype=jnp.int32)).astype(jnp.float32)
    angles = places[:, None] * inverse[None, :]
    angles = jnp.concatenate([angles, angles], axis=-1)
    return (jnp.cos(angles)[:, None, :], jnp.sin(angles)[:, None, :])


def rotate(values, cosine, sine):
    half_width = values.shape[-1] // 2
    turned = jnp.concatenate([-values[..., half_width:], values[..., :half_width]], axis=-1)
    return values * cosine + turned * sine


def rotate_back(grad_in, cosine, sine):
    half_width = grad_in.shape[-1] // 2
    scaled = grad_in * sine
    turned = jnp.concatenate([scaled[..., half_width:], -scaled[..., :half_width]], axis=-1)
    return grad_in * cosine + turned


def attend_forward(queries, query_seg, seg_row, key_low, value_low, score_scale):
    row_count, heads_here, depth = queries.shape
    initial = (
        jnp.full((heads_here, row_count), MASKED, jnp.float32),
        jnp.zeros((heads_here, row_count), jnp.float32),
        jnp.zeros((row_count, heads_here, depth), jnp.float32),
    )
    key_piece = lax.all_gather(key_low, "ctx", axis=0, tiled=True)
    value_piece = lax.all_gather(value_low, "ctx", axis=0, tiled=True)
    piece_rows = key_piece.shape[0]
    block_size = math.gcd(piece_rows, 512)
    blocks = (
        key_piece.reshape(piece_rows // block_size, block_size, heads_here, depth),
        value_piece.reshape(piece_rows // block_size, block_size, heads_here, depth),
        seg_row.reshape(piece_rows // block_size, block_size),
    )

    def step(state, block_data):
        running_peak, running_total, accum = state
        key_block, value_block, block_seg = block_data
        scores = jnp.einsum("qhe,khe->hqk", queries, key_block, preferred_element_type=jnp.float32)
        same_doc = (query_seg[:, None] == block_seg[None, :])[None]
        logits = jnp.where(same_doc, scores * score_scale, MASKED)
        new_peak = jnp.maximum(running_peak, jnp.max(logits, axis=-1))
        rescale = jnp.exp(running_peak - new_peak)
        weights = jnp.where(same_doc, jnp.exp(logits - new_peak[:, :, None]), 0.0)
        running_total = running_total * rescale + jnp.sum(weights, axis=-1)
        mixed_out = jnp.einsum(
            "hqk,khe->qhe",
            weights.astype(jnp.bfloat16),
            value_block,
            preferred_element_type=jnp.float32,
        )
        accum = accum * rescale.T[:, :, None] + mixed_out
        return ((new_peak, running_total, accum), None)

    result, unused = lax.scan(step, initial, blocks)
    running_peak, running_total, accum = result
    return (accum / running_total.T[:, :, None], running_peak + jnp.log(running_total))


def probs_and_grads(
    query_block, key_block, grad_block, value_block, same_doc, log_total, delta_rows, score_scale
):
    scores = jnp.einsum("qhe,khe->hqk", query_block, key_block, preferred_element_type=jnp.float32)
    probs = jnp.where(same_doc, jnp.exp(scores * score_scale - log_total[:, :, None]), 0.0)
    prob_grad = jnp.einsum(
        "qhe,khe->hqk", grad_block, value_block, preferred_element_type=jnp.float32
    )
    score_grad = (probs * (prob_grad - delta_rows[:, :, None]) * score_scale).astype(jnp.bfloat16)
    return (probs.astype(jnp.bfloat16), score_grad)


def attend_backward(
    queries, key_low, value_low, grad_low, log_total, delta_rows, query_seg, seg_row, score_scale
):
    row_count, heads_here, depth = queries.shape
    seq_length = seg_row.shape[0]
    block_size = math.gcd(seq_length, 512)
    block_count = seq_length // block_size
    key_all, value_all = (
        lax.all_gather(key_low, "ctx", axis=0, tiled=True),
        lax.all_gather(value_low, "ctx", axis=0, tiled=True),
    )
    blocks = (
        key_all.reshape(block_count, block_size, heads_here, depth),
        value_all.reshape(block_count, block_size, heads_here, depth),
        seg_row.reshape(block_count, block_size),
    )

    def key_step(query_acc, block_data):
        key_block, value_block, block_seg = block_data
        same_doc = (query_seg[:, None] == block_seg[None, :])[None]
        prob_low, score_grad = probs_and_grads(
            queries, key_block, grad_low, value_block, same_doc, log_total, delta_rows, score_scale
        )
        query_acc = query_acc + jnp.einsum(
            "hqk,khe->qhe", score_grad, key_block, preferred_element_type=jnp.float32
        )
        key_part = jnp.einsum(
            "hqk,qhe->khe", score_grad, queries, preferred_element_type=jnp.float32
        )
        value_part = jnp.einsum(
            "hqk,qhe->khe", prob_low, grad_low, preferred_element_type=jnp.float32
        )
        return (query_acc, (key_part, value_part))

    query_grad, key_value_parts = lax.scan(
        key_step, jnp.zeros((row_count, heads_here, depth), jnp.float32), blocks
    )
    key_parts = key_value_parts[0].reshape(seq_length, heads_here * depth)
    value_parts = key_value_parts[1].reshape(seq_length, heads_here * depth)
    key_grad, value_grad = (
        lax.psum_scatter(
            key_parts.astype(jnp.bfloat16), "ctx", scatter_dimension=0, tiled=True
        ).astype(jnp.float32),
        lax.psum_scatter(
            value_parts.astype(jnp.bfloat16), "ctx", scatter_dimension=0, tiled=True
        ).astype(jnp.float32),
    )
    key_grad = key_grad.reshape(row_count, heads_here, depth)
    value_grad = value_grad.reshape(row_count, heads_here, depth)
    return (query_grad, key_grad, value_grad)


def per_device(
    tokens,
    segments,
    attn_gain,
    qkv_weight,
    out_weight,
    mlp_gain,
    inner_weight,
    outer_weight,
    cotangent,
):
    qkv_full, out_full, gain_one = (
        lax.all_gather(qkv_weight, "fsdp", axis=0, tiled=True),
        lax.all_gather(out_weight, "fsdp", axis=1, tiled=True),
        lax.all_gather(attn_gain, "fsdp", axis=0, tiled=True),
    )
    inner_full, outer_full, gain_two = (
        lax.all_gather(inner_weight, "fsdp", axis=0, tiled=True),
        lax.all_gather(outer_weight, "fsdp", axis=1, tiled=True),
        lax.all_gather(mlp_gain, "fsdp", axis=0, tiled=True),
    )
    seq_count, row_count, model_width = tokens.shape
    local_width = qkv_full.shape[2]
    heads_here = local_width // HD
    score_scale = HD ** (-0.5)
    offset = lax.axis_index("ctx") * row_count
    cosine, sine = angle_tables(row_count, offset, HD)
    input_rows = tokens.reshape(-1, model_width).astype(jnp.float32)
    normed_one, norm_one_back = jax.vjp(normalize, input_rows, gain_one.astype(jnp.float32))
    first_low = normed_one.astype(jnp.bfloat16)
    projected_output = jnp.einsum(
        "td,dcf->tcf", first_low, qkv_full, preferred_element_type=jnp.float32
    )
    projected_output = projected_output.reshape(seq_count, row_count, 3, heads_here, HD)
    query_low = rotate(projected_output[:, :, 0], cosine, sine).astype(jnp.bfloat16)
    key_low = rotate(projected_output[:, :, 1], cosine, sine).astype(jnp.bfloat16)
    value_low = projected_output[:, :, 2].astype(jnp.bfloat16)
    seq_index = 0
    seg_row = segments[seq_index]
    query_seg = lax.dynamic_slice_in_dim(seg_row, offset, row_count)
    raw_out, log_total = attend_forward(
        query_low[seq_index],
        query_seg,
        seg_row,
        key_low[seq_index],
        value_low[seq_index],
        score_scale,
    )
    query_segs = [query_seg]
    raw_outs = [raw_out]
    log_totals = [log_total]
    attended_low = jnp.stack(raw_outs).astype(jnp.bfloat16).reshape(-1, local_width)
    attn_part = jnp.dot(attended_low, out_full, preferred_element_type=jnp.float32)
    middle_activation = input_rows + lax.psum(attn_part.astype(jnp.bfloat16), "tp").astype(
        jnp.float32
    )
    normed_two, norm_two_back = jax.vjp(normalize, middle_activation, gain_two.astype(jnp.float32))
    second_low = normed_two.astype(jnp.bfloat16)
    hidden_input = jnp.einsum(
        "td,dcf->tcf", second_low, inner_full, preferred_element_type=jnp.float32
    )
    hidden_state, geglu_back = jax.vjp(geglu, hidden_input[:, 0], hidden_input[:, 1])
    hidden_low = hidden_state.astype(jnp.bfloat16)
    mlp_part = jnp.dot(hidden_low, outer_full, preferred_element_type=jnp.float32)
    block_out = (
        middle_activation + lax.psum(mlp_part.astype(jnp.bfloat16), "tp").astype(jnp.float32)
    ).astype(jnp.bfloat16)
    out_cot = cotangent.reshape(-1, model_width)
    outer_local = jnp.einsum("tf,td->fd", hidden_low, out_cot, preferred_element_type=jnp.float32)
    hidden_grad = jnp.einsum("td,fd->tf", out_cot, outer_full, preferred_element_type=jnp.float32)
    gate_grad, up_grad = geglu_back(hidden_grad)
    inner_low = jnp.stack([gate_grad, up_grad], axis=1).astype(jnp.bfloat16)
    inner_local = jnp.einsum(
        "td,tcf->dcf", second_low, inner_low, preferred_element_type=jnp.float32
    )
    normed_two_grad = lax.psum(
        jnp.einsum("tcf,dcf->td", inner_low, inner_full, preferred_element_type=jnp.float32).astype(
            jnp.bfloat16
        ),
        "tp",
    ).astype(jnp.float32)
    middle_part, gain_two_grad = norm_two_back(normed_two_grad)
    middle_grad = out_cot.astype(jnp.float32) + middle_part
    attn_low = middle_grad.astype(jnp.bfloat16)
    out_local = jnp.einsum("tf,td->fd", attended_low, attn_low, preferred_element_type=jnp.float32)
    attended_grad = jnp.einsum("td,fd->tf", attn_low, out_full, preferred_element_type=jnp.float32)
    attended_grad = attended_grad.astype(jnp.bfloat16).reshape(seq_count, row_count, heads_here, HD)
    seq_index = 0
    grad_low = attended_grad[seq_index]
    delta_rows = jnp.sum(grad_low.astype(jnp.float32) * raw_outs[seq_index], axis=-1).T
    query_grad, key_grad, value_grad = attend_backward(
        query_low[seq_index],
        key_low[seq_index],
        value_low[seq_index],
        grad_low,
        log_totals[seq_index],
        delta_rows,
        query_segs[seq_index],
        segments[seq_index],
        score_scale,
    )
    stacked = jnp.stack(
        [rotate_back(query_grad, cosine, sine), rotate_back(key_grad, cosine, sine), value_grad],
        axis=1,
    )
    qkv_grads = stacked.reshape(row_count, 3, local_width)
    qkv_low = qkv_grads.astype(jnp.bfloat16)
    qkv_local = jnp.einsum("td,tcf->dcf", first_low, qkv_low, preferred_element_type=jnp.float32)
    normed_one_grad = lax.psum(
        jnp.einsum("tcf,dcf->td", qkv_low, qkv_full, preferred_element_type=jnp.float32).astype(
            jnp.bfloat16
        ),
        "tp",
    ).astype(jnp.float32)
    input_part, gain_one_grad = norm_one_back(normed_one_grad)
    input_grad = (middle_grad + input_part).reshape(tokens.shape)
    summed = (
        lax.psum_scatter(gain_one_grad, ("fsdp", "ctx"), scatter_dimension=0, tiled=True),
        lax.psum_scatter(qkv_local, ("fsdp", "ctx"), scatter_dimension=0, tiled=True),
        lax.psum_scatter(out_local, ("fsdp", "ctx"), scatter_dimension=1, tiled=True),
        lax.psum_scatter(gain_two_grad, ("fsdp", "ctx"), scatter_dimension=0, tiled=True),
        lax.psum_scatter(inner_local, ("fsdp", "ctx"), scatter_dimension=0, tiled=True),
        lax.psum_scatter(outer_local, ("fsdp", "ctx"), scatter_dimension=1, tiled=True),
    )
    gain_one_sum, qkv_sum, out_sum, gain_two_sum, inner_sum, outer_sum = summed
    shards = (
        lax.all_gather(gain_one_sum.astype(jnp.bfloat16), "ctx", axis=0, tiled=True).astype(
            gain_one_sum.dtype
        ),
        lax.all_gather(qkv_sum.astype(jnp.bfloat16), "ctx", axis=0, tiled=True).astype(
            qkv_sum.dtype
        ),
        lax.all_gather(out_sum.astype(jnp.bfloat16), "ctx", axis=1, tiled=True).astype(
            out_sum.dtype
        ),
        lax.all_gather(gain_two_sum.astype(jnp.bfloat16), "ctx", axis=0, tiled=True).astype(
            gain_two_sum.dtype
        ),
        lax.all_gather(inner_sum.astype(jnp.bfloat16), "ctx", axis=0, tiled=True).astype(
            inner_sum.dtype
        ),
        lax.all_gather(outer_sum.astype(jnp.bfloat16), "ctx", axis=1, tiled=True).astype(
            outer_sum.dtype
        ),
    )
    return (
        block_out.reshape(tokens.shape),
        input_grad,
        shards[0],
        shards[1],
        shards[2],
        shards[3],
        shards[4],
        shards[5],
    )


LANES = 128
BLOCK = 256
EXTRA = 32
COST = 0.0
WIDE_VMEM = 62 * 1024 * 1024


def hop(value, axis, bit, count):
    return lax.ppermute(value, axis, [(i, i ^ bit) for i in range(count)])


def after(values, *earlier):
    values = list(values)
    return list(lax.optimization_barrier(tuple(values) + earlier))[: len(values)]


def lane_half(shape):
    return lax.broadcasted_iota(jnp.int32, shape, 1) < HD


def swap_halves(values):
    lane = lax.broadcasted_iota(jnp.int32, values.shape, 1)
    low_part = lax.rem(lane, HD) < HD // 2
    return jnp.where(
        low_part,
        pltpu.roll(values, LANES - HD // 2, 1),
        pltpu.roll(values, HD // 2, 1),
    )


def dot_nt(left, right):
    return lax.dot_general(left, right, (((1,), (1,)), ((), ())), preferred_element_type=jnp.float32)


def dot_nn(left, right):
    return lax.dot_general(left, right, (((1,), (0,)), ((), ())), preferred_element_type=jnp.float32)


def dot_tn(left, right):
    return lax.dot_general(left, right, (((0,), (0,)), ((), ())), preferred_element_type=jnp.float32)


def one_head(values, head):
    first = lane_half(values.shape)
    keep = first if head == 0 else jnp.logical_not(first)
    return jnp.where(keep, values, jnp.zeros_like(values))


def part_of(index, size):
    return pl.ds(pl.multiple_of(index * size, size), size)


def standardize(values):
    row_mean = jnp.mean(values, axis=-1, keepdims=True)
    centered = values - row_mean
    spread = jnp.mean(centered * centered, axis=-1, keepdims=True)
    scale = lax.rsqrt(spread + EPSILON)
    return centered * scale, scale


def standardize_back(normed, scale, grad):
    inner = jnp.mean(grad * normed, axis=-1, keepdims=True)
    return scale * (grad - jnp.mean(grad, axis=-1, keepdims=True) - normed * inner)


def local_call(body, outs, places, operands, scratch=(), flops=0, transcendentals=0):
    moved = sum(math.prod(o.shape) * o.dtype.itemsize for o in list(operands) + list(outs))
    return pl.pallas_call(
        body,
        name=body.__name__ if hasattr(body, "__name__") else body.func.__name__,
        out_shape=tuple(outs),
        in_specs=[pl.BlockSpec(memory_space=pltpu.SMEM)]
        + [pl.BlockSpec(memory_space=pltpu.VMEM)] * len(operands),
        out_specs=tuple([pl.BlockSpec(memory_space=pltpu.VMEM)] * len(outs)),
        scratch_shapes=list(scratch),
        compiler_params=pltpu.CompilerParams(vmem_limit_bytes=WIDE_VMEM),
        cost_estimate=pl.CostEstimate(
            flops=int(flops * COST), bytes_accessed=int(moved * COST), transcendentals=int(transcendentals * COST)
        ),
    )(places, *operands)


def low_shape(*shape):
    return jax.ShapeDtypeStruct(shape, jnp.bfloat16)


def wide_shape(*shape):
    return jax.ShapeDtypeStruct(shape, jnp.float32)


def project_block(block, at, *refs):
    f, t = at[0], at[2]
    count = len(refs) - 12
    tokens_in, (w0, w1, w2, w3, cos_ref, sin_ref) = refs[:count], refs[count : count + 6]
    h_ref, q_ref, k_ref, v_ref, gain_ref, x_ref = refs[count + 6 :]
    weights = (w0, w1, w2, w3)
    columns = [part_of(f ^ r, w0.shape[1]) for r in range(4)]
    heads = 3 * LANES
    for r, weight in enumerate(weights):
        gain_ref[:, columns[r]] = weight[heads : heads + EXTRA, :].astype(jnp.float32)[:8, :]
    if count == 1:
        tokens = tokens_in[0][...]
    else:
        half = tokens_in[0].shape[0]
        x_ref[part_of(t, half), :] = tokens_in[0][...]
        x_ref[part_of(1 - t, half), :] = tokens_in[1][...]
        tokens = x_ref[...]
    h_ref[...] = (standardize(tokens.astype(jnp.float32))[0] * gain_ref[0:1, :]).astype(jnp.bfloat16)
    projected = 0.0
    for r, weight in enumerate(weights):
        projected += dot_nt(h_ref[:, columns[r]], weight[:heads, :])
    rows = slice(block * tokens.shape[0], (block + 1) * tokens.shape[0])
    cosine, sine = cos_ref[rows, :], sin_ref[rows, :]
    for ref, part in ((q_ref, projected[:, :LANES]), (k_ref, projected[:, LANES : 2 * LANES])):
        ref[...] = (part * cosine + swap_halves(part) * sine).astype(jnp.bfloat16)
    v_ref[...] = projected[:, 2 * LANES :].astype(jnp.bfloat16)


def joined(refs):
    return jnp.concatenate([ref[...] for ref in refs], axis=0)


def attention_forward(at, *refs):
    c = at[1]
    query_refs, key_refs, value_refs, seg_col, seg_line = refs[:4], refs[4:8], refs[8:12], refs[12], refs[13]
    raw_ref, low_ref, lse_ref = refs[14:]
    rows_here = query_refs[0].shape[0]
    keys, values = joined(key_refs), joined(value_refs)
    for k in range(4):
        rows = slice(k * rows_here, (k + 1) * rows_here)
        queries = query_refs[k][...] * jnp.bfloat16(HD ** (-0.5))
        same = seg_col[rows, :] == seg_line[...]
        outs, logs = [], []
        for head in range(2):
            scores = dot_nt(one_head(queries, head), keys)
            scores = jnp.where(same, scores, MASKED)
            peak = jnp.max(scores, axis=1, keepdims=True)
            weights = jnp.exp(scores - peak)
            total = jnp.sum(weights, axis=1, keepdims=True)
            probs = (weights * (1.0 / total)).astype(jnp.bfloat16)
            outs.append(dot_nn(probs, values))
            logs.append(peak + jnp.log(total))
        raw = jnp.where(lane_half(outs[0].shape), outs[0], outs[1])
        raw_ref[rows, :] = raw
        for b in range(2):
            low_ref[part_of((c ^ k) * 2 + b, rows_here), :] = raw.astype(jnp.bfloat16)
        lane = lax.broadcasted_iota(jnp.int32, (rows_here, LANES), 1)
        lse_ref[:, rows] = jnp.where(lane == 0, logs[0], logs[1]).T[:8, :]


def attention_backward(
    at, q0, q1, q2, q3, k0, k1, k2, k3, v0, v1, v2, v3, do_ref, raw_ref, lse_ref, cos_ref, sin_ref,
    seg_col, seg_line, out_ref, turned_ref,
):
    c = at[1]
    rows_here = q0.shape[0]
    grads = jnp.concatenate([do_ref[part_of(c ^ k, rows_here), :] for k in range(4)], axis=0)
    product = grads.astype(jnp.float32) * raw_ref[...]
    first = lane_half(product.shape)
    whole = jnp.sum(jnp.where(first, product, 0.0), axis=1, keepdims=True)
    other = jnp.sum(jnp.where(first, 0.0, product), axis=1, keepdims=True)
    lane = lax.broadcasted_iota(jnp.int32, product.shape, 1)
    delta = jnp.where(lane == 0, whole, other).T
    scale = HD ** (-0.5)
    queries = joined((q0, q1, q2, q3))
    scaled = queries * jnp.bfloat16(scale)
    for k in range(4):
        rows, place = slice(k * rows_here, (k + 1) * rows_here), part_of(c ^ k, rows_here)
        keys, values = (k0, k1, k2, k3)[k][...], (v0, v1, v2, v3)[k][...]
        keys_turned = keys.T
        same = seg_col[rows, :] == seg_line[...]
        key_parts, value_parts = [], []
        for head in range(2):
            scores = dot_nt(one_head(keys, head), scaled)
            probs = jnp.where(same, jnp.exp(scores - lse_ref[head : head + 1, :]), 0.0)
            prob_grad = dot_nt(one_head(values, head), grads)
            score_grad = (probs * (prob_grad - delta[head : head + 1, :])).astype(jnp.bfloat16)
            value_parts.append(dot_nn(probs.astype(jnp.bfloat16), grads))
            key_parts.append(dot_nn(score_grad, scaled))
            here = slice(head * HD, (head + 1) * HD)
            part = dot_nn(keys_turned[here, :], score_grad)
            if k == 0:
                turned_ref[here, :] = part
            else:
                turned_ref[here, :] += part
        half = lane_half(key_parts[0].shape)
        key_grad = jnp.where(half, key_parts[0], key_parts[1])
        value_grad = jnp.where(half, value_parts[0], value_parts[1])
        key_grad = key_grad * cos_ref[rows, :] - swap_halves(key_grad) * sin_ref[rows, :]
        out_ref[place, LANES : 2 * LANES] = key_grad.astype(jnp.bfloat16)
        out_ref[place, 2 * LANES :] = value_grad.astype(jnp.bfloat16)
    for k in range(4):
        rows, place = slice(k * rows_here, (k + 1) * rows_here), part_of(c ^ k, rows_here)
        query_grad = turned_ref[:, rows].T * scale
        query_grad = query_grad * cos_ref[rows, :] - swap_halves(query_grad) * sin_ref[rows, :]
        out_ref[place, :LANES] = query_grad.astype(jnp.bfloat16)


def attended_heads(ref, rows_here, sides):
    return jnp.concatenate([ref[part_of(k * 2 + b, rows_here), :] for b in sides for k in range(4)], axis=1)


def feed_forward(
    at, attended_ref, x_ref, cot_ref, gain_ref,
    o0, o1, o2, o3, inner0, inner1, inner2, inner3, outer0, outer1, outer2, outer3,
    mid_ref, normed_ref, second_ref, acts_ref,
):
    f, t = at[0], at[2]
    rows_here = x_ref.shape[0]
    attended = attended_heads(attended_ref, rows_here, (t, 1 - t))
    inners, outers = (inner0, inner1, inner2, inner3), (outer0, outer1, outer2, outer3)
    columns = [part_of(f ^ r, o0.shape[1]) for r in range(4)]
    for r, weight in enumerate((o0, o1, o2, o3)):
        mid_ref[:, columns[r]] = x_ref[:, columns[r]].astype(jnp.float32) + dot_nn(attended, weight[...])
    normed = standardize(mid_ref[...])[0]
    normed_ref[...] = normed
    second_ref[...] = (normed * gain_ref[1:2, :]).astype(jnp.bfloat16)
    units = outer0.shape[0]
    for start in range(0, units, BLOCK):
        stop = min(start + BLOCK, units)
        gate, up, hid_grad = 0.0, 0.0, 0.0
        for r in range(4):
            rows = second_ref[:, columns[r]]
            gate += dot_nt(rows, inners[r][start:stop, :])
            up += dot_nt(rows, inners[r][units + start : units + stop, :])
            hid_grad += dot_nt(cot_ref[:, columns[r]], outers[r][start:stop, :])
        below = 0.5 + 0.5 * lax.erf(gate * (2.0 ** -0.5))
        density = jnp.exp(-0.5 * gate * gate) * ((2.0 * math.pi) ** -0.5)
        active = gate * below
        acts_ref[:rows_here, start:stop] = (active * up).astype(jnp.bfloat16)
        acts_ref[rows_here : 2 * rows_here, start:stop] = (
            hid_grad * up * (below + gate * density)
        ).astype(jnp.bfloat16)
        acts_ref[2 * rows_here :, start:stop] = (hid_grad * active).astype(jnp.bfloat16)


def feed_forward_back(
    at, acts_ref, normed_ref, inner0, inner1, inner2, inner3, mine_ref, other_ref, gain_grad_ref, low_ref
):
    f, t = at[0], at[2]
    rows_here = normed_ref.shape[0]
    units = inner0.shape[0] // 2
    gate_grad = acts_ref[rows_here : 2 * rows_here, :units]
    up_grad = acts_ref[2 * rows_here :, :units]
    for r, inner in enumerate((inner0, inner1, inner2, inner3)):
        columns = part_of(f ^ r, inner.shape[1])
        part = dot_nn(gate_grad, inner[:units, :]) + dot_nn(up_grad, inner[units:, :])
        low_ref[:, columns] = part.astype(jnp.bfloat16)
        gain_grad_ref[:, columns] = jnp.sum(part * normed_ref[:, columns], axis=0, keepdims=True)
    half = mine_ref.shape[0]
    mine_ref[...] = low_ref[part_of(t, half), :]
    other_ref[...] = low_ref[part_of(1 - t, half), :]


def feed_forward_out(at, acts_ref, outer0, outer1, outer2, outer3, out_ref):
    f = at[0]
    hidden = acts_ref[: out_ref.shape[0], : outer0.shape[0]]
    for r, weight in enumerate((outer0, outer1, outer2, outer3)):
        out_ref[:, part_of(f ^ r, weight.shape[1])] = dot_nn(hidden, weight[...]).astype(jnp.bfloat16)


def head_gradients(
    at, mine_ref, other_ref, mid_ref, cot_ref, gain_ref, o0, o1, o2, o3, da_ref, out_ref
):
    f, t = at[0], at[2]
    rows = part_of(t, da_ref.shape[0])
    grad = (mine_ref[...].astype(jnp.float32) + other_ref[...].astype(jnp.float32)) * gain_ref[1:2, :]
    normed, scale = standardize(mid_ref[rows, :])
    mid_grad = cot_ref[rows, :].astype(jnp.float32) + standardize_back(normed, scale, grad)
    da_ref[...] = mid_grad.astype(jnp.bfloat16)
    total = 0.0
    for r, weight in enumerate((o0, o1, o2, o3)):
        total += dot_nt(da_ref[:, part_of(f ^ r, weight.shape[1])], weight[...])
    for b in range(2):
        for k in range(4):
            at_part = (b * 4 + k) * LANES
            out_ref[part_of(k * 2 + (t ^ b), da_ref.shape[0]), :] = total[:, at_part : at_part + LANES].astype(
                jnp.bfloat16
            )


def store_piece(r, value, send_ref, keep_ref, keep_across_ref, rows=slice(None)):
    if r in (1, 3):
        send_ref[r // 2, rows, :] = value
    else:
        (keep_ref if r == 0 else keep_across_ref)[rows, :] = value


def extra_rows(row):
    lines = lax.broadcasted_iota(jnp.int32, (EXTRA, row.shape[1]), 0)
    return jnp.where(lines == 0, row, 0.0).astype(jnp.bfloat16)


def joined_sums(
    at, up_keep, up_x, out_keep, out_x, outer_ref, outer_arrived, joined_ref, outer_sum, payload_ref
):
    c = at[1]
    rows, units = up_keep.shape[0], outer_ref.shape[0]
    joined_ref[:rows, :] = up_keep[...] + up_x[...]
    joined_ref[rows:, :] = out_keep[...] + out_x[...]
    outer_sum[...] = outer_ref[...] + outer_arrived[...]
    at_end = jnp.logical_or(c == 0, c == 3)

    @pl.when(at_end)
    def _():
        payload_ref[...] = joined_ref[...]

    @pl.when(jnp.logical_not(at_end))
    def _():
        payload_ref[:units, :] = outer_sum[...]
        payload_ref[units:, :] = jnp.zeros_like(payload_ref[units:, :])


def pair_columns(f, shard):
    return part_of(f, shard), part_of(f ^ 2, shard)


def mlp_gradients(
    at, own_ref, other_ref, second_ref, second_other, cot_ref, cot_other,
    outer_keep, outer_cross, gate_keep, gate_cross, up_keep, up_cross,
):
    f = at[0]
    units, shard = outer_keep.shape
    tokens = cot_ref.shape[0]
    early = gate_keep.shape[0] - units
    parts = (
        (0, 0, units, cot_ref, cot_other, outer_keep, outer_cross, 0),
        (1, 0, units, second_ref, second_other, gate_keep, gate_cross, 0),
        (2, 0, early, second_ref, second_other, gate_keep, gate_cross, units),
        (2, early, units, second_ref, second_other, up_keep, up_cross, 0),
    )
    for i, start, stop, right, right_other, keep, cross, first in parts:
        rows = slice(i * tokens, (i + 1) * tokens)
        for columns, out_ref in zip(pair_columns(f, shard), (keep, cross)):
            value = dot_tn(own_ref[rows, start:stop], right[:, columns])
            value += dot_tn(other_ref[rows, start:stop], right_other[:, columns])
            out_ref[first : first + stop - start, :] = value.astype(jnp.bfloat16)


def out_gradients(
    at, attended_ref, attended_other, da0, da1, da2, da3, gain_grad_ref, gain_grad_other, keep_ref, cross_ref
):
    f, t = at[0], at[2]
    half, rows_here = da0.shape[0], 2 * da0.shape[0]
    shard = keep_ref.shape[1]
    heads = [attended_heads(ref, rows_here, (t,)) for ref in (attended_ref, attended_other)]
    for columns, out_ref in zip(pair_columns(f, shard), (keep_ref, cross_ref)):
        value = 0.0
        for rows_of, own, other in ((heads[0], da0, da1), (heads[1], da2, da3)):
            first = jnp.where(t == 0, own[:, columns], other[:, columns])
            second = jnp.where(t == 0, other[:, columns], own[:, columns])
            value += dot_tn(rows_of, jnp.concatenate([first, second], axis=0))
        out_ref[: 4 * LANES, :] = value.astype(jnp.bfloat16)
        out_ref[4 * LANES :, :] = extra_rows(gain_grad_ref[:, columns] + gain_grad_other[:, columns])


def qkv_gradients(at, grad_ref, h0, h1, h2, h3, w0, w1, w2, w3, gain_ref, *outs):
    f, c = at[0], at[1]
    rows, shard = grad_ref.shape[1], w0.shape[1]
    rows_here = h0.shape[0]
    for r in (1, 3, 2, 0):
        columns = part_of(f ^ r, shard)
        value = 0.0
        for k, left in enumerate((h0, h1, h2, h3)):
            value += dot_tn(grad_ref[part_of(c ^ k, rows_here), :], left[:, columns])
        store_piece(r, value.astype(jnp.bfloat16), *outs, rows=slice(0, rows))
        weight = (w0, w1, w2, w3)[r][:rows, :].astype(jnp.float32)
        gain_grad = jnp.sum(weight * value, axis=0, keepdims=True) / gain_ref[0:1, columns]
        store_piece(r, extra_rows(gain_grad), *outs, rows=slice(rows, rows + EXTRA))


def first_gradients(at, grad_ref, q0, q1, q2, q3, rest0, rest1, rest2, rest3, low_ref):
    f, c = at[0], at[1]
    rows_here = low_ref.shape[0]
    grads = [grad_ref[part_of(c ^ k, rows_here), :] for k in range(4)]
    others = jnp.concatenate(grads[1:], axis=1)
    heads = 3 * LANES
    for r in range(4):
        own, rest = (q0, q1, q2, q3)[r], (rest0, rest1, rest2, rest3)[r]
        part = dot_nn(grads[0], own[:heads, :]) + dot_nn(others, rest[...])
        low_ref[:, part_of(f ^ r, own.shape[1])] = part.astype(jnp.bfloat16)


def input_gradients(at, mine_ref, other_ref, x_ref, gain_ref, da_mine, da_other, out_ref):
    t, half = at[2], da_mine.shape[0]
    grad = (mine_ref[...].astype(jnp.float32) + other_ref[...].astype(jnp.float32)) * gain_ref[0:1, :]
    normed, scale = standardize(x_ref[...].astype(jnp.float32))
    out_ref[...] = standardize_back(normed, scale, grad)
    out_ref[part_of(t, half), :] += da_mine[...].astype(jnp.float32)
    out_ref[part_of(1 - t, half), :] += da_other[...].astype(jnp.float32)


def qkv_layout(at, p0, p1, p2, p3, out_ref):
    c = at[1]
    for k, part in enumerate((p0, p1, p2, p3)):
        for j in range(3):
            out_ref[j, :, part_of(c ^ k, LANES)] = part[j * LANES : (j + 1) * LANES, :].astype(jnp.float32).T


def short_sequences(
    tokens, segments, attn_gain, qkv_weight, out_weight, mlp_gain, inner_weight, outer_weight, cotangent
):
    f = lax.axis_index("fsdp")
    c = lax.axis_index("ctx")
    t = lax.axis_index("tp")
    here = jnp.stack([f, c, t]).astype(jnp.int32)
    row_count, width = tokens.shape[1:]
    half_rows = row_count // 2
    shard = attn_gain.shape[0]
    units = inner_weight.shape[2]
    length = segments.shape[1]
    heads = 3 * LANES
    c_order = [c ^ r for r in range(4)]
    seg_row = jnp.concatenate(
        [lax.dynamic_slice_in_dim(segments[0], p * row_count, row_count) for p in c_order]
    )
    seg_col, seg_line = seg_row.reshape(length, 1), seg_row.reshape(1, length)
    own_tokens = tokens[0]
    out_cot = cotangent[0]

    def across(value):
        return hop(value, "fsdp", 2, 4)

    def beside(value):
        return hop(value, "fsdp", 1, 4)

    def over_tp(value):
        return hop(value, "tp", 1, 2)

    def over_ctx(value, bits):
        return value if bits == 0 else hop(value, "ctx", bits, 4)

    def gathered(value, crossed):
        return [value, beside(value), crossed, beside(crossed)]

    own_half = lax.dynamic_slice_in_dim(own_tokens, t * half_rows, half_rows)
    halves = [over_ctx(own_half, r) for r in (1, 2, 3)]

    by_ctx = [
        lax.dynamic_slice_in_dim(qkv_weight, p * LANES, LANES, 2).reshape(shard, heads).T for p in c_order
    ]
    gain_rows = jnp.concatenate(
        [attn_gain[None], mlp_gain[None], jnp.zeros((EXTRA - 2, shard), attn_gain.dtype)], axis=0
    )
    qkv_own = jnp.concatenate([by_ctx[0], gain_rows], axis=0)
    qkv_rest = jnp.concatenate(by_ctx[1:], axis=0)
    out_own = out_weight
    inner_own = jnp.concatenate([inner_weight[:, 0].T, inner_weight[:, 1].T], axis=0)
    outer_own = outer_weight

    qkv_crossed = across(qkv_own)
    qkv_here = gathered(qkv_own, qkv_crossed)
    out_other = over_tp(out_own)
    inner_crossed = across(inner_own)

    cosines, sines = zip(*[angle_tables(row_count, p * row_count, HD) for p in c_order])
    cosine, sine = jnp.concatenate(cosines, axis=0), jnp.concatenate(sines, axis=0)
    sign = jnp.where(jnp.arange(HD) < HD // 2, -1.0, 1.0).astype(jnp.float32)
    cosine = jnp.concatenate([cosine[:, 0]] * 2, axis=1)
    sine = jnp.concatenate([sine[:, 0] * sign] * 2, axis=1)

    def project(k, block):
        return local_call(
            functools.partial(project_block, k),
            [low_shape(row_count, width)] + [low_shape(row_count, LANES)] * 3 + [wide_shape(8, width)],
            here,
            [*block, *qkv_here, cosine, sine],
            scratch=[pltpu.VMEM((row_count, width), jnp.bfloat16)],
            flops=2 * row_count * width * heads,
        )

    projected = [project(0, [own_tokens])]
    for k in (1, 2, 3):
        half, qkv_rest = after([halves[k - 1], qkv_rest], *([projected[k - 2][1]] if k > 1 else []))
        if k == 2:
            half, out_other = lax.optimization_barrier((half, out_other))
            out_pair = jnp.concatenate([out_own, out_other], axis=0)
            out_crossed = across(out_pair)
        projected.append(project(k, [half, over_tp(half)]))
    h_parts, queries, keys, values = [[p[i] for p in projected] for i in range(4)]
    gain_all = projected[0][4]

    raw, low, lse = local_call(
        attention_forward,
        [wide_shape(length, LANES), low_shape(2 * length, LANES), wide_shape(8, length)],
        here,
        [*queries, *keys, *values, seg_col, seg_line],
        flops=8 * length * length * LANES,
        transcendentals=2 * length * length,
    )

    def between_all(value):
        return lax.all_to_all(value, ("ctx", "tp"), 0, 0, tiled=True)

    def between_ctx(value):
        return lax.all_to_all(value, "ctx", 0, 0, tiled=True)

    inner_crossed, out_crossed = after([inner_crossed, out_crossed], low)
    (outer_own,) = after([outer_own], inner_crossed)
    attended, outer_crossed, *weights = lax.optimization_barrier(
        (between_all(low), across(outer_own), *gathered(inner_own, inner_crossed), *gathered(out_pair, out_crossed))
    )
    inner_all, out_all = weights[:4], weights[4:]
    outer_all = gathered(outer_own, outer_crossed)

    padded = (units + LANES - 1) // LANES * LANES
    middle, normed_two, second_low, acts = local_call(
        feed_forward,
        [wide_shape(row_count, width)] * 2 + [low_shape(row_count, width), low_shape(3 * row_count, padded)],
        here,
        [attended, own_tokens, out_cot, gain_all, *out_all, *inner_all, *outer_all],
    )

    def close(*values):
        return lax.optimization_barrier(values)

    def add_pairs(*pairs):
        return [lax.optimization_barrier(mine + arrived) for mine, arrived in pairs]

    def inwards(value):
        return lax.ppermute(value, "ctx", [(0, 1), (3, 2)])

    def across_middle(value):
        return lax.ppermute(value, "ctx", [(1, 2), (2, 1)])

    def outwards(value):
        return lax.ppermute(value, "ctx", [(1, 0), (2, 3)])

    at_end = jnp.logical_or(c == 0, c == 3)

    part_mine, part_other, gain_two_part = local_call(
        feed_forward_back,
        [low_shape(half_rows, width)] * 2 + [wide_shape(1, width)],
        here,
        [acts, normed_two, *inner_all],
        scratch=[pltpu.VMEM((row_count, width), jnp.bfloat16)],
    )
    acts_other, second_low_other, cot_other, attended_beside, part_mine, part_other, gain_two_part = close(
        beside(acts), beside(second_low), beside(out_cot), beside(attended), part_mine, part_other, gain_two_part
    )

    early = units // (4 * LANES) * LANES * 2
    mlp_grads = local_call(
        mlp_gradients,
        [low_shape(rows, shard) for rows in (units, units, units + early, units + early, units - early, units - early)],
        here,
        [acts, acts_other, second_low, second_low_other, out_cot, cot_other],
        flops=2 * 3 * row_count * width * units,
    )
    arrived, rest_crossed, gain_two_other, *mlp_grads = close(
        over_tp(part_other), across(qkv_rest), beside(gain_two_part), *mlp_grads
    )
    outer_keep, outer_cross, gate_keep, gate_cross, up_keep, up_cross = mlp_grads

    attn_low, head_grads = local_call(
        head_gradients,
        [low_shape(half_rows, width), low_shape(length, LANES)],
        here,
        [part_mine, arrived, middle, out_cot, gain_all, *out_all],
        flops=row_count * width * width,
    )
    (mlp_part,) = local_call(feed_forward_out, [low_shape(row_count, width)], here, [acts, *outer_all])
    head_grads, outer_x, attn_tp, attn_core, mlp_part, *rest_all = close(
        between_all(head_grads), across(outer_cross), over_tp(attn_low), beside(attn_low),
        mlp_part, *gathered(qkv_rest, rest_crossed),
    )
    attn_diagonal = beside(attn_tp)

    (outer_a,) = add_pairs((outer_keep, outer_x))
    (projected_grads,) = local_call(
        attention_backward,
        [low_shape(length, heads)],
        here,
        [*queries, *keys, *values, head_grads, raw, lse, cosine, sine, seg_col, seg_line],
        scratch=[pltpu.VMEM((LANES, length), jnp.float32)],
        flops=20 * length * length * LANES,
        transcendentals=2 * length * length,
    )
    out_keep, out_cross = local_call(
        out_gradients,
        [low_shape(4 * LANES + EXTRA, shard)] * 2,
        here,
        [attended, attended_beside, attn_low, attn_tp, attn_core, attn_diagonal, gain_two_part, gain_two_other],
        flops=2 * row_count * width * 4 * LANES,
    )
    outer_in, gate_x, mlp_other, projected_grads, out_keep, out_cross = close(
        inwards(outer_a), across(gate_cross), over_tp(mlp_part), projected_grads, out_keep, out_cross
    )

    gate_a, outer_b = add_pairs((gate_keep, gate_x), (outer_a, outer_in))
    qkv_parts = local_call(
        qkv_gradients,
        [low_shape(2, heads + EXTRA, shard)] + [low_shape(heads + EXTRA, shard)] * 2,
        here,
        [projected_grads, *h_parts, *qkv_here, gain_all],
        flops=2 * length * width * heads,
    )
    first_in, up_x, out_x, gate_in, outer_mid, *qkv_parts = close(
        between_ctx(projected_grads), across(up_cross), across(out_cross), inwards(gate_a), across_middle(outer_b),
        *qkv_parts,
    )

    qkv_sent, qkv_keep, qkv_keep_across = qkv_parts
    joined_rows = units - early + 4 * LANES + EXTRA
    up_a, outer_c, payload = local_call(
        joined_sums,
        [low_shape(joined_rows, shard), low_shape(units, shard), low_shape(joined_rows, shard)],
        here,
        [up_keep, up_x, out_keep, out_x, outer_b, outer_mid],
    )
    (gate_b,) = add_pairs((gate_a, gate_in))
    (first_low_part,) = local_call(
        first_gradients,
        [low_shape(row_count, width)],
        here,
        [first_in, *qkv_here, *rest_all],
        flops=2 * row_count * width * 4 * heads,
    )
    up_in, gate_mid, qkv_received, first_low_part = close(
        over_ctx(payload, 1), across_middle(gate_b), beside(qkv_sent), first_low_part
    )
    outer_out = up_in[:units]

    up_b, gate_c = add_pairs((up_a, up_in), (gate_b, gate_mid))
    qkv_cross = qkv_keep_across + qkv_received[1]
    outer_grad = jnp.where(at_end, outer_out, outer_c).astype(jnp.float32)
    first_other, up_mid, gate_out, qkv_x, outer_grad = close(
        over_tp(first_low_part), across_middle(up_b), outwards(gate_c), across(qkv_cross), outer_grad
    )

    (up_c,) = add_pairs((up_b, up_mid))
    qkv_sum = lax.optimization_barrier(
        (qkv_keep.astype(jnp.float32) + qkv_received[0].astype(jnp.float32) + qkv_x.astype(jnp.float32)).astype(
            jnp.bfloat16
        )
    )
    (input_grad,) = local_call(
        input_gradients,
        [wide_shape(row_count, width)],
        here,
        [first_low_part, first_other, own_tokens, gain_all, attn_low, attn_tp],
    )
    gate_sum = jnp.where(at_end, gate_out, gate_c)
    block_out = (
        middle + (mlp_part.astype(jnp.float32) + mlp_other.astype(jnp.float32))
    ).astype(jnp.bfloat16)
    up_out, input_grad, gate_sum, block_out, *qkv_sums = close(
        outwards(up_c), input_grad, gate_sum, block_out, *[over_ctx(qkv_sum, k) for k in (1, 2, 3)]
    )
    qkv_sums = [qkv_sum, *qkv_sums]
    up_sum = jnp.where(at_end, up_out, up_c)
    late = units - early
    out_grad = up_sum[late : late + 4 * LANES].astype(jnp.float32)

    (qkv_grad,) = local_call(qkv_layout, [wide_shape(3, shard, 4 * LANES)], here, qkv_sums)
    gain_lines = [part[heads].astype(jnp.float32) for part in qkv_sums]
    up_grad = jnp.concatenate([gate_sum[units:], up_sum[:late]], axis=0)
    gain_grads = jnp.stack(
        [(gain_lines[0] + gain_lines[1]) + (gain_lines[2] + gain_lines[3]), up_sum[late + 4 * LANES].astype(jnp.float32)]
    )
    gain_grads = gain_grads + over_tp(gain_grads)

    return (
        block_out[None],
        input_grad[None],
        gain_grads[0],
        qkv_grad.transpose(1, 0, 2),
        out_grad,
        gain_grads[1],
        jnp.stack([gate_sum[:units].T, up_grad.T], axis=1).astype(jnp.float32),
        outer_grad,
    )


def solution(mesh):
    placed = (
        P("fsdp", "ctx", None),
        P("fsdp", None),
        P("fsdp"),
        P("fsdp", None, "tp"),
        P("tp", "fsdp"),
        P("fsdp"),
        P("fsdp", None, "tp"),
        P("tp", "fsdp"),
        P("fsdp", "ctx", None),
    )
    sizes = dict(mesh.shape)

    def layer(*args):
        tokens, segments, qkv_weight = args[0], args[1], args[3]
        heads_apart = qkv_weight.shape[2] == 4 * LANES
        short = segments.shape[1] == 4 * tokens.shape[1] and segments.shape[1] <= 1024
        small = (sizes["fsdp"], sizes["ctx"], sizes["tp"]) == (4, 4, 2)
        if small and short and heads_apart and tokens.shape[0] == 1:
            return short_sequences(*args)
        return per_device(*args)

    return jax.shard_map(
        layer,
        mesh=mesh,
        in_specs=placed,
        out_specs=(
            P("fsdp", "ctx", None),
            P("fsdp", "ctx", None),
            P("fsdp"),
            P("fsdp", None, "tp"),
            P("tp", "fsdp"),
            P("fsdp"),
            P("fsdp", None, "tp"),
            P("tp", "fsdp"),
        ),
        check_vma=False,
    )
```
